128 devices in a mesh: rep: 16 (over x, y_hi, core), tp: 8 (over z, y_lo).
Axes of the slice: x: 4, y: 4 (y_hi: 2, y_lo: 2; y = y_hi * 2 + y_lo), z: 4, core: 2. Of those that a mesh axis runs over, the one named last changes fastest.
Arguments:
- new_tokens: bfloat16 [4, 256, 8192], P(None, 'rep'), may hold values from -6 to 6
- norm_gain: bfloat16 [8192], replicated, may hold values from 0.099609375 to 1.8984375
- w_query: bfloat16 [8192, 8192], P('rep', 'tp'), may hold values from -0.0625 to 0.0625
- w_keyval: bfloat16 [8192, 2, 1024], P('rep', None, 'tp'), may hold values from -0.0625 to 0.0625
- w_output: bfloat16 [8192, 8192], P('tp', 'rep'), may hold values from -0.5 to 0.5
- kv_cache: bfloat16 [256, 2, 768, 1024], P('rep', None, None, 'tp'), may hold values from -200 to 200
- block_counts: int32 [256], P('rep'), may hold values from 1 to 6, 512 in all
- new_slot: int32 [256], P('rep'), may hold values from 0 to 255, as said below
Outputs:
- layer_out: bfloat16 [4, 256, 8192], P(None, 'rep', 'tp')
- cache_moved: bfloat16 [256, 2, 768, 1024], P('rep', None, None, 'tp')
The draws below stay inside these ranges and needn't reach their ends.
Inputs may be any that keep to these rules, and one draw needn't show every extreme that they name: new_slot is a permutation of the 256 slots; the request in old slot o goes to new replica new_slot[o] // 16; the 16 requests of each old replica (aligned blocks of 16 old slots) go to 8 new replicas, exactly 2 to each.
All inputs are finite; a program needn't handle non-finite values. No bound on the sum of `block_counts` on one device may be relied on, other than what follows from the above.
Results may differ from the reference program's by a relative error of at most 0.019.
Values may be sent and summed in bfloat16 or wider, within the bound.
No kernel may reach another device: no remote copies, remote signals or barrier semaphores. Data moves between devices by JAX's collectives and lax.ppermute only.
A program may use at most 192 MiB of HBM per device.

```python
import math
import jax
import jax.numpy as jnp
import numpy as np
from jax import lax

DMODEL = 8192
QHEADS = 64
KVHEADS = 8
HEADDIM = 128
ROWS = 16
STEPS = 4
BLOCK = 128
MAXBLK = 6
CAP = 2
REQS = 256
SPAN = 768


def draw_kv_cache(key, part):
    key = jax.random.fold_in(key, 11)
    first = jax.random.fold_in(key, 0)
    shape = (REQS, 2, SPAN, KVHEADS * HEADDIM)
    values = jax.random.truncated_normal(first, -6.0, 6.0, shape, jnp.float32)
    return values.astype(jnp.bfloat16)


def draw_new_slot(key, part):
    key = jax.random.fold_in(key, 7)
    first, second, third = jax.random.split(key, 3)
    replicas = REQS // ROWS
    shuffled = jax.random.permutation(first, replicas).astype(jnp.int32)
    order_rank = jnp.arange(replicas, dtype=jnp.int32)
    priority = jnp.where(shuffled == replicas // 2, -2, jnp.where(shuffled == 1, -1, order_rank))
    ranked = jnp.argsort(priority, stable=True)
    offsets = shuffled[ranked][:ROWS // CAP]
    local = jax.vmap(lambda item: jax.random.permutation(item, ROWS))(jax.random.split(second, replicas))
    shuffles = jax.vmap(lambda item: jax.random.permutation(item, ROWS))(jax.random.split(third, replicas))
    target = (jnp.arange(replicas)[:, None] + offsets[local // CAP]) % replicas
    new_local = shuffles[target, local]
    return (target * ROWS + new_local).reshape(REQS).astype(jnp.int32)


def steps_of(own_key, dims, cuts, low, largest):
    factor_of, own = 1.0, jax.random.fold_in(own_key, 6)
    for axis_at, blocks in cuts:
        heights = jnp.exp(jax.random.uniform(jax.random.fold_in(own, axis_at), (blocks,), jnp.float32, low / len(cuts), largest / len(cuts)))
        factor_of = factor_of * jnp.repeat(heights, dims[axis_at] // blocks).reshape([-1 if axis == axis_at else 1 for axis in range(len(dims))])
    return factor_of


def length_profile(count, total, bound, skew):
    weights = [(1 << 20) // math.isqrt(standing ** skew) + 1 for standing in range(2, count + 1)]
    rest, given = total - bound - (count - 1), [1] * (count - 1)
    while rest > 0:
        candidates = [i for i in range(count - 1) if given[i] < bound]
        pool, remaining = sum([weights[i] for i in candidates]), rest
        for i in candidates:
            more = min(bound - given[i], max(1, remaining * weights[i] // pool), rest)
            given[i] = given[i] + more
            rest = rest - more
    return np.array([bound] + given)


def uneven(key, number_of, total, limit, lean):
    if number_of == 2:
        one = jax.random.randint(key, (), max(1, total - limit), min(limit, total - 1) + 1)
        return jnp.stack([one, total - one])
    lengths = jnp.asarray(length_profile(number_of, total, limit, lean), jnp.int32)
    pairs = (number_of - 1) // 2
    source_of, taker = lengths[1:1 + 2 * pairs:2], lengths[2:2 + 2 * pairs:2]
    room = jnp.minimum(source_of - 1, limit - taker)
    moved = jax.random.randint(jax.random.fold_in(key, 1), (pairs,), 0, 1 << 20) % (room + 1)
    lengths = lengths.at[1:1 + 2 * pairs:2].set(source_of - moved).at[2:2 + 2 * pairs:2].set(taker + moved)
    return lengths[jax.random.permutation(jax.random.fold_in(key, 2), number_of)]


def bell_draw(stream_key, shape, scale, most, cuts=(), held_as=jnp.bfloat16):
    values = jax.random.normal(stream_key, shape, jnp.float32) * scale
    if len(cuts) > 0:
        values = steps_of(stream_key, shape, cuts, -0.22, 0.18) * values
    return jnp.clip(values, min=-most, max=most).astype(held_as)


def setup_inputs(seed: int = 0) -> dict:
    arg_keys = jax.random.split(jax.random.key(seed), 9)
    return {
        "new_tokens": bell_draw(arg_keys[0], (STEPS, REQS, DMODEL), 1.0, 6.0, ((1, 16),)),
        "norm_gain": jnp.clip(1.0 + 0.18 * jax.random.normal(arg_keys[1], (DMODEL,), jnp.float32), 0.099609375, 1.8984375).astype(jnp.bfloat16),
        "w_query": bell_draw(arg_keys[2], (DMODEL, QHEADS * HEADDIM), DMODEL ** -0.5, 0.0625, ((0, 16), (1, 8))),
        "w_keyval": bell_draw(arg_keys[3], (DMODEL, 2, KVHEADS * HEADDIM), DMODEL ** -0.5, 0.0625, ((0, 16), (2, 8))),
        "w_output": bell_draw(arg_keys[4], (QHEADS * HEADDIM, DMODEL), (QHEADS * HEADDIM // 64) ** -0.5, 0.5, ((0, 8), (1, 16))),
        "kv_cache": draw_kv_cache(jax.random.fold_in(arg_keys[8], 71), 0),
        "block_counts": uneven(arg_keys[6], REQS, 2 * REQS, MAXBLK, 2).astype(jnp.int32),
        "new_slot": draw_new_slot(jax.random.fold_in(arg_keys[8], 71), 0),
    }


def reference(new_tokens, norm_gain, w_query, w_keyval, w_output, kv_cache, block_counts, new_slot):
    inputs_f = new_tokens.astype(jnp.float32)
    inverse = lax.rsqrt(lax.optimization_barrier(jnp.mean(inputs_f * inputs_f, axis=-1, keepdims=True)) + 1e-05)
    normed = (inputs_f * inverse * norm_gain.astype(jnp.float32)).astype(jnp.bfloat16)
    flat = normed.reshape(STEPS * REQS, DMODEL)
    group = QHEADS // KVHEADS
    query = jnp.dot(flat, w_query, preferred_element_type=jnp.float32).astype(jnp.bfloat16)
    query = query.reshape(STEPS, REQS, KVHEADS, group, HEADDIM)
    fresh = jnp.dot(flat, w_keyval.reshape(DMODEL, 2 * KVHEADS * HEADDIM), preferred_element_type=jnp.float32)
    fresh = fresh.astype(jnp.bfloat16).reshape(STEPS, REQS, 2, KVHEADS, HEADDIM)
    owner = jnp.zeros((REQS,), jnp.int32).at[new_slot].set(jnp.arange(REQS, dtype=jnp.int32))
    moved_blocks = block_counts[owner]
    alive = jnp.arange(SPAN)[None, :] < (moved_blocks * BLOCK)[:, None]
    cache_moved = jnp.where(alive[:, None, :, None], kv_cache[owner], jnp.zeros((), jnp.bfloat16))
    factor = 1.0 / HEADDIM ** 0.5
    causal = jnp.arange(STEPS)[None, :] <= jnp.arange(STEPS)[:, None]

    def attend(index):
        one_query = lax.dynamic_index_in_dim(query, index, 1, keepdims=False).astype(jnp.float32)
        one_fresh = lax.dynamic_index_in_dim(fresh, index, 1, keepdims=False).astype(jnp.float32)
        one_cache = lax.dynamic_index_in_dim(cache_moved, index, 0, keepdims=False).astype(jnp.float32)
        blocks = lax.dynamic_index_in_dim(moved_blocks, index, 0, keepdims=False)
        old_keys = one_cache[0].reshape(SPAN, KVHEADS, HEADDIM)
        old_values = one_cache[1].reshape(SPAN, KVHEADS, HEADDIM)
        cache_scores = jnp.einsum('tkgd,lkd->kgtl', one_query, old_keys) * factor
        live = jnp.arange(SPAN) < blocks * BLOCK
        cache_scores = jnp.where(live, cache_scores, -1e+30)
        fresh_scores = jnp.einsum('tkgd,ukd->kgtu', one_query, one_fresh[:, 0]) * factor
        fresh_scores = jnp.where(causal, fresh_scores, -1e+30)
        peak = jnp.maximum(lax.optimization_barrier(jnp.max(cache_scores, -1)), lax.optimization_barrier(jnp.max(fresh_scores, -1)))
        cache_exp = jnp.exp(cache_scores - peak[..., None])
        fresh_exp = jnp.exp(fresh_scores - peak[..., None])
        total = lax.optimization_barrier(jnp.sum(cache_exp, -1)) + lax.optimization_barrier(jnp.sum(fresh_exp, -1))
        cache_prob = (cache_exp / total[..., None]).astype(jnp.bfloat16).astype(jnp.float32)
        fresh_prob = (fresh_exp / total[..., None]).astype(jnp.bfloat16).astype(jnp.float32)
        result = jnp.einsum('kgtl,lkd->tkgd', cache_prob, old_values)
        result = result + jnp.einsum('kgtu,ukd->tkgd', fresh_prob, one_fresh[:, 1])
        return result.astype(jnp.bfloat16)
    attended = lax.map(attend, jnp.arange(REQS, dtype=jnp.int32))
    attended = jnp.transpose(attended, (1, 0, 2, 3, 4)).reshape(STEPS * REQS, QHEADS * HEADDIM)
    layer_out = jnp.dot(attended, w_output, preferred_element_type=jnp.float32).astype(jnp.bfloat16)
    return (layer_out.reshape(STEPS, REQS, DMODEL), cache_moved)
```

```python
import jax
import jax.numpy as jnp
from jax import lax
from jax.sharding import PartitionSpec as P

HEADDIM = 128
BLOCK = 128
CAP = 2


def per_device(
    new_tokens, norm_gain, w_query, w_keyval, w_output, kv_cache, block_counts, new_slot
):
    reps = lax.axis_size("rep")
    tps = lax.axis_size("tp")
    rep_index = lax.axis_index("rep")
    core = rep_index % 2
    chips = reps // 2
    same_core = [[2 * chip + one for chip in range(chips)] for one in range(2)]
    other_core = [(one, one ^ 1) for one in range(reps)]
    num_steps, num_rows, feat_width = new_tokens.shape
    row_total = num_steps * num_rows
    all_rows = reps * row_total
    depth = feat_width // reps
    head_cols = w_query.shape[1]
    pair_cols = w_keyval.shape[2]
    group = head_cols // pair_cols
    out_cols = w_output.shape[1]
    span_len = kv_cache.shape[2]

    inputs_f = new_tokens.astype(jnp.float32)
    inverse = lax.rsqrt(jnp.mean(inputs_f * inputs_f, axis=-1, keepdims=True) + 1e-05)
    normed = (inputs_f * inverse * norm_gain.astype(jnp.float32)).astype(jnp.bfloat16)
    slabs = normed.reshape(row_total, reps, depth).transpose(1, 0, 2)
    table = jnp.concatenate([new_slot, block_counts]).astype(jnp.bfloat16)
    table = jnp.pad(table[None], ((0, 15), (0, depth - 2 * num_rows)))
    slabs = jnp.concatenate([slabs, jnp.broadcast_to(table, (reps, 16, depth))], axis=1)
    slabs = lax.all_to_all(slabs, "rep", split_axis=0, concat_axis=0, tiled=True)
    features = slabs[:, :row_total].reshape(all_rows, depth)
    table = slabs[:, row_total, : 2 * num_rows].astype(jnp.int32)
    slot_grid, length_grid = table[:, :num_rows], table[:, num_rows:]
    slot_table, length_table = slot_grid.reshape(-1), length_grid.reshape(-1)

    new_row = (slot_grid // num_rows * row_total + slot_grid % num_rows)[:, None, :]
    new_row = new_row + num_rows * jnp.arange(num_steps)[None, :, None]
    shuffle = (
        new_row.reshape(-1)[:, None] == jnp.arange(all_rows)[None, :]
    ).astype(jnp.bfloat16)
    features = jnp.dot(shuffle, features, preferred_element_type=jnp.bfloat16)
    weights = jnp.concatenate([w_query, w_keyval.reshape(depth, 2 * pair_cols)], axis=1)
    partial = jnp.dot(features, weights, preferred_element_type=jnp.float32)
    partial = partial.reshape(chips, 2, row_total, -1)
    mine = lax.dynamic_index_in_dim(partial, core, 1, keepdims=False)
    theirs = lax.dynamic_index_in_dim(partial, 1 - core, 1, keepdims=False)
    theirs = lax.ppermute(theirs.astype(jnp.bfloat16), "rep", other_core)
    pair_sum = (mine + theirs.astype(jnp.float32)).astype(jnp.bfloat16)
    pair_sum = lax.all_to_all(
        pair_sum, "rep", split_axis=0, concat_axis=0, tiled=True, axis_index_groups=same_core
    )
    projected = jnp.sum(pair_sum.astype(jnp.float32), axis=0).astype(jnp.bfloat16)
    query = projected[:, :head_cols].reshape(num_steps, num_rows, group, HEADDIM)
    fresh = projected[:, head_cols:].reshape(num_steps, num_rows, 2, HEADDIM)

    live = jnp.arange(span_len)[None, :] < (block_counts * BLOCK)[:, None]
    factor = 1.0 / HEADDIM**0.5
    cache_scores = (
        jnp.einsum("trgd,rld->rgtl", query, kv_cache[:, 0], preferred_element_type=jnp.float32)
        * factor
    )
    cache_scores = jnp.where(live[:, None, None, :], cache_scores, -1e30)
    fresh_scores = (
        jnp.einsum("trgd,urd->rgtu", query, fresh[:, :, 0], preferred_element_type=jnp.float32)
        * factor
    )
    causal = jnp.arange(num_steps)[None, :] <= jnp.arange(num_steps)[:, None]
    fresh_scores = jnp.where(causal, fresh_scores, -1e30)
    peak = jnp.maximum(jnp.max(cache_scores, -1), jnp.max(fresh_scores, -1))
    cache_exp = jnp.exp(cache_scores - peak[..., None])
    fresh_exp = jnp.exp(fresh_scores - peak[..., None])
    total = jnp.sum(cache_exp, -1) + jnp.sum(fresh_exp, -1)
    cache_prob = (cache_exp / total[..., None]).astype(jnp.bfloat16)
    fresh_prob = (fresh_exp / total[..., None]).astype(jnp.bfloat16)
    mixed = jnp.einsum(
        "rgtl,rld->trgd", cache_prob, kv_cache[:, 1], preferred_element_type=jnp.float32
    )
    mixed = mixed + jnp.einsum(
        "rgtu,urd->trgd", fresh_prob, fresh[:, :, 1], preferred_element_type=jnp.float32
    )
    attended = mixed.astype(jnp.bfloat16).reshape(row_total, head_cols)

    attended = lax.all_to_all(
        jnp.broadcast_to(attended[None], (reps, row_total, head_cols)),
        "rep",
        split_axis=0,
        concat_axis=0,
        tiled=True,
    ).reshape(all_rows, head_cols)
    attended = jnp.einsum("on,oc->nc", shuffle, attended, preferred_element_type=jnp.bfloat16)
    partial_out = jnp.dot(attended, w_output, preferred_element_type=jnp.float32)
    partial_out = lax.all_to_all(
        partial_out.astype(jnp.bfloat16).reshape(tps, all_rows // tps, out_cols),
        "tp",
        split_axis=0,
        concat_axis=0,
        tiled=True,
    )
    summed = jnp.sum(partial_out.astype(jnp.float32), axis=0).astype(jnp.bfloat16)
    summed = summed.reshape(2, row_total, out_cols)
    straight = [
        (r * tps + t, (2 * t + r % 2) * tps + r // 2) for r in range(reps) for t in range(tps)
    ]
    crossed = [
        (r * tps + t, (2 * t + 1 - r % 2) * tps + r // 2) for r in range(reps) for t in range(tps)
    ]
    near = lax.ppermute(
        lax.dynamic_index_in_dim(summed, core, 0, keepdims=False), ("rep", "tp"), straight
    )
    far = lax.ppermute(
        lax.dynamic_index_in_dim(summed, 1 - core, 0, keepdims=False), ("rep", "tp"), crossed
    )
    layer_out = jnp.where(
        core == 0,
        jnp.concatenate([near, far], axis=1),
        jnp.concatenate([far, near], axis=1),
    ).reshape(num_steps, num_rows, 2 * out_cols)

    grid_target = slot_grid // num_rows
    same_target = grid_target[:, :, None] == grid_target[:, None, :]
    earlier = jnp.arange(num_rows)[None, :] < jnp.arange(num_rows)[:, None]
    position = jnp.sum(same_target & earlier[None], axis=-1)
    bucket = grid_target * CAP + position
    arrival = jnp.arange(reps, dtype=jnp.int32)[:, None] * CAP + position
    my_bucket = lax.dynamic_index_in_dim(bucket, rep_index, 0, keepdims=False)
    slot_hit = my_bucket[None, :] == jnp.arange(reps * CAP, dtype=jnp.int32)[:, None]
    source_row = jnp.sum(
        jnp.where(slot_hit, jnp.arange(num_rows, dtype=jnp.int32)[None, :], 0), axis=1
    )
    outgoing = kv_cache[source_row]
    received = lax.all_to_all(outgoing, "rep", split_axis=0, concat_axis=0, tiled=True)
    my_slots = rep_index * num_rows + jnp.arange(num_rows, dtype=jnp.int32)
    slot_match = slot_table[None, :] == my_slots[:, None]
    pick_index = jnp.sum(jnp.where(slot_match, arrival.reshape(-1)[None, :], 0), axis=1)
    moved_blocks = jnp.sum(jnp.where(slot_match, length_table[None, :], 0), axis=1)
    moved_live = jnp.arange(span_len)[None, :] < (moved_blocks * BLOCK)[:, None]
    cache_moved = jnp.where(
        moved_live[:, None, :, None], received[pick_index], jnp.zeros((), jnp.bfloat16)
    )
    return (layer_out, cache_moved)


def solution(mesh):
    placed = (
        P(None, "rep", None),
        P(),
        P("rep", "tp"),
        P("rep", None, "tp"),
        P("tp", "rep"),
        P("rep", None, None, "tp"),
        P("rep"),
        P("rep"),
    )
    return jax.shard_map(
        per_device,
        mesh=mesh,
        in_specs=placed,
        out_specs=(P(None, "rep", "tp"), P("rep", None, None, "tp")),
        check_vma=False,
    )
```

```python
import jax
import jax.numpy as jnp
from jax import lax
from jax.experimental import pallas as pl
from jax.experimental.pallas import tpu as pltpu
from jax.sharding import PartitionSpec as P

HEADDIM = 128
BLOCK = 128
FIRST = 24
LATER = 8


def chip_shift(reps, shift):
    across, along = reps // 4, shift // 2
    pairs = []
    for one in range(reps):
        x, y, core = one // 4, one // 2 % 2, one % 2
        there = (x + along) % across * 4 + (y + shift) % 2 * 2 + core
        pairs.append((one, there))
    return pairs


def shift_between(source, target, chips):
    along = (target // 2 - source // 2) % (chips // 2)
    return along * 2 + (target - source) % 2


def route(slot_table, length_table, my_chip, chips):
    count = slot_table.shape[0] // chips
    lengths = length_table.reshape(chips, count)
    targets = (slot_table // count).reshape(chips, count)
    shared = targets[:, :, None] == targets[:, None, :]
    order = jnp.arange(count)
    place = jnp.sum(
        jnp.where(shared & (order[None, :] < order[:, None]), lengths[:, None, :], 0), axis=-1
    )
    sources = jnp.arange(chips, dtype=jnp.int32)[:, None]
    shifts = shift_between(sources, targets, chips)
    most = jnp.max(jnp.where(shifts > 0, place + lengths, 0))
    both = jnp.stack([shifts, place, lengths])
    pack_table = lax.dynamic_index_in_dim(both, my_chip, 1, keepdims=False)
    wanted = my_chip * count + order
    match = slot_table[None, :] == wanted[:, None]
    fields = jnp.concatenate(
        [
            both.reshape(3, -1),
            jnp.broadcast_to(order[None, :], (chips, count)).reshape(1, -1).astype(jnp.int32),
        ]
    )
    unpack_table = jnp.sum(jnp.where(match[None], fields[:, None, :], 0), axis=-1)
    return pack_table.astype(jnp.int32), unpack_table.astype(jnp.int32), most.astype(jnp.int32)


def blocks_of(cache, rows, block, core=None):
    span = pl.ds(pl.multiple_of(block * BLOCK, BLOCK), BLOCK)
    if core is None:
        return cache.at[rows, span]
    return cache.at[rows, core, span]


def pack_body(scalars, table, cache, lent, *rest):
    outs, sem = rest[:-1], rest[-1]
    core, start = scalars[0], scalars[1]
    room = outs[0].shape[0]
    requests = table.shape[1]
    half = requests // 2

    def send(at, total):
        shift, place, length = table[0, at], table[1, at], table[2, at]
        row = at % half
        low = jnp.maximum(start - place, 0)
        high = jnp.minimum(length, start + room - place)
        own = at // half == core
        for one, out in enumerate(outs, 1):

            @pl.when((shift == one) & own)
            def _():
                @pl.loop(low, high)
                def _(block):
                    pltpu.make_async_copy(
                        blocks_of(cache, row, block, core), out.at[place + block - start], sem
                    ).start()

            @pl.when((shift == one) & jnp.logical_not(own))
            def _():
                @pl.loop(low, high)
                def _(block):
                    pltpu.make_async_copy(
                        blocks_of(lent, row, block), out.at[place + block - start], sem
                    ).start()

        return total + jnp.where(shift > 0, jnp.maximum(high - low, 0), 0)

    total = lax.fori_loop(0, requests, send, jnp.int32(0))

    @pl.loop(0, total)
    def _(_):
        pltpu.make_async_copy(outs[0].at[0], outs[0].at[0], sem).wait()


def any_space(number):
    return [pl.BlockSpec(memory_space=pl.ANY)] * number


def smem_space(number):
    return [pl.BlockSpec(memory_space=pltpu.SMEM)] * number


def moved_cost(size):
    return pl.CostEstimate(flops=0, bytes_accessed=size, transcendentals=0)


def pack_kernel(core, start, table, cache, lent, room):
    block = jax.ShapeDtypeStruct((room, BLOCK, HEADDIM), jnp.bfloat16)
    scalars = jnp.stack([core, jnp.asarray(start, jnp.int32)]).astype(jnp.int32)
    return pl.pallas_call(
        pack_body,
        out_shape=[block] * 7,
        in_specs=smem_space(2) + any_space(2),
        out_specs=any_space(7),
        scratch_shapes=[pltpu.SemaphoreType.DMA],
        cost_estimate=moved_cost(8 << 20),
        name="pack_blocks",
    )(scalars, table, cache, lent)


def unpack_body(scalars, table, cache, lent, *rest):
    pieces, (moved, theirs, zeros, sem_mine, sem_theirs) = rest[:7], rest[7:]
    core = scalars[0]
    room = pieces[0].shape[0]
    half = theirs.shape[0]
    zeros[...] = jnp.zeros_like(zeros)
    most = cache.shape[2] // BLOCK

    def receive(slot, mine):
        at = jnp.where(mine, core, 1 - core) * half + slot
        sem = sem_mine if mine else sem_theirs
        shift, place, length, owner = table[0, at], table[1, at], table[2, at], table[3, at]
        row = owner % half
        inside = jnp.where(shift > 0, jnp.clip(room - place, 0, length), length)

        def target(block, many=1):
            span = pl.ds(pl.multiple_of(block * BLOCK, BLOCK), many * BLOCK)
            return moved.at[slot, core, span] if mine else theirs.at[slot, span]

        for one, piece in enumerate(pieces, 1):

            @pl.when(shift == one)
            def _():
                @pl.loop(0, inside)
                def _(block):
                    pltpu.make_async_copy(piece.at[place + block], target(block), sem).start()

        own = owner // half == core

        @pl.when((shift == 0) & own)
        def _():
            @pl.loop(0, inside)
            def _(block):
                pltpu.make_async_copy(
                    blocks_of(cache, row, block, core), target(block), sem
                ).start()

        @pl.when((shift == 0) & jnp.logical_not(own))
        def _():
            @pl.loop(0, inside)
            def _(block):
                pltpu.make_async_copy(blocks_of(lent, row, block), target(block), sem).start()

        rest_at = inside
        for many in (4, 2, 1):
            hit = (most - inside) & many

            @pl.when(hit > 0)
            def _():
                pltpu.make_async_copy(
                    zeros.at[pl.ds(0, many * BLOCK)], target(rest_at, many), sem
                ).start()

            rest_at = rest_at + hit

    @pl.loop(0, half)
    def _(slot):
        receive(slot, False)

    @pl.loop(0, half)
    def _(slot):
        receive(slot, True)

    pltpu.make_async_copy(theirs, theirs, sem_theirs).wait()
    pltpu.make_async_copy(theirs, theirs, sem_mine).wait()


def unpack_kernel(core, table, cache, lent, pieces):
    rows, _, span, width = cache.shape
    return pl.pallas_call(
        unpack_body,
        out_shape=[
            jax.ShapeDtypeStruct(cache.shape, jnp.bfloat16),
            jax.ShapeDtypeStruct((rows, span, width), jnp.bfloat16),
        ],
        in_specs=smem_space(2) + any_space(9),
        out_specs=any_space(2),
        scratch_shapes=[
            pltpu.VMEM((4 * BLOCK, width), jnp.bfloat16),
            pltpu.SemaphoreType.DMA,
            pltpu.SemaphoreType.DMA,
        ],
        cost_estimate=moved_cost(10 << 20),
        name="unpack_blocks",
    )(core[None].astype(jnp.int32), table, cache, lent, *pieces)


def unpack_more_body(scalars, table, *rest):
    pieces, (_, _, moved, theirs, sem) = rest[:7], rest[7:]
    core, start = scalars[0], scalars[1]
    room = pieces[0].shape[0]
    half = theirs.shape[0]

    def receive(at, total):
        shift, place, length = table[0, at], table[1, at], table[2, at]
        slot = at % half
        low = jnp.maximum(start - place, 0)
        high = jnp.minimum(length, start + room - place)
        mine = at // half == core
        for one, piece in enumerate(pieces, 1):

            @pl.when((shift == one) & mine)
            def _():
                @pl.loop(low, high)
                def _(block):
                    pltpu.make_async_copy(
                        piece.at[place + block - start], blocks_of(moved, slot, block, core), sem
                    ).start()

            @pl.when((shift == one) & jnp.logical_not(mine))
            def _():
                @pl.loop(low, high)
                def _(block):
                    pltpu.make_async_copy(
                        piece.at[place + block - start], blocks_of(theirs, slot, block), sem
                    ).start()

        return total + jnp.where(shift > 0, jnp.maximum(high - low, 0), 0)

    total = lax.fori_loop(0, 2 * half, receive, jnp.int32(0))

    @pl.loop(0, total)
    def _(_):
        pltpu.make_async_copy(pieces[0].at[0], pieces[0].at[0], sem).wait()


def unpack_more_kernel(core, start, table, pieces, moved, theirs):
    return pl.pallas_call(
        unpack_more_body,
        out_shape=[
            jax.ShapeDtypeStruct(moved.shape, moved.dtype),
            jax.ShapeDtypeStruct(theirs.shape, theirs.dtype),
        ],
        in_specs=smem_space(2) + any_space(9),
        out_specs=any_space(2),
        scratch_shapes=[pltpu.SemaphoreType.DMA],
        input_output_aliases={9: 0, 10: 1},
        name="unpack_later_blocks",
    )(jnp.stack([core, start]).astype(jnp.int32), table, *pieces, moved, theirs)


def finish_body(scalars, returned, _, moved, sem):
    copy = pltpu.make_async_copy(returned, moved.at[:, 1 - scalars[0]], sem)
    copy.start()
    copy.wait()


def finish_kernel(core, returned, moved):
    return pl.pallas_call(
        finish_body,
        out_shape=jax.ShapeDtypeStruct(moved.shape, moved.dtype),
        in_specs=smem_space(1) + any_space(2),
        out_specs=any_space(1)[0],
        scratch_shapes=[pltpu.SemaphoreType.DMA],
        input_output_aliases={2: 0},
        cost_estimate=moved_cost(6 << 20),
        name="put_other_kind",
    )(core[None].astype(jnp.int32), returned, moved)


def per_device(
    new_tokens, norm_gain, w_query, w_keyval, w_output, kv_cache, block_counts, new_slot
):
    reps = lax.axis_size("rep")
    tps = lax.axis_size("tp")
    rep_index = lax.axis_index("rep")
    core = rep_index % 2
    chips = reps // 2
    same_core = [[2 * chip + one for chip in range(chips)] for one in range(2)]
    other_core = [(one, one ^ 1) for one in range(reps)]
    num_steps, num_rows, feat_width = new_tokens.shape
    row_total = num_steps * num_rows
    all_rows = reps * row_total
    depth = feat_width // reps
    head_cols = w_query.shape[1]
    pair_cols = w_keyval.shape[2]
    group = head_cols // pair_cols
    out_cols = w_output.shape[1]
    span_len = kv_cache.shape[2]

    lent = lax.ppermute(
        lax.dynamic_index_in_dim(kv_cache, 1 - core, 1, keepdims=False), "rep", other_core
    )

    inputs_f = new_tokens.astype(jnp.float32)
    inverse = lax.rsqrt(jnp.mean(inputs_f * inputs_f, axis=-1, keepdims=True) + 1e-05)
    normed = (inputs_f * inverse * norm_gain.astype(jnp.float32)).astype(jnp.bfloat16)
    slabs = normed.reshape(row_total, reps, depth).transpose(1, 0, 2)
    table = jnp.concatenate([new_slot, block_counts]).astype(jnp.bfloat16)
    table = jnp.pad(table[None], ((0, 15), (0, depth - 2 * num_rows)))
    slabs = jnp.concatenate([slabs, jnp.broadcast_to(table, (reps, 16, depth))], axis=1)
    slabs = lax.all_to_all(slabs, "rep", split_axis=0, concat_axis=0, tiled=True)
    features = slabs[:, :row_total].reshape(all_rows, depth)
    table = slabs[:, row_total, : 2 * num_rows].astype(jnp.int32)
    slot_grid, length_grid = table[:, :num_rows], table[:, num_rows:]
    slot_table, length_table = slot_grid.reshape(-1), length_grid.reshape(-1)

    new_row = (slot_grid // num_rows * row_total + slot_grid % num_rows)[:, None, :]
    new_row = new_row + num_rows * jnp.arange(num_steps)[None, :, None]
    shuffle = (
        new_row.reshape(-1)[:, None] == jnp.arange(all_rows)[None, :]
    ).astype(jnp.bfloat16)
    features = jnp.dot(shuffle, features, preferred_element_type=jnp.bfloat16)
    weights = jnp.concatenate([w_query, w_keyval.reshape(depth, 2 * pair_cols)], axis=1)
    partial = jnp.dot(features, weights, preferred_element_type=jnp.float32)
    partial = partial.reshape(chips, 2, row_total, -1)
    mine = lax.dynamic_index_in_dim(partial, core, 1, keepdims=False)
    theirs = lax.dynamic_index_in_dim(partial, 1 - core, 1, keepdims=False)
    theirs = lax.ppermute(theirs.astype(jnp.bfloat16), "rep", other_core)
    pair_sum = (mine + theirs.astype(jnp.float32)).astype(jnp.bfloat16)
    pair_sum = lax.all_to_all(
        pair_sum, "rep", split_axis=0, concat_axis=0, tiled=True, axis_index_groups=same_core
    )
    projected = jnp.sum(pair_sum.astype(jnp.float32), axis=0).astype(jnp.bfloat16)
    query = projected[:, :head_cols].reshape(num_steps, num_rows, group, HEADDIM)
    fresh = projected[:, head_cols:].reshape(num_steps, num_rows, 2, HEADDIM)

    live = jnp.arange(span_len)[None, :] < (block_counts * BLOCK)[:, None]
    factor = 1.0 / HEADDIM**0.5
    cache_scores = (
        jnp.einsum("trgd,rld->rgtl", query, kv_cache[:, 0], preferred_element_type=jnp.float32)
        * factor
    )
    cache_scores = jnp.where(live[:, None, None, :], cache_scores, -1e30)
    fresh_scores = (
        jnp.einsum("trgd,urd->rgtu", query, fresh[:, :, 0], preferred_element_type=jnp.float32)
        * factor
    )
    causal = jnp.arange(num_steps)[None, :] <= jnp.arange(num_steps)[:, None]
    fresh_scores = jnp.where(causal, fresh_scores, -1e30)
    peak = jnp.maximum(jnp.max(cache_scores, -1), jnp.max(fresh_scores, -1))
    cache_exp = jnp.exp(cache_scores - peak[..., None])
    fresh_exp = jnp.exp(fresh_scores - peak[..., None])
    total = jnp.sum(cache_exp, -1) + jnp.sum(fresh_exp, -1)
    cache_prob = (cache_exp / total[..., None]).astype(jnp.bfloat16)
    fresh_prob = (fresh_exp / total[..., None]).astype(jnp.bfloat16)
    mixed = jnp.einsum(
        "rgtl,rld->trgd", cache_prob, kv_cache[:, 1], preferred_element_type=jnp.float32
    )
    mixed = mixed + jnp.einsum(
        "rgtu,urd->trgd", fresh_prob, fresh[:, :, 1], preferred_element_type=jnp.float32
    )
    attended = mixed.astype(jnp.bfloat16).reshape(row_total, head_cols)

    attended = lax.all_to_all(
        jnp.broadcast_to(attended[None], (reps, row_total, head_cols)),
        "rep",
        split_axis=0,
        concat_axis=0,
        tiled=True,
    ).reshape(all_rows, head_cols)
    attended = jnp.einsum("on,oc->nc", shuffle, attended, preferred_element_type=jnp.bfloat16)
    partial_out = jnp.dot(attended, w_output, preferred_element_type=jnp.float32)
    partial_out = lax.all_to_all(
        partial_out.astype(jnp.bfloat16).reshape(tps, all_rows // tps, out_cols),
        "tp",
        split_axis=0,
        concat_axis=0,
        tiled=True,
    )
    summed = jnp.sum(partial_out.astype(jnp.float32), axis=0).astype(jnp.bfloat16)
    summed = summed.reshape(2, row_total, out_cols)
    straight = [
        (r * tps + t, (2 * t + r % 2) * tps + r // 2) for r in range(reps) for t in range(tps)
    ]
    crossed = [
        (r * tps + t, (2 * t + 1 - r % 2) * tps + r // 2) for r in range(reps) for t in range(tps)
    ]
    near = lax.ppermute(
        lax.dynamic_index_in_dim(summed, core, 0, keepdims=False), ("rep", "tp"), straight
    )
    far = lax.ppermute(
        lax.dynamic_index_in_dim(summed, 1 - core, 0, keepdims=False), ("rep", "tp"), crossed
    )
    layer_out = jnp.where(
        core == 0,
        jnp.concatenate([near, far], axis=1),
        jnp.concatenate([far, near], axis=1),
    ).reshape(num_steps, num_rows, 2 * out_cols)

    my_chip = rep_index // 2
    pack_table, unpack_table, most = route(slot_table, length_table, my_chip, chips)
    sent = pack_kernel(core, 0, pack_table, kv_cache, lent, FIRST)
    arrived = [
        lax.ppermute(piece, "rep", chip_shift(reps, shift)) for shift, piece in enumerate(sent, 1)
    ]
    cache_moved, theirs = unpack_kernel(core, unpack_table, kv_cache, lent, arrived)

    def more(state):
        start, moved, other = state
        pieces = pack_kernel(core, start, pack_table, kv_cache, lent, LATER)
        pieces = [
            lax.ppermute(piece, "rep", chip_shift(reps, shift))
            for shift, piece in enumerate(pieces, 1)
        ]
        moved, other = unpack_more_kernel(core, start, unpack_table, pieces, moved, other)
        return start + LATER, moved, other

    _, cache_moved, theirs = lax.while_loop(
        lambda state: state[0] < most, more, (jnp.int32(FIRST), cache_moved, theirs)
    )
    returned = lax.ppermute(theirs, "rep", other_core)
    cache_moved = finish_kernel(core, returned, cache_moved)
    return (layer_out, cache_moved)


def solution(mesh):
    placed = (
        P(None, "rep", None),
        P(),
        P("rep", "tp"),
        P("rep", None, "tp"),
        P("tp", "rep"),
        P("rep", None, None, "tp"),
        P("rep"),
        P("rep"),
    )
    return jax.shard_map(
        per_device,
        mesh=mesh,
        in_specs=placed,
        out_specs=(P(None, "rep", "tp"), P("rep", None, None, "tp")),
        check_vma=False,
    )
```

```python
import jax
import jax.numpy as jnp
from jax import lax
from jax.experimental import pallas as pl
from jax.experimental.pallas import tpu as pltpu
from jax.sharding import PartitionSpec as P

HEADDIM = 128
BLOCK = 128
FIRST = 24
LATER = 8
VMEM_LIMIT = 32 << 20


def chip_shift(reps, shift):
    across, along = reps // 4, shift // 2
    pairs = []
    for one in range(reps):
        x, y, core = one // 4, one // 2 % 2, one % 2
        there = (x + along) % across * 4 + (y + shift) % 2 * 2 + core
        pairs.append((one, there))
    return pairs


def shift_between(source, target, chips):
    along = (target // 2 - source // 2) % (chips // 2)
    return along * 2 + (target - source) % 2


def route(slot_table, length_table, my_chip, chips):
    count = slot_table.shape[0] // chips
    lengths = length_table.reshape(chips, count)
    targets = (slot_table // count).reshape(chips, count)
    shared = targets[:, :, None] == targets[:, None, :]
    order = jnp.arange(count)
    place = jnp.sum(
        jnp.where(shared & (order[None, :] < order[:, None]), lengths[:, None, :], 0), axis=-1
    )
    sources = jnp.arange(chips, dtype=jnp.int32)[:, None]
    shifts = shift_between(sources, targets, chips)
    most = jnp.max(jnp.where(shifts > 0, place + lengths, 0))
    both = jnp.stack([shifts, place, lengths])
    pack_table = lax.dynamic_index_in_dim(both, my_chip, 1, keepdims=False)
    wanted = my_chip * count + order
    match = slot_table[None, :] == wanted[:, None]
    fields = jnp.concatenate(
        [
            both.reshape(3, -1),
            jnp.broadcast_to(order[None, :], (chips, count)).reshape(1, -1).astype(jnp.int32),
        ]
    )
    unpack_table = jnp.sum(jnp.where(match[None], fields[:, None, :], 0), axis=-1)
    return pack_table.astype(jnp.int32), unpack_table.astype(jnp.int32), most.astype(jnp.int32)


def blocks_of(cache, rows, block, core=None):
    span = pl.ds(pl.multiple_of(block * BLOCK, BLOCK), BLOCK)
    if core is None:
        return cache.at[rows, span]
    return cache.at[rows, core, span]


def pack_body(scalars, table, cache, lent, *rest):
    outs, held, sem, out_sem = rest[:7], rest[7], rest[8], rest[9]
    core, start = scalars[0], scalars[1]
    room = outs[0].shape[0]
    requests = table.shape[1]
    half = requests // 2

    def send(at, total):
        shift, place, length = table[0, at], table[1, at], table[2, at]
        row = at % half
        low = jnp.maximum(start - place, 0)
        high = jnp.minimum(length, start + room - place)
        own = at // half == core
        line = shift - 1

        @pl.when((shift > 0) & own)
        def _():
            @pl.loop(low, high)
            def _(block):
                pltpu.make_async_copy(
                    blocks_of(cache, row, block, core), held.at[line, place + block - start], sem
                ).start()

        @pl.when((shift > 0) & jnp.logical_not(own))
        def _():
            @pl.loop(low, high)
            def _(block):
                pltpu.make_async_copy(
                    blocks_of(lent, row, block), held.at[line, place + block - start], sem
                ).start()

        return total + jnp.where(shift > 0, jnp.maximum(high - low, 0), 0)

    total = lax.fori_loop(0, requests, send, jnp.int32(0))

    @pl.loop(0, total)
    def _(_):
        pltpu.make_async_copy(held.at[0, 0], held.at[0, 0], sem).wait()

    copies = [
        pltpu.make_async_copy(held.at[line], out, out_sem.at[line])
        for line, out in enumerate(outs)
    ]
    for copy in copies:
        copy.start()
    for copy in copies:
        copy.wait()


def any_space(number):
    return [pl.BlockSpec(memory_space=pl.ANY)] * number


def smem_space(number):
    return [pl.BlockSpec(memory_space=pltpu.SMEM)] * number


def moved_cost(size):
    return pl.CostEstimate(flops=0, bytes_accessed=size, transcendentals=0)


def pack_kernel(core, start, table, cache, lent, room):
    block = jax.ShapeDtypeStruct((room, BLOCK, HEADDIM), jnp.bfloat16)
    scalars = jnp.stack([core, jnp.asarray(start, jnp.int32)]).astype(jnp.int32)
    return pl.pallas_call(
        pack_body,
        out_shape=[block] * 7,
        in_specs=smem_space(2) + any_space(2),
        out_specs=any_space(7),
        scratch_shapes=[
            pltpu.VMEM((7,) + block.shape, jnp.bfloat16),
            pltpu.SemaphoreType.DMA,
            pltpu.SemaphoreType.DMA((7,)),
        ],
        compiler_params=pltpu.CompilerParams(vmem_limit_bytes=VMEM_LIMIT),
        cost_estimate=moved_cost(8 << 20),
        name="pack_blocks",
    )(scalars, table, cache, lent)


def unpack_body(scalars, table, cache, lent, *rest):
    pieces, (moved, theirs, held, sem, out_sem) = rest[:7], rest[7:]
    core = scalars[0]
    room = pieces[0].shape[0]
    half = theirs.shape[0]
    most = cache.shape[2] // BLOCK

    def receive(at, total):
        shift, place, length, owner = table[0, at], table[1, at], table[2, at], table[3, at]
        row = owner % half
        inside = jnp.where(shift > 0, jnp.clip(room - place, 0, length), length)
        own = owner // half == core

        def fetch(condition, source):
            @pl.when(condition)
            def _():
                @pl.loop(0, inside)
                def _(block):
                    pltpu.make_async_copy(source(block), blocks_of(held, at, block), sem).start()

        for one, piece in enumerate(pieces, 1):
            fetch(shift == one, lambda block, piece=piece: piece.at[place + block])
        fetch((shift == 0) & own, lambda block: blocks_of(cache, row, block, core))
        fetch((shift == 0) & jnp.logical_not(own), lambda block: blocks_of(lent, row, block))

        @pl.loop(inside, most)
        def _(block):
            span = pl.ds(pl.multiple_of(block * BLOCK, BLOCK), BLOCK)
            held[at, span] = jnp.zeros((BLOCK, HEADDIM), held.dtype)

        return total + inside

    total = lax.fori_loop(0, 2 * half, receive, jnp.int32(0))

    @pl.loop(0, total)
    def _(_):
        pltpu.make_async_copy(pieces[0].at[0], pieces[0].at[0], sem).wait()

    copies = [
        pltpu.make_async_copy(held.at[pl.ds((1 - core) * half, half)], theirs, out_sem.at[0]),
        pltpu.make_async_copy(held.at[pl.ds(core * half, half)], moved.at[:, core], out_sem.at[1]),
    ]
    for copy in copies:
        copy.start()
    for copy in copies:
        copy.wait()


def unpack_kernel(core, table, cache, lent, pieces):
    rows, _, span, width = cache.shape
    return pl.pallas_call(
        unpack_body,
        out_shape=[
            jax.ShapeDtypeStruct(cache.shape, jnp.bfloat16),
            jax.ShapeDtypeStruct((rows, span, width), jnp.bfloat16),
        ],
        in_specs=smem_space(2) + any_space(9),
        out_specs=any_space(2),
        scratch_shapes=[
            pltpu.VMEM((2 * rows, span, width), jnp.bfloat16),
            pltpu.SemaphoreType.DMA,
            pltpu.SemaphoreType.DMA((2,)),
        ],
        compiler_params=pltpu.CompilerParams(vmem_limit_bytes=VMEM_LIMIT),
        cost_estimate=moved_cost(10 << 20),
        name="unpack_blocks",
    )(core[None].astype(jnp.int32), table, cache, lent, *pieces)


def unpack_more_body(scalars, table, *rest):
    pieces, (_, _, moved, theirs, held, sem) = rest[:7], rest[7:]
    core, start = scalars[0], scalars[1]
    room = pieces[0].shape[0]
    half = theirs.shape[0]
    fetches = [
        pltpu.make_async_copy(piece, held.at[line], sem) for line, piece in enumerate(pieces)
    ]
    for fetch in fetches:
        fetch.start()
    for fetch in fetches:
        fetch.wait()

    def receive(at, total):
        shift, place, length = table[0, at], table[1, at], table[2, at]
        slot = at % half
        low = jnp.maximum(start - place, 0)
        high = jnp.minimum(length, start + room - place)
        mine = at // half == core
        line = shift - 1

        @pl.when((shift > 0) & mine)
        def _():
            @pl.loop(low, high)
            def _(block):
                pltpu.make_async_copy(
                    held.at[line, place + block - start], blocks_of(moved, slot, block, core), sem
                ).start()

        @pl.when((shift > 0) & jnp.logical_not(mine))
        def _():
            @pl.loop(low, high)
            def _(block):
                pltpu.make_async_copy(
                    held.at[line, place + block - start], blocks_of(theirs, slot, block), sem
                ).start()

        return total + jnp.where(shift > 0, jnp.maximum(high - low, 0), 0)

    total = lax.fori_loop(0, 2 * half, receive, jnp.int32(0))

    @pl.loop(0, total)
    def _(_):
        pltpu.make_async_copy(held.at[0, 0], held.at[0, 0], sem).wait()


def unpack_more_kernel(core, start, table, pieces, moved, theirs):
    return pl.pallas_call(
        unpack_more_body,
        out_shape=[
            jax.ShapeDtypeStruct(moved.shape, moved.dtype),
            jax.ShapeDtypeStruct(theirs.shape, theirs.dtype),
        ],
        in_specs=smem_space(2) + any_space(9),
        out_specs=any_space(2),
        scratch_shapes=[
            pltpu.VMEM((7,) + pieces[0].shape, jnp.bfloat16),
            pltpu.SemaphoreType.DMA,
        ],
        compiler_params=pltpu.CompilerParams(vmem_limit_bytes=VMEM_LIMIT),
        input_output_aliases={9: 0, 10: 1},
        name="unpack_later_blocks",
    )(jnp.stack([core, start]).astype(jnp.int32), table, *pieces, moved, theirs)


def finish_body(scalars, returned, _, moved, held, in_sem, out_sem):
    parts = in_sem.shape[0]
    rows = returned.shape[0] // parts
    spans = [pl.ds(part * rows, rows) for part in range(parts)]
    fetches = [
        pltpu.make_async_copy(returned.at[span], held.at[span], in_sem.at[part])
        for part, span in enumerate(spans)
    ]
    stores = [
        pltpu.make_async_copy(held.at[span], moved.at[span, 1 - scalars[0]], out_sem.at[part])
        for part, span in enumerate(spans)
    ]
    for fetch in fetches:
        fetch.start()
    for fetch, store in zip(fetches, stores):
        fetch.wait()
        store.start()
    for store in stores:
        store.wait()


def finish_kernel(core, returned, moved):
    return pl.pallas_call(
        finish_body,
        out_shape=jax.ShapeDtypeStruct(moved.shape, moved.dtype),
        in_specs=smem_space(1) + any_space(2),
        out_specs=any_space(1)[0],
        scratch_shapes=[
            pltpu.VMEM(returned.shape, returned.dtype),
            pltpu.SemaphoreType.DMA((4,)),
            pltpu.SemaphoreType.DMA((4,)),
        ],
        compiler_params=pltpu.CompilerParams(vmem_limit_bytes=VMEM_LIMIT),
        input_output_aliases={2: 0},
        cost_estimate=moved_cost(6 << 20),
        name="put_other_kind",
    )(core[None].astype(jnp.int32), returned, moved)


def per_device(
    new_tokens, norm_gain, w_query, w_keyval, w_output, kv_cache, block_counts, new_slot
):
    reps = lax.axis_size("rep")
    tps = lax.axis_size("tp")
    rep_index = lax.axis_index("rep")
    core = rep_index % 2
    chips = reps // 2
    same_core = [[2 * chip + one for chip in range(chips)] for one in range(2)]
    other_core = [(one, one ^ 1) for one in range(reps)]
    num_steps, num_rows, feat_width = new_tokens.shape
    row_total = num_steps * num_rows
    all_rows = reps * row_total
    depth = feat_width // reps
    head_cols = w_query.shape[1]
    pair_cols = w_keyval.shape[2]
    group = head_cols // pair_cols
    out_cols = w_output.shape[1]
    span_len = kv_cache.shape[2]

    lent = lax.ppermute(
        lax.dynamic_index_in_dim(kv_cache, 1 - core, 1, keepdims=False), "rep", other_core
    )

    inputs_f = new_tokens.astype(jnp.float32)
    inverse = lax.rsqrt(jnp.mean(inputs_f * inputs_f, axis=-1, keepdims=True) + 1e-05)
    normed = (inputs_f * inverse * norm_gain.astype(jnp.float32)).astype(jnp.bfloat16)
    slabs = normed.reshape(row_total, reps, depth).transpose(1, 0, 2)
    table = jnp.concatenate([new_slot, block_counts]).astype(jnp.bfloat16)
    table = jnp.pad(table[None], ((0, 15), (0, depth - 2 * num_rows)))
    slabs = jnp.concatenate([slabs, jnp.broadcast_to(table, (reps, 16, depth))], axis=1)
    slabs = lax.all_to_all(slabs, "rep", split_axis=0, concat_axis=0, tiled=True)
    features = slabs[:, :row_total].reshape(all_rows, depth)
    table = slabs[:, row_total, : 2 * num_rows].astype(jnp.int32)
    slot_grid, length_grid = table[:, :num_rows], table[:, num_rows:]
    slot_table, length_table = slot_grid.reshape(-1), length_grid.reshape(-1)

    new_row = (slot_grid // num_rows * row_total + slot_grid % num_rows)[:, None, :]
    new_row = new_row + num_rows * jnp.arange(num_steps)[None, :, None]
    shuffle = (
        new_row.reshape(-1)[:, None] == jnp.arange(all_rows)[None, :]
    ).astype(jnp.bfloat16)
    features = jnp.dot(shuffle, features, preferred_element_type=jnp.bfloat16)
    weights = jnp.concatenate([w_query, w_keyval.reshape(depth, 2 * pair_cols)], axis=1)
    partial = jnp.dot(features, weights, preferred_element_type=jnp.float32)
    partial = partial.reshape(chips, 2, row_total, -1)
    mine = lax.dynamic_index_in_dim(partial, core, 1, keepdims=False)
    theirs = lax.dynamic_index_in_dim(partial, 1 - core, 1, keepdims=False)
    theirs = lax.ppermute(theirs.astype(jnp.bfloat16), "rep", other_core)
    pair_sum = (mine + theirs.astype(jnp.float32)).astype(jnp.bfloat16)
    pair_sum = lax.all_to_all(
        pair_sum, "rep", split_axis=0, concat_axis=0, tiled=True, axis_index_groups=same_core
    )
    projected = jnp.sum(pair_sum.astype(jnp.float32), axis=0).astype(jnp.bfloat16)
    query = projected[:, :head_cols].reshape(num_steps, num_rows, group, HEADDIM)
    fresh = projected[:, head_cols:].reshape(num_steps, num_rows, 2, HEADDIM)

    live = jnp.arange(span_len)[None, :] < (block_counts * BLOCK)[:, None]
    factor = 1.0 / HEADDIM**0.5
    cache_scores = (
        jnp.einsum("trgd,rld->rgtl", query, kv_cache[:, 0], preferred_element_type=jnp.float32)
        * factor
    )
    cache_scores = jnp.where(live[:, None, None, :], cache_scores, -1e30)
    fresh_scores = (
        jnp.einsum("trgd,urd->rgtu", query, fresh[:, :, 0], preferred_element_type=jnp.float32)
        * factor
    )
    causal = jnp.arange(num_steps)[None, :] <= jnp.arange(num_steps)[:, None]
    fresh_scores = jnp.where(causal, fresh_scores, -1e30)
    peak = jnp.maximum(jnp.max(cache_scores, -1), jnp.max(fresh_scores, -1))
    cache_exp = jnp.exp(cache_scores - peak[..., None])
    fresh_exp = jnp.exp(fresh_scores - peak[..., None])
    total = jnp.sum(cache_exp, -1) + jnp.sum(fresh_exp, -1)
    cache_prob = (cache_exp / total[..., None]).astype(jnp.bfloat16)
    fresh_prob = (fresh_exp / total[..., None]).astype(jnp.bfloat16)
    mixed = jnp.einsum(
        "rgtl,rld->trgd", cache_prob, kv_cache[:, 1], preferred_element_type=jnp.float32
    )
    mixed = mixed + jnp.einsum(
        "rgtu,urd->trgd", fresh_prob, fresh[:, :, 1], preferred_element_type=jnp.float32
    )
    attended = mixed.astype(jnp.bfloat16).reshape(row_total, head_cols)

    attended = lax.all_to_all(
        jnp.broadcast_to(attended[None], (reps, row_total, head_cols)),
        "rep",
        split_axis=0,
        concat_axis=0,
        tiled=True,
    ).reshape(all_rows, head_cols)
    attended = jnp.einsum("on,oc->nc", shuffle, attended, preferred_element_type=jnp.bfloat16)
    partial_out = jnp.dot(attended, w_output, preferred_element_type=jnp.float32)
    partial_out = lax.all_to_all(
        partial_out.astype(jnp.bfloat16).reshape(tps, all_rows // tps, out_cols),
        "tp",
        split_axis=0,
        concat_axis=0,
        tiled=True,
    )
    summed = jnp.sum(partial_out.astype(jnp.float32), axis=0).astype(jnp.bfloat16)
    summed = summed.reshape(2, row_total, out_cols)
    straight = [
        (r * tps + t, (2 * t + r % 2) * tps + r // 2) for r in range(reps) for t in range(tps)
    ]
    crossed = [
        (r * tps + t, (2 * t + 1 - r % 2) * tps + r // 2) for r in range(reps) for t in range(tps)
    ]
    near = lax.ppermute(
        lax.dynamic_index_in_dim(summed, core, 0, keepdims=False), ("rep", "tp"), straight
    )
    far = lax.ppermute(
        lax.dynamic_index_in_dim(summed, 1 - core, 0, keepdims=False), ("rep", "tp"), crossed
    )
    layer_out = jnp.where(
        core == 0,
        jnp.concatenate([near, far], axis=1),
        jnp.concatenate([far, near], axis=1),
    ).reshape(num_steps, num_rows, 2 * out_cols)

    my_chip = rep_index // 2
    pack_table, unpack_table, most = route(slot_table, length_table, my_chip, chips)
    sent = pack_kernel(core, 0, pack_table, kv_cache, lent, FIRST)
    arrived = [
        lax.ppermute(piece, "rep", chip_shift(reps, shift)) for shift, piece in enumerate(sent, 1)
    ]
    cache_moved, theirs = unpack_kernel(core, unpack_table, kv_cache, lent, arrived)

    def more(state):
        start, moved, other = state
        pieces = pack_kernel(core, start, pack_table, kv_cache, lent, LATER)
        pieces = [
            lax.ppermute(piece, "rep", chip_shift(reps, shift))
            for shift, piece in enumerate(pieces, 1)
        ]
        moved, other = unpack_more_kernel(core, start, unpack_table, pieces, moved, other)
        return start + LATER, moved, other

    _, cache_moved, theirs = lax.while_loop(
        lambda state: state[0] < most, more, (jnp.int32(FIRST), cache_moved, theirs)
    )
    returned = lax.ppermute(theirs, "rep", other_core)
    cache_moved = finish_kernel(core, returned, cache_moved)
    return (layer_out, cache_moved)


def solution(mesh):
    placed = (
        P(None, "rep", None),
        P(),
        P("rep", "tp"),
        P("rep", None, "tp"),
        P("tp", "rep"),
        P("rep", None, None, "tp"),
        P("rep"),
        P("rep"),
    )
    return jax.shard_map(
        per_device,
        mesh=mesh,
        in_specs=placed,
        out_specs=(P(None, "rep", "tp"), P("rep", None, None, "tp")),
        check_vma=False,
    )
```

```python
import jax
import jax.numpy as jnp
from jax import lax
from jax.experimental import pallas as pl
from jax.experimental.pallas import tpu as pltpu
from jax.sharding import PartitionSpec as P

HEADDIM = 128
BLOCK = 128
ROOM = 38
LATER = 4
VMEM_LIMIT = 56 << 20


def line_pairs(reps, line, along_first):
    across, pairs = reps // 4, []
    for one in range(reps):
        x, y, core = one // 4, one // 2 % 2, one % 2
        if core == along_first:
            pairs.append((one, (x + (1, 3, 2)[line]) % across * 4 + y * 2 + core))
        elif line < 2:
            pairs.append((one, x * 4 + (1 - y) * 2 + core))
    return pairs


def places(key, lengths):
    order = jnp.arange(key.shape[0])
    before = (key[:, None] == key[None, :]) & (order[None, :] < order[:, None])
    return jnp.sum(jnp.where(before, lengths[None, :], 0), axis=-1)


def x_leg(source, target, key, lengths):
    along = (target // 2 - source // 2) % 4
    moves = along > 0
    place = places(key, jnp.where(moves, lengths, 0))
    line = jnp.where(along == 1, 0, jnp.where(along == 3, 1, 2))
    return moves, line * ROOM + place, jnp.where(moves, ROOM - place, lengths)


def y_leg(source, target, key, lengths):
    moves = target % 2 != source % 2
    place = places(key, jnp.where(moves, lengths, 0))
    return moves, place, jnp.where(moves, 2 * ROOM - place, lengths)


def first_leg(core, source, target, lengths):
    x = x_leg(source, target, source * 4 + target // 2, lengths)
    y = y_leg(source, target, source * 2 + target % 2, lengths)
    return [jnp.where(core == 0, one, other) for one, other in zip(x, y)]


def second_leg(core, source, target, lengths):
    x = x_leg(source, target, source // 2 * 8 + target, lengths)
    y = y_leg(source, target, source % 2 * 8 + target, lengths)
    return [jnp.where(core == 0, one, other) for one, other in zip(y, x)]


def pick(match, fields):
    return jnp.sum(jnp.where(match[None], jnp.stack(fields)[:, None, :], 0), axis=-1).astype(
        jnp.int32
    )


def blocks_of(cache, rows, block, core=None):
    span = pl.ds(pl.multiple_of(block * BLOCK, BLOCK), BLOCK)
    if core is None:
        return cache.at[rows, span]
    return cache.at[rows, core, span]


def fetch_blocks(entry, core, cache, lent, legs, put, sem):
    place, at, count = entry

    def fetch(condition, source):
        @pl.when(condition)
        def _():
            @pl.loop(0, count)
            def _(block):
                pltpu.make_async_copy(source(block), put(block), sem).start()

    fetch(place == 1, lambda block: blocks_of(cache, at, block, core))
    fetch(place == 2, lambda block: blocks_of(lent, at, block))
    for number, lines in enumerate(legs, 3):

        @pl.when(place == number)
        def _():
            @pl.loop(0, count)
            def _(block):
                spot = at + block
                for one, line in enumerate(lines):

                    @pl.when(spot // ROOM == one)
                    def _():
                        pltpu.make_async_copy(
                            line.at[spot - one * ROOM], put(block), sem
                        ).start()

    return jnp.where(place > 0, jnp.maximum(count, 0), 0)


def wait_blocks(total, example, sem):
    @pl.loop(0, total)
    def _(_):
        pltpu.make_async_copy(example, example, sem).wait()


def pack_body(core, table, cache, lent, *rest):
    lines, (out, held, sem, out_sem) = rest[:-6], (rest[-6:-3],) + rest[-3:]

    def send(at, total):
        to = table[2, at]
        entry = (table[0, at], table[1, at], table[3, at])
        return total + fetch_blocks(
            entry, core[0], cache, lent, [lines], lambda block: held.at[to + block], sem
        )

    total = lax.fori_loop(0, table.shape[1], send, jnp.int32(0))
    wait_blocks(total, held.at[0], sem)
    copies = [
        pltpu.make_async_copy(held.at[pl.ds(line * ROOM, ROOM)], one, out_sem.at[line])
        for line, one in enumerate(out)
    ]
    for copy in copies:
        copy.start()
    for copy in copies:
        copy.wait()


def any_space(number):
    return [pl.BlockSpec(memory_space=pl.ANY)] * number


def smem_space(number):
    return [pl.BlockSpec(memory_space=pltpu.SMEM)] * number


def moved_cost(size):
    return pl.CostEstimate(flops=0, bytes_accessed=size, transcendentals=0)


def pack_kernel(core, table, cache, lent, lines):
    line = jax.ShapeDtypeStruct((ROOM, BLOCK, HEADDIM), jnp.bfloat16)
    return pl.pallas_call(
        pack_body,
        out_shape=[line] * 3,
        in_specs=smem_space(2) + any_space(2 + len(lines)),
        out_specs=any_space(3),
        scratch_shapes=[
            pltpu.VMEM((3 * ROOM, BLOCK, HEADDIM), jnp.bfloat16),
            pltpu.SemaphoreType.DMA,
            pltpu.SemaphoreType.DMA((3,)),
        ],
        compiler_params=pltpu.CompilerParams(vmem_limit_bytes=VMEM_LIMIT),
        cost_estimate=moved_cost(8 << 20),
        name="pack_blocks",
    )(core[None].astype(jnp.int32), table, cache, lent, *lines)


def unpack_body(scalars, table, cache, lent, *rest):
    first, second, rest = rest[:3], rest[3:6], rest[6:]
    _, moved, theirs, held, sem, out_sem = rest
    core = scalars[0]
    half = theirs.shape[0]
    most = cache.shape[2] // BLOCK

    def receive(at, total):
        count = table[2, at]
        entry = (table[0, at], table[1, at], count)

        @pl.loop(count, most)
        def _(block):
            span = pl.ds(pl.multiple_of(block * BLOCK, BLOCK), BLOCK)
            held[at, span] = jnp.zeros((BLOCK, HEADDIM), held.dtype)

        return total + fetch_blocks(
            entry, core, cache, lent, [first, second], lambda block: blocks_of(held, at, block), sem
        )

    total = lax.fori_loop(0, 2 * half, receive, jnp.int32(0))
    wait_blocks(total, first[0].at[0], sem)
    copies = [
        pltpu.make_async_copy(held.at[pl.ds((1 - core) * half, half)], theirs, out_sem.at[0]),
        pltpu.make_async_copy(held.at[pl.ds(core * half, half)], moved.at[:, core], out_sem.at[1]),
    ]
    for copy in copies:
        copy.start()
    for copy in copies:
        copy.wait()


def unpack_kernel(core, table, cache, lent, first, second, after):
    rows, _, span, width = cache.shape
    return pl.pallas_call(
        unpack_body,
        out_shape=[
            jax.ShapeDtypeStruct(cache.shape, jnp.bfloat16),
            jax.ShapeDtypeStruct((rows, span, width), jnp.bfloat16),
        ],
        in_specs=smem_space(2) + any_space(9),
        out_specs=any_space(2),
        scratch_shapes=[
            pltpu.VMEM((2 * rows, span, width), jnp.bfloat16),
            pltpu.SemaphoreType.DMA,
            pltpu.SemaphoreType.DMA((2,)),
        ],
        compiler_params=pltpu.CompilerParams(vmem_limit_bytes=VMEM_LIMIT),
        cost_estimate=moved_cost(10 << 20),
        name="unpack_blocks",
    )(core[None].astype(jnp.int32), table, cache, lent, *first, *second, after)


def pack_more_body(scalars, table, cache, lent, out, held, sem):
    core, start = scalars[0], scalars[1]
    room = out.shape[1]
    requests = table.shape[1]
    half = requests // 2

    def send(at, total):
        line, place, skip, left = (table[field, at] for field in range(4))
        low = jnp.maximum(start - place, 0)
        count = jnp.maximum(jnp.minimum(left, start + room - place) - low, 0)

        def fetch(condition, source):
            @pl.when(condition)
            def _():
                @pl.loop(0, count)
                def _(block):
                    pltpu.make_async_copy(
                        source(skip + low + block), held.at[line, place + low + block - start], sem
                    ).start()

        row = at % half
        fetch(at // half == core, lambda block: blocks_of(cache, row, block, core))
        fetch(at // half != core, lambda block: blocks_of(lent, row, block))
        return total + count

    total = lax.fori_loop(0, requests, send, jnp.int32(0))
    wait_blocks(total, held.at[0, 0], sem)
    copy = pltpu.make_async_copy(held, out, sem)
    copy.start()
    copy.wait()


def pack_more_kernel(core, start, table, cache, lent, chips):
    lines = jax.ShapeDtypeStruct((chips, LATER, BLOCK, HEADDIM), jnp.bfloat16)
    return pl.pallas_call(
        pack_more_body,
        out_shape=lines,
        in_specs=smem_space(2) + any_space(2),
        out_specs=any_space(1)[0],
        scratch_shapes=[pltpu.VMEM(lines.shape, lines.dtype), pltpu.SemaphoreType.DMA],
        compiler_params=pltpu.CompilerParams(vmem_limit_bytes=VMEM_LIMIT),
        name="pack_later_blocks",
    )(jnp.stack([core, start]).astype(jnp.int32), table, cache, lent)


def unpack_more_body(scalars, table, pieces, _moved, _theirs, moved, theirs, held, sem):
    core, start = scalars[0], scalars[1]
    room = pieces.shape[1]
    half = theirs.shape[0]
    copy = pltpu.make_async_copy(pieces, held, sem)
    copy.start()
    copy.wait()

    def receive(at, total):
        line, place, skip, left = (table[field, at] for field in range(4))
        slot = at % half
        low = jnp.maximum(start - place, 0)
        count = jnp.maximum(jnp.minimum(left, start + room - place) - low, 0)

        def put(condition, target):
            @pl.when(condition)
            def _():
                @pl.loop(0, count)
                def _(block):
                    pltpu.make_async_copy(
                        held.at[line, place + low + block - start], target(skip + low + block), sem
                    ).start()

        put(at // half == core, lambda block: blocks_of(moved, slot, block, core))
        put(at // half != core, lambda block: blocks_of(theirs, slot, block))
        return total + count

    total = lax.fori_loop(0, 2 * half, receive, jnp.int32(0))
    wait_blocks(total, held.at[0, 0], sem)


def unpack_more_kernel(core, start, table, pieces, moved, theirs):
    return pl.pallas_call(
        unpack_more_body,
        out_shape=[
            jax.ShapeDtypeStruct(moved.shape, moved.dtype),
            jax.ShapeDtypeStruct(theirs.shape, theirs.dtype),
        ],
        in_specs=smem_space(2) + any_space(3),
        out_specs=any_space(2),
        scratch_shapes=[pltpu.VMEM(pieces.shape, pieces.dtype), pltpu.SemaphoreType.DMA],
        input_output_aliases={3: 0, 4: 1},
        compiler_params=pltpu.CompilerParams(vmem_limit_bytes=VMEM_LIMIT),
        name="unpack_later_blocks",
    )(jnp.stack([core, start]).astype(jnp.int32), table, pieces, moved, theirs)


def finish_body(scalars, returned, _, moved, held, in_sem, out_sem):
    parts = in_sem.shape[0]
    rows = returned.shape[0] // parts
    spans = [pl.ds(part * rows, rows) for part in range(parts)]
    fetches = [
        pltpu.make_async_copy(returned.at[span], held.at[span], in_sem.at[part])
        for part, span in enumerate(spans)
    ]
    stores = [
        pltpu.make_async_copy(held.at[span], moved.at[span, 1 - scalars[0]], out_sem.at[part])
        for part, span in enumerate(spans)
    ]
    for fetch in fetches:
        fetch.start()
    for fetch, store in zip(fetches, stores):
        fetch.wait()
        store.start()
    for store in stores:
        store.wait()


def finish_kernel(core, returned, moved):
    return pl.pallas_call(
        finish_body,
        out_shape=jax.ShapeDtypeStruct(moved.shape, moved.dtype),
        in_specs=smem_space(1) + any_space(2),
        out_specs=any_space(1)[0],
        scratch_shapes=[
            pltpu.VMEM(returned.shape, returned.dtype),
            pltpu.SemaphoreType.DMA((4,)),
            pltpu.SemaphoreType.DMA((4,)),
        ],
        compiler_params=pltpu.CompilerParams(vmem_limit_bytes=VMEM_LIMIT),
        input_output_aliases={2: 0},
        cost_estimate=moved_cost(6 << 20),
        name="put_other_kind",
    )(core[None].astype(jnp.int32), returned, moved)


def norm_body(tokens, gain, table, out):
    rows, width = tokens.shape
    reps, _, depth = out.shape
    chunk = 1024
    total = jnp.zeros((rows, 1), jnp.float32)
    for at in range(0, width, chunk):
        part = tokens[:, at : at + chunk].astype(jnp.float32)
        total = total + jnp.sum(part * part, axis=-1, keepdims=True)
    inverse = lax.rsqrt(total * (1.0 / width) + 1e-05)
    for rep in range(reps):
        span = slice(rep * depth, (rep + 1) * depth)
        part = tokens[:, span].astype(jnp.float32) * inverse * gain[:, span].astype(jnp.float32)
        out[rep, :rows] = part.astype(jnp.bfloat16)
        out[rep, rows:] = table[...]


def norm_kernel(tokens, gain, table, reps):
    rows, width = tokens.shape
    return pl.pallas_call(
        norm_body,
        out_shape=jax.ShapeDtypeStruct((reps, rows + 16, width // reps), jnp.bfloat16),
        compiler_params=pltpu.CompilerParams(vmem_limit_bytes=VMEM_LIMIT),
        cost_estimate=moved_cost(4 << 20),
        name="norm_rows",
    )(tokens, gain, table)


def project_body(core, slabs, w_query, w_keyval, _, mine, theirs, held):
    reps, rows, depth = slabs.shape
    count = 16
    steps = (rows - count) // count
    requests = reps * count
    owners = slabs[:, rows - count :, :requests].reshape(requests, requests).astype(jnp.float32)
    number = lax.broadcasted_iota(jnp.int32, (requests, requests), 1).astype(jnp.float32)
    shuffle = jnp.where(owners == number, 1.0, 0.0).astype(jnp.bfloat16)
    query_cols = w_query.shape[1]
    for step in range(steps):
        span = slice(step * count, (step + 1) * count)
        features = slabs[:, span].reshape(requests, depth)
        features = jnp.dot(shuffle, features, preferred_element_type=jnp.float32)
        features = features.astype(jnp.bfloat16)
        for weight, at in ((w_query, 0), (w_keyval, query_cols)):
            product = jnp.dot(features, weight[...], preferred_element_type=jnp.float32)
            width = product.shape[1]
            held[:, :, at : at + width] = product.astype(jnp.bfloat16).reshape(reps, count, width)
        for one in range(2):

            @pl.when(core[0] == one)
            def _():
                for chip in range(reps // 2):
                    mine[chip, span] = held[2 * chip + one]
                    theirs[chip, span] = held[2 * chip + 1 - one]


def project_kernel(core, slabs, w_query, w_keyval, after):
    reps, rows, _ = slabs.shape
    width = w_query.shape[1] + w_keyval.shape[1]
    half = jax.ShapeDtypeStruct((reps // 2, rows - 16, width), jnp.bfloat16)
    vmem = pl.BlockSpec(memory_space=pltpu.VMEM)
    return pl.pallas_call(
        project_body,
        out_shape=[half, half],
        in_specs=smem_space(1) + [vmem] * 3 + any_space(1),
        out_specs=[vmem] * 2,
        scratch_shapes=[pltpu.VMEM((reps, 16, width), jnp.bfloat16)],
        compiler_params=pltpu.CompilerParams(vmem_limit_bytes=VMEM_LIMIT),
        cost_estimate=moved_cost(6 << 20),
        name="project_rows",
    )(core[None].astype(jnp.int32), slabs, w_query, w_keyval, after)


def attend_body(counts, sums, cache, *rest):
    out, queries, keys, values, mixed = rest[-5:]
    at = pl.program_id(0)
    together, _, span, width = cache.shape
    rows = sums.shape[1]
    per_step = 16
    steps = rows // per_step
    heads = (sums.shape[2] - 2 * width) // width

    @pl.when(at == 0)
    def _():
        for head in range(heads + 2):
            cols = slice(head * width, (head + 1) * width)
            total = jnp.sum(sums[:, :, cols].astype(jnp.float32), axis=0)
            total = total.astype(jnp.bfloat16).astype(jnp.float32)
            if head < heads:
                queries[head * rows : (head + 1) * rows] = total
            elif head == heads:
                keys[...] = total
            else:
                values[...] = total

    many = heads * steps
    flat = (((1,), (1,)), ((), ()))
    factor = 1.0 / width**0.5
    for one in range(together):
        request = at * together + one
        live = counts[request] * BLOCK
        query = queries[pl.ds(request, many, stride=per_step)].astype(jnp.bfloat16)
        key = keys[pl.ds(request, steps, stride=per_step)].astype(jnp.bfloat16)
        value = values[pl.ds(request, steps, stride=per_step)].astype(jnp.bfloat16)
        old = lax.dot_general(query, cache[one, 0], flat, preferred_element_type=jnp.float32)
        place = lax.broadcasted_iota(jnp.int32, (many, span), 1)
        old = jnp.where(place < live, old * factor, -1e30)
        new = lax.dot_general(query, key, flat, preferred_element_type=jnp.float32)
        later = lax.broadcasted_iota(jnp.int32, (many, steps), 1)
        step = lax.broadcasted_iota(jnp.int32, (many, steps), 0) % steps
        new = jnp.where(later <= step, new * factor, -1e30)
        peak = jnp.maximum(
            jnp.max(old, axis=-1, keepdims=True), jnp.max(new, axis=-1, keepdims=True)
        )
        old = jnp.exp(old - peak)
        new = jnp.exp(new - peak)
        total = jnp.sum(old, axis=-1, keepdims=True) + jnp.sum(new, axis=-1, keepdims=True)
        old = (old / total).astype(jnp.bfloat16)
        new = (new / total).astype(jnp.bfloat16)
        result = jnp.dot(old, cache[one, 1], preferred_element_type=jnp.float32)
        result = result + jnp.dot(new, value, preferred_element_type=jnp.float32)
        mixed[pl.ds(request, many, stride=per_step)] = result

    @pl.when(at == pl.num_programs(0) - 1)
    def _():
        for head in range(heads):
            cols = slice(head * width, (head + 1) * width)
            out[:, cols] = mixed[head * rows : (head + 1) * rows].astype(jnp.bfloat16)


def attend_kernel(counts, sums, cache, after):
    requests, kinds, span, width = cache.shape
    rows = sums.shape[1]
    cols = sums.shape[2] - 2 * width
    heads = cols // width
    together = 4
    return pl.pallas_call(
        attend_body,
        out_shape=jax.ShapeDtypeStruct((rows, cols), jnp.bfloat16),
        grid=(requests // together,),
        in_specs=smem_space(1)
        + [
            pl.BlockSpec(sums.shape, lambda at: (0, 0, 0)),
            pl.BlockSpec((together, kinds, span, width), lambda at: (at, 0, 0, 0)),
        ]
        + any_space(len(after)),
        out_specs=pl.BlockSpec((rows, cols), lambda at: (0, 0)),
        scratch_shapes=[
            pltpu.VMEM((heads * rows, width), jnp.float32),
            pltpu.VMEM((rows, width), jnp.float32),
            pltpu.VMEM((rows, width), jnp.float32),
            pltpu.VMEM((heads * rows, width), jnp.float32),
        ],
        compiler_params=pltpu.CompilerParams(vmem_limit_bytes=VMEM_LIMIT),
        cost_estimate=moved_cost(16 << 20),
        name="attend_old_place",
    )(counts, sums, cache, *after)


def output_body(core, slabs, near, far, weight, *rest):
    out = rest[-1]
    reps, rows, half = near.shape
    count = 16
    steps = rows // count
    requests = reps * count
    owners = slabs[:, rows:, :requests].reshape(requests, requests).astype(jnp.float32)
    number = lax.broadcasted_iota(jnp.int32, (requests, requests), 1).astype(jnp.float32)
    shuffle = jnp.where(owners == number, 1.0, 0.0).astype(jnp.bfloat16)
    first = pl.multiple_of(core[0] * half, half)
    second = pl.multiple_of((1 - core[0]) * half, half)
    for step in range(steps):
        span = slice(step * count, (step + 1) * count)
        product = jnp.dot(
            near[:, span].reshape(requests, half),
            weight[pl.ds(first, half)],
            preferred_element_type=jnp.float32,
        )
        product = product + jnp.dot(
            far[:, span].reshape(requests, half),
            weight[pl.ds(second, half)],
            preferred_element_type=jnp.float32,
        )
        product = lax.dot_general(
            shuffle,
            product.astype(jnp.bfloat16),
            (((0,), (0,)), ((), ())),
            preferred_element_type=jnp.float32,
        )
        out[:, span] = product.astype(jnp.bfloat16).reshape(reps, count, -1)


def output_kernel(core, slabs, near, far, weight, after):
    reps, rows, _ = near.shape
    vmem = pl.BlockSpec(memory_space=pltpu.VMEM)
    return pl.pallas_call(
        output_body,
        out_shape=jax.ShapeDtypeStruct((reps, rows, weight.shape[1]), jnp.bfloat16),
        in_specs=smem_space(1) + [vmem] * 4 + any_space(len(after)),
        out_specs=vmem,
        compiler_params=pltpu.CompilerParams(vmem_limit_bytes=VMEM_LIMIT),
        cost_estimate=moved_cost(6 << 20),
        name="output_rows",
    )(core[None].astype(jnp.int32), slabs, near, far, weight, *after)


def per_device(
    new_tokens, norm_gain, w_query, w_keyval, w_output, kv_cache, block_counts, new_slot
):
    reps = lax.axis_size("rep")
    tps = lax.axis_size("tp")
    rep_index = lax.axis_index("rep")
    core = rep_index % 2
    chips = reps // 2
    same_core = [[2 * chip + one for chip in range(chips)] for one in range(2)]
    other_core = [(one, one ^ 1) for one in range(reps)]
    num_steps, num_rows, feat_width = new_tokens.shape
    row_total = num_steps * num_rows
    all_rows = reps * row_total
    depth = feat_width // reps
    head_cols = w_query.shape[1]
    pair_cols = w_keyval.shape[2]
    out_cols = w_output.shape[1]

    own_table = jnp.stack([new_slot, block_counts])
    other_table = lax.ppermute(own_table, "rep", other_core)
    lent = lax.ppermute(
        lax.dynamic_index_in_dim(kv_cache, 1 - core, 1, keepdims=False), "rep", other_core
    )

    column = lax.broadcasted_iota(jnp.int32, (num_rows, depth), 1)
    table = jnp.where(column < depth // 2, new_slot[:, None], block_counts[:, None])
    slabs = norm_kernel(
        new_tokens.reshape(row_total, feat_width), norm_gain[None], table.astype(jnp.bfloat16), reps
    )
    slabs = lax.all_to_all(slabs, "rep", split_axis=0, concat_axis=0, tiled=True)
    slot_table = slabs[:, row_total:, 0].astype(jnp.int32).reshape(-1)
    length_table = slabs[:, row_total:, depth // 2].astype(jnp.int32).reshape(-1)

    my_chip = rep_index // 2
    pair_table = jnp.where(
        core == 0,
        jnp.concatenate([own_table, other_table], axis=1),
        jnp.concatenate([other_table, own_table], axis=1),
    )
    chip_rows = 2 * num_rows
    pair_slots, pair_lengths = pair_table[0], pair_table[1]
    moves, spot, fits = first_leg(
        core, jnp.broadcast_to(my_chip, (chip_rows,)), pair_slots // chip_rows, pair_lengths
    )
    order = jnp.arange(chip_rows, dtype=jnp.int32)
    at_home = jnp.where(order // num_rows == core, 1, 2)
    pack_table = jnp.stack(
        [
            jnp.where(moves, at_home, 0),
            order % num_rows,
            spot,
            jnp.clip(fits, 0, pair_lengths),
        ]
    ).astype(jnp.int32)
    sent = pack_kernel(core, pack_table, kv_cache, lent, [])
    leg_one = [
        lax.ppermute(piece, "rep", line_pairs(reps, line, 0)) for line, piece in enumerate(sent)
    ]

    every = jnp.arange(reps * num_rows, dtype=jnp.int32)
    source, target = every // chip_rows, slot_table // chip_rows
    plans = []
    for one in range(2):
        moves_one, spot_one, fits_one = first_leg(one, source, target, length_table)
        moves_two, spot_two, fits_two = second_leg(one, source, target, length_table)
        done = jnp.clip(jnp.minimum(fits_one, fits_two), 0, length_table)
        missed = length_table - done
        late_place = places(source * chips + target, missed)
        plans.append((moves_one, spot_one, moves_two, spot_two, done, missed, late_place))
    most = jnp.maximum(*[jnp.max(jnp.where(plan[5] > 0, plan[6] + plan[5], 0)) for plan in plans])
    moves_one, spot_one, moves_two, spot_two, done, missed, late_place = [
        jnp.where(core == 0, one, other) for one, other in zip(*plans)
    ]
    between = jnp.where(core == 0, target // 2 * 2 + source % 2, source // 2 * 2 + target % 2)
    home = jnp.where(every // num_rows % 2 == core, 1, 2)
    from_home = every % num_rows
    passing = jnp.where(moves_two & (between == my_chip), 1, 0)
    wanted = jnp.arange(2 * chip_rows, dtype=jnp.int32)
    across_chip = my_chip // 2 * 2 + 1 - my_chip % 2
    passing_match = jnp.where(
        core == 0,
        (slot_table[None, :] == (across_chip * chip_rows + wanted)[:, None])
        & (wanted < chip_rows)[:, None],
        every[None, :] == (my_chip // 2 * 2 * chip_rows + wanted)[:, None],
    )
    passing_table = pick(
        passing_match,
        [
            passing * jnp.where(moves_one, 3, home),
            jnp.where(moves_one, spot_one, from_home),
            spot_two,
            done,
        ],
    )
    leg_two = [
        lax.ppermute(piece, "rep", line_pairs(reps, line, 1))
        for line, piece in enumerate(pack_kernel(core, passing_table, kv_cache, lent, leg_one))
    ]

    mine, theirs = project_kernel(
        core, slabs, w_query, w_keyval.reshape(depth, 2 * pair_cols), sent[0]
    )
    theirs = lax.ppermute(theirs, "rep", other_core)
    pair_sum = (mine.astype(jnp.float32) + theirs.astype(jnp.float32)).astype(jnp.bfloat16)
    pair_sum = lax.all_to_all(
        pair_sum, "rep", split_axis=0, concat_axis=0, tiled=True, axis_index_groups=same_core
    )

    attended = attend_kernel(block_counts, pair_sum, kv_cache, leg_one)

    halves = attended.reshape(row_total, 2, head_cols // 2)
    kept = lax.dynamic_index_in_dim(halves, core, 1, keepdims=False)
    given = lax.dynamic_index_in_dim(halves, 1 - core, 1, keepdims=False)
    given = lax.ppermute(given, "rep", other_core)
    kept = jnp.where(core == 0, jnp.stack([kept, given]), jnp.stack([given, kept]))
    near = lax.all_to_all(
        jnp.broadcast_to(kept[None], (chips,) + kept.shape),
        "rep",
        split_axis=0,
        concat_axis=0,
        tiled=True,
        axis_index_groups=same_core,
    ).reshape(reps, row_total, head_cols // 2)
    near, *_ = lax.optimization_barrier((near, *leg_two))
    far = lax.ppermute(near, "rep", other_core)

    partial_out = output_kernel(core, slabs, near, far, w_output, [])
    exchanged = lax.all_to_all(
        partial_out.reshape(tps, all_rows // tps, out_cols),
        "tp",
        split_axis=0,
        concat_axis=0,
        tiled=True,
    )
    first, exchanged = lax.optimization_barrier((jnp.int32(0), exchanged))
    summed = jnp.sum(exchanged.astype(jnp.float32), axis=0).astype(jnp.bfloat16)
    summed = summed.reshape(2, row_total, out_cols)
    straight = [
        (r * tps + t, (2 * t + r % 2) * tps + r // 2) for r in range(reps) for t in range(tps)
    ]
    crossed = [
        (r * tps + t, (2 * t + 1 - r % 2) * tps + r // 2) for r in range(reps) for t in range(tps)
    ]
    left = lax.ppermute(
        lax.dynamic_index_in_dim(summed, core, 0, keepdims=False), ("rep", "tp"), straight
    )
    right = lax.ppermute(
        lax.dynamic_index_in_dim(summed, 1 - core, 0, keepdims=False), ("rep", "tp"), crossed
    )
    layer_out = jnp.where(
        core == 0,
        jnp.concatenate([left, right], axis=1),
        jnp.concatenate([right, left], axis=1),
    ).reshape(num_steps, num_rows, 2 * out_cols)

    arrive_match = slot_table[None, :] == (my_chip * chip_rows + order)[:, None]
    unpack_table = pick(
        arrive_match,
        [
            jnp.where(moves_two, 4, jnp.where(moves_one, 3, home)),
            jnp.where(moves_two, spot_two, jnp.where(moves_one, spot_one, from_home)),
            done,
        ],
    )
    cache_moved, held = unpack_kernel(
        core, unpack_table, kv_cache, lent, leg_one, leg_two, partial_out
    )

    late_fields = [late_place, done, missed]
    late_pack = pick(
        every[None, :] == (my_chip * chip_rows + order)[:, None], [target] + late_fields
    )
    late_unpack = pick(arrive_match, [source] + late_fields)

    def more(state):
        start, moved, other = state
        pieces = lax.all_to_all(
            pack_more_kernel(core, start, late_pack, kv_cache, lent, chips),
            "rep",
            split_axis=0,
            concat_axis=0,
            tiled=True,
            axis_index_groups=same_core,
        )
        moved, other = unpack_more_kernel(core, start, late_unpack, pieces, moved, other)
        return start + LATER, moved, other

    _, cache_moved, held = lax.while_loop(
        lambda state: state[0] < most, more, (first, cache_moved, held)
    )
    returned = lax.ppermute(held, "rep", other_core)
    cache_moved = finish_kernel(core, returned, cache_moved)
    return (layer_out, cache_moved)


def solution(mesh):
    placed = (
        P(None, "rep", None),
        P(),
        P("rep", "tp"),
        P("rep", None, "tp"),
        P("tp", "rep"),
        P("rep", None, None, "tp"),
        P("rep"),
        P("rep"),
    )
    return jax.shard_map(
        per_device,
        mesh=mesh,
        in_specs=placed,
        out_specs=(P(None, "rep", "tp"), P("rep", None, None, "tp")),
        check_vma=False,
    )
```

```python
import functools

import jax
import jax.numpy as jnp
from jax import lax
from jax.experimental import pallas as pl
from jax.experimental.pallas import tpu as pltpu
from jax.sharding import PartitionSpec as P

HEADDIM = 128
BLOCK = 128
ROOM = 38
LATER = 4
VMEM_LIMIT = 56 << 20
VMEM_COMPUTE = 24 << 20


def line_pairs(reps, line, along_first):
    across, pairs = reps // 4, []
    for one in range(reps):
        x, y, core = one // 4, one // 2 % 2, one % 2
        if core == along_first:
            pairs.append((one, (x + (1, 3, 2)[line]) % across * 4 + y * 2 + core))
        elif line < 2:
            pairs.append((one, x * 4 + (1 - y) * 2 + core))
    return pairs


def places(key, lengths):
    order = jnp.arange(key.shape[0])
    before = (key[:, None] == key[None, :]) & (order[None, :] < order[:, None])
    return jnp.sum(jnp.where(before, lengths[None, :], 0), axis=-1)


def x_leg(source, target, key, lengths):
    along = (target // 2 - source // 2) % 4
    moves = along > 0
    place = places(key, jnp.where(moves, lengths, 0))
    line = jnp.where(along == 1, 0, jnp.where(along == 3, 1, 2))
    return moves, line * ROOM + place, jnp.where(moves, ROOM - place, lengths)


def y_leg(source, target, key, lengths):
    moves = target % 2 != source % 2
    place = places(key, jnp.where(moves, lengths, 0))
    return moves, place, jnp.where(moves, 2 * ROOM - place, lengths)


def first_leg(core, source, target, lengths):
    x = x_leg(source, target, source * 4 + target // 2, lengths)
    y = y_leg(source, target, source * 2 + target % 2, lengths)
    return [jnp.where(core == 0, one, other) for one, other in zip(x, y)]


def second_leg(core, source, target, lengths):
    x = x_leg(source, target, source // 2 * 8 + target, lengths)
    y = y_leg(source, target, source % 2 * 8 + target, lengths)
    return [jnp.where(core == 0, one, other) for one, other in zip(y, x)]


def pick(match, fields):
    return jnp.sum(jnp.where(match[None], jnp.stack(fields)[:, None, :], 0), axis=-1).astype(
        jnp.int32
    )


def blocks_of(cache, rows, block, core=None):
    span = pl.ds(pl.multiple_of(block * BLOCK, BLOCK), BLOCK)
    if core is None:
        return cache.at[rows, span]
    return cache.at[rows, core, span]


def fetch_blocks(entry, core, cache, lent, legs, put, sem):
    place, at, count = entry

    def fetch(condition, source):
        @pl.when(condition)
        def _():
            @pl.loop(0, count)
            def _(block):
                pltpu.make_async_copy(source(block), put(block), sem).start()

    fetch(place == 1, lambda block: blocks_of(cache, at, block, core))
    fetch(place == 2, lambda block: blocks_of(lent, at, block, core))
    for number, lines in enumerate(legs, 3):

        @pl.when(place == number)
        def _():
            @pl.loop(0, count)
            def _(block):
                spot = at + block
                for one, line in enumerate(lines):

                    @pl.when(spot // ROOM == one)
                    def _():
                        pltpu.make_async_copy(
                            line.at[spot - one * ROOM], put(block), sem
                        ).start()

    return jnp.where(place > 0, jnp.maximum(count, 0), 0)


def wait_blocks(total, example, sem):
    @pl.loop(0, total)
    def _(_):
        pltpu.make_async_copy(example, example, sem).wait()


def pack_body(legs, core, table, cache, lent, *rest):
    lines, (out, held, sem, out_sem) = rest[:legs], (rest[-6:-3],) + rest[-3:]

    def send(at, total):
        to = table[2, at]
        entry = (table[0, at], table[1, at], table[3, at])
        return total + fetch_blocks(
            entry, core[0], cache, lent, [lines], lambda block: held.at[to + block], sem
        )

    total = lax.fori_loop(0, table.shape[1], send, jnp.int32(0))
    wait_blocks(total, held.at[0], sem)
    copies = [
        pltpu.make_async_copy(held.at[pl.ds(line * ROOM, ROOM)], one, out_sem.at[line])
        for line, one in enumerate(out)
    ]
    for copy in copies:
        copy.start()
    for copy in copies:
        copy.wait()


def any_space(number):
    return [pl.BlockSpec(memory_space=pl.ANY)] * number


def smem_space(number):
    return [pl.BlockSpec(memory_space=pltpu.SMEM)] * number


def moved_cost(size):
    return pl.CostEstimate(flops=0, bytes_accessed=size, transcendentals=0)


def pack_kernel(core, table, cache, lent, lines, cost):
    line = jax.ShapeDtypeStruct((ROOM, BLOCK, HEADDIM), jnp.bfloat16)
    return pl.pallas_call(
        functools.partial(pack_body, len(lines)),
        out_shape=[line] * 3,
        in_specs=smem_space(2) + any_space(2 + len(lines)),
        out_specs=any_space(3),
        scratch_shapes=[
            pltpu.VMEM((3 * ROOM, BLOCK, HEADDIM), jnp.bfloat16),
            pltpu.SemaphoreType.DMA,
            pltpu.SemaphoreType.DMA((3,)),
        ],
        compiler_params=pltpu.CompilerParams(vmem_limit_bytes=VMEM_LIMIT),
        cost_estimate=moved_cost(cost),
        name="pack_blocks",
    )(core[None].astype(jnp.int32), table, cache, lent, *lines)


def unpack_body(scalars, table, cache, lent, *rest):
    first, second, rest = rest[:3], rest[3:6], rest[6:]
    _, moved, theirs, held, sem, out_sem = rest
    core = scalars[0]
    half = theirs.shape[0]
    most = cache.shape[2] // BLOCK

    def receive(at, total):
        count = table[2, at]
        entry = (table[0, at], table[1, at], count)

        @pl.loop(count, most)
        def _(block):
            span = pl.ds(pl.multiple_of(block * BLOCK, BLOCK), BLOCK)
            held[at, span] = jnp.zeros((BLOCK, HEADDIM), held.dtype)

        return total + fetch_blocks(
            entry, core, cache, lent, [first, second], lambda block: blocks_of(held, at, block), sem
        )

    total = lax.fori_loop(0, 2 * half, receive, jnp.int32(0))
    wait_blocks(total, first[0].at[0], sem)
    copies = [
        pltpu.make_async_copy(held.at[pl.ds((1 - core) * half, half)], theirs, out_sem.at[0]),
        pltpu.make_async_copy(held.at[pl.ds(core * half, half)], moved.at[:, core], out_sem.at[1]),
    ]
    for copy in copies:
        copy.start()
    for copy in copies:
        copy.wait()


def unpack_kernel(core, table, cache, lent, first, second, after):
    rows, _, span, width = cache.shape
    return pl.pallas_call(
        unpack_body,
        out_shape=[
            jax.ShapeDtypeStruct(cache.shape, jnp.bfloat16),
            jax.ShapeDtypeStruct((rows, span, width), jnp.bfloat16),
        ],
        in_specs=smem_space(2) + any_space(9),
        out_specs=any_space(2),
        scratch_shapes=[
            pltpu.VMEM((2 * rows, span, width), jnp.bfloat16),
            pltpu.SemaphoreType.DMA,
            pltpu.SemaphoreType.DMA((2,)),
        ],
        compiler_params=pltpu.CompilerParams(vmem_limit_bytes=VMEM_LIMIT),
        cost_estimate=moved_cost(10 << 20),
        name="unpack_blocks",
    )(core[None].astype(jnp.int32), table, cache, lent, *first, *second, after)


def pack_more_body(scalars, table, cache, lent, out, held, sem):
    core, start = scalars[0], scalars[1]
    room = out.shape[1]
    requests = table.shape[1]
    half = requests // 2

    def send(at, total):
        line, place, skip, left = (table[field, at] for field in range(4))
        low = jnp.maximum(start - place, 0)
        count = jnp.maximum(jnp.minimum(left, start + room - place) - low, 0)

        def fetch(condition, source):
            @pl.when(condition)
            def _():
                @pl.loop(0, count)
                def _(block):
                    pltpu.make_async_copy(
                        source(skip + low + block), held.at[line, place + low + block - start], sem
                    ).start()

        row = at % half
        fetch(at // half == core, lambda block: blocks_of(cache, row, block, core))
        fetch(at // half != core, lambda block: blocks_of(lent, row, block, core))
        return total + count

    total = lax.fori_loop(0, requests, send, jnp.int32(0))
    wait_blocks(total, held.at[0, 0], sem)
    copy = pltpu.make_async_copy(held, out, sem)
    copy.start()
    copy.wait()


def pack_more_kernel(core, start, table, cache, lent, chips):
    lines = jax.ShapeDtypeStruct((chips, LATER, BLOCK, HEADDIM), jnp.bfloat16)
    return pl.pallas_call(
        pack_more_body,
        out_shape=lines,
        in_specs=smem_space(2) + any_space(2),
        out_specs=any_space(1)[0],
        scratch_shapes=[pltpu.VMEM(lines.shape, lines.dtype), pltpu.SemaphoreType.DMA],
        compiler_params=pltpu.CompilerParams(vmem_limit_bytes=VMEM_LIMIT),
        name="pack_later_blocks",
    )(jnp.stack([core, start]).astype(jnp.int32), table, cache, lent)


def unpack_more_body(scalars, table, pieces, _moved, _theirs, moved, theirs, held, sem):
    core, start = scalars[0], scalars[1]
    room = pieces.shape[1]
    half = theirs.shape[0]
    copy = pltpu.make_async_copy(pieces, held, sem)
    copy.start()
    copy.wait()

    def receive(at, total):
        line, place, skip, left = (table[field, at] for field in range(4))
        slot = at % half
        low = jnp.maximum(start - place, 0)
        count = jnp.maximum(jnp.minimum(left, start + room - place) - low, 0)

        def put(condition, target):
            @pl.when(condition)
            def _():
                @pl.loop(0, count)
                def _(block):
                    pltpu.make_async_copy(
                        held.at[line, place + low + block - start], target(skip + low + block), sem
                    ).start()

        put(at // half == core, lambda block: blocks_of(moved, slot, block, core))
        put(at // half != core, lambda block: blocks_of(theirs, slot, block))
        return total + count

    total = lax.fori_loop(0, 2 * half, receive, jnp.int32(0))
    wait_blocks(total, held.at[0, 0], sem)


def unpack_more_kernel(core, start, table, pieces, moved, theirs):
    return pl.pallas_call(
        unpack_more_body,
        out_shape=[
            jax.ShapeDtypeStruct(moved.shape, moved.dtype),
            jax.ShapeDtypeStruct(theirs.shape, theirs.dtype),
        ],
        in_specs=smem_space(2) + any_space(3),
        out_specs=any_space(2),
        scratch_shapes=[pltpu.VMEM(pieces.shape, pieces.dtype), pltpu.SemaphoreType.DMA],
        input_output_aliases={3: 0, 4: 1},
        compiler_params=pltpu.CompilerParams(vmem_limit_bytes=VMEM_LIMIT),
        name="unpack_later_blocks",
    )(jnp.stack([core, start]).astype(jnp.int32), table, pieces, moved, theirs)


def finish_body(scalars, returned, _, moved, held, in_sem, out_sem):
    parts = in_sem.shape[0]
    rows = returned.shape[0] // parts
    spans = [pl.ds(part * rows, rows) for part in range(parts)]
    fetches = [
        pltpu.make_async_copy(returned.at[span], held.at[span], in_sem.at[part])
        for part, span in enumerate(spans)
    ]
    stores = [
        pltpu.make_async_copy(held.at[span], moved.at[span, 1 - scalars[0]], out_sem.at[part])
        for part, span in enumerate(spans)
    ]
    for fetch in fetches:
        fetch.start()
    for fetch, store in zip(fetches, stores):
        fetch.wait()
        store.start()
    for store in stores:
        store.wait()


def finish_kernel(core, returned, moved):
    return pl.pallas_call(
        finish_body,
        out_shape=jax.ShapeDtypeStruct(moved.shape, moved.dtype),
        in_specs=smem_space(1) + any_space(2),
        out_specs=any_space(1)[0],
        scratch_shapes=[
            pltpu.VMEM(returned.shape, returned.dtype),
            pltpu.SemaphoreType.DMA((4,)),
            pltpu.SemaphoreType.DMA((4,)),
        ],
        compiler_params=pltpu.CompilerParams(vmem_limit_bytes=VMEM_LIMIT),
        input_output_aliases={2: 0},
        cost_estimate=moved_cost(6 << 20),
        name="put_other_kind",
    )(core[None].astype(jnp.int32), returned, moved)


def norm_body(slots, counts, tokens, gain, out):
    rows, width = tokens.shape
    reps, _, depth = out.shape
    chunk = 1024
    total = jnp.zeros((rows, 1), jnp.float32)
    for at in range(0, width, chunk):
        part = tokens[:, at : at + chunk].astype(jnp.float32)
        total = total + jnp.sum(part * part, axis=-1, keepdims=True)
    inverse = lax.rsqrt(total * (1.0 / width) + 1e-05)
    shape = (slots.shape[0], depth)
    row = lax.broadcasted_iota(jnp.int32, shape, 0)
    left = lax.broadcasted_iota(jnp.int32, shape, 1) < depth // 2
    table = jnp.zeros(shape, jnp.int32)
    for one in range(slots.shape[0]):
        table = jnp.where(row == one, jnp.where(left, slots[one], counts[one]), table)
    table = table.astype(jnp.float32).astype(jnp.bfloat16)
    for rep in range(reps):
        span = slice(rep * depth, (rep + 1) * depth)
        scale = gain[span].astype(jnp.float32).reshape(1, depth)
        part = tokens[:, span].astype(jnp.float32) * inverse * scale
        out[rep, :rows] = part.astype(jnp.bfloat16)
        out[rep, rows:] = table


def norm_kernel(slots, counts, tokens, gain, reps):
    rows, width = tokens.shape
    vmem = pl.BlockSpec(memory_space=pltpu.VMEM)
    return pl.pallas_call(
        norm_body,
        out_shape=jax.ShapeDtypeStruct((reps, rows + 16, width // reps), jnp.bfloat16),
        in_specs=smem_space(2) + [vmem] * 2,
        out_specs=vmem,
        compiler_params=pltpu.CompilerParams(vmem_limit_bytes=VMEM_COMPUTE),
        cost_estimate=moved_cost(4 << 20),
        name="norm_rows",
    )(slots, counts, tokens, gain)


def project_body(pick, core, slabs, w_query, w_keyval, *rest):
    out = rest[-1]
    reps, rows, depth = slabs.shape
    chips = reps // 2
    count = 16
    steps = (rows - count) // count
    requests = reps * count
    core = core[0] if pick == 0 else 1 - core[0]
    owners = slabs[:, rows - count :, :requests].reshape(chips, 2, count, requests)
    owners = jnp.where(core == 0, owners[:, 0], owners[:, 1])
    owners = owners.reshape(requests // 2, requests).astype(jnp.float32)
    number = lax.broadcasted_iota(jnp.int32, owners.shape, 1).astype(jnp.float32)
    shuffle = jnp.where(owners == number, 1.0, 0.0).astype(jnp.bfloat16)
    query_cols = w_query.shape[1]
    for step in range(steps):
        span = slice(step * count, (step + 1) * count)
        features = slabs[:, span].reshape(requests, depth)
        features = jnp.dot(shuffle, features, preferred_element_type=jnp.float32)
        features = features.astype(jnp.bfloat16)
        for weight, at in ((w_query, 0), (w_keyval, query_cols)):
            product = jnp.dot(features, weight[...], preferred_element_type=jnp.float32)
            width = product.shape[1]
            product = product.reshape(chips, count, width)
            if pick == 0:
                product = product + rest[0][:, span, at : at + width].astype(jnp.float32)
            out[:, span, at : at + width] = product.astype(jnp.bfloat16)


def project_kernel(pick, core, slabs, w_query, w_keyval, operands):
    reps, rows, _ = slabs.shape
    width = w_query.shape[1] + w_keyval.shape[1]
    vmem = pl.BlockSpec(memory_space=pltpu.VMEM)
    return pl.pallas_call(
        functools.partial(project_body, pick),
        out_shape=jax.ShapeDtypeStruct((reps // 2, rows - 16, width), jnp.bfloat16),
        in_specs=smem_space(1)
        + [vmem] * 3
        + ([vmem] if pick == 0 else any_space(len(operands))),
        out_specs=vmem,
        compiler_params=pltpu.CompilerParams(vmem_limit_bytes=VMEM_COMPUTE),
        cost_estimate=moved_cost(4 << 20),
        name="project_rows",
    )(core[None].astype(jnp.int32), slabs, w_query, w_keyval, *operands)


def attend_body(core, counts, sums, cache, *rest):
    kept, given, queries, keys, values, mixed = rest[-6:]
    at = pl.program_id(0)
    together, _, span, width = cache.shape
    rows = sums.shape[1]
    per_step = 16
    steps = rows // per_step
    heads = (sums.shape[2] - 2 * width) // width

    @pl.when(at == 0)
    def _():
        for head in range(heads + 2):
            cols = slice(head * width, (head + 1) * width)
            total = jnp.sum(sums[:, :, cols].astype(jnp.float32), axis=0)
            total = total.astype(jnp.bfloat16).astype(jnp.float32)
            if head < heads:
                queries[head * rows : (head + 1) * rows] = total
            elif head == heads:
                keys[...] = total
            else:
                values[...] = total

    many = heads * steps
    flat = (((1,), (1,)), ((), ()))
    factor = 1.0 / width**0.5
    longest = counts[at * together]
    for one in range(1, together):
        longest = jnp.maximum(longest, counts[at * together + one])

    def attend(reach):
        for one in range(together):
            request = at * together + one
            live = counts[request] * BLOCK
            query = queries[pl.ds(request, many, stride=per_step)].astype(jnp.bfloat16)
            key = keys[pl.ds(request, steps, stride=per_step)].astype(jnp.bfloat16)
            value = values[pl.ds(request, steps, stride=per_step)].astype(jnp.bfloat16)
            old = lax.dot_general(
                query, cache[one, 0, :reach], flat, preferred_element_type=jnp.float32
            )
            place = lax.broadcasted_iota(jnp.int32, (many, reach), 1)
            old = jnp.where(place < live, old * factor, -1e30)
            new = lax.dot_general(query, key, flat, preferred_element_type=jnp.float32)
            later = lax.broadcasted_iota(jnp.int32, (many, steps), 1)
            step = lax.broadcasted_iota(jnp.int32, (many, steps), 0) % steps
            new = jnp.where(later <= step, new * factor, -1e30)
            peak = jnp.maximum(
                jnp.max(old, axis=-1, keepdims=True), jnp.max(new, axis=-1, keepdims=True)
            )
            old = jnp.exp(old - peak)
            new = jnp.exp(new - peak)
            total = jnp.sum(old, axis=-1, keepdims=True) + jnp.sum(new, axis=-1, keepdims=True)
            share = 1.0 / total
            old = (old * share).astype(jnp.bfloat16)
            new = (new * share).astype(jnp.bfloat16)
            result = jnp.dot(old, cache[one, 1, :reach], preferred_element_type=jnp.float32)
            result = result + jnp.dot(new, value, preferred_element_type=jnp.float32)
            mixed[pl.ds(request, many, stride=per_step)] = result

    short = span // 2

    @pl.when(longest * BLOCK <= short)
    def _():
        attend(short)

    @pl.when(longest * BLOCK > short)
    def _():
        attend(span)

    @pl.when(at == pl.num_programs(0) - 1)
    def _():
        for one in range(2):

            @pl.when(core[0] == one)
            def _():
                for head in range(heads):
                    out = kept if head // (heads // 2) == one else given
                    at = head % (heads // 2) * width
                    out[:, at : at + width] = mixed[head * rows : (head + 1) * rows].astype(
                        jnp.bfloat16
                    )


def attend_kernel(core, counts, sums, cache, after):
    requests, kinds, span, width = cache.shape
    rows = sums.shape[1]
    cols = sums.shape[2] - 2 * width
    heads = cols // width
    together = 4
    return pl.pallas_call(
        attend_body,
        out_shape=[jax.ShapeDtypeStruct((rows, cols // 2), jnp.bfloat16)] * 2,
        grid=(requests // together,),
        in_specs=smem_space(2)
        + [
            pl.BlockSpec(sums.shape, lambda at: (0, 0, 0)),
            pl.BlockSpec((together, kinds, span, width), lambda at: (at, 0, 0, 0)),
        ]
        + any_space(len(after)),
        out_specs=[pl.BlockSpec((rows, cols // 2), lambda at: (0, 0))] * 2,
        scratch_shapes=[
            pltpu.VMEM((heads * rows, width), jnp.float32),
            pltpu.VMEM((rows, width), jnp.float32),
            pltpu.VMEM((rows, width), jnp.float32),
            pltpu.VMEM((heads * rows, width), jnp.float32),
        ],
        compiler_params=pltpu.CompilerParams(vmem_limit_bytes=VMEM_COMPUTE),
        cost_estimate=moved_cost(16 << 20),
        name="attend_old_place",
    )(core[None].astype(jnp.int32), counts, sums, cache, *after)


def output_body(core, slabs, near, far, weight, *rest):
    out = rest[-1]
    reps, rows, half = near.shape
    count = 16
    steps = rows // count
    requests = reps * count
    owners = slabs[:, rows:, :requests].reshape(requests, requests).astype(jnp.float32)
    number = lax.broadcasted_iota(jnp.int32, (requests, requests), 1).astype(jnp.float32)
    shuffle = jnp.where(owners == number, 1.0, 0.0).astype(jnp.bfloat16)
    first = pl.multiple_of(core[0] * half, half)
    second = pl.multiple_of((1 - core[0]) * half, half)
    for step in range(steps):
        span = slice(step * count, (step + 1) * count)
        product = jnp.dot(
            near[:, span].reshape(requests, half),
            weight[pl.ds(first, half)],
            preferred_element_type=jnp.float32,
        )
        product = product + jnp.dot(
            far[:, span].reshape(requests, half),
            weight[pl.ds(second, half)],
            preferred_element_type=jnp.float32,
        )
        product = lax.dot_general(
            shuffle,
            product.astype(jnp.bfloat16),
            (((0,), (0,)), ((), ())),
            preferred_element_type=jnp.float32,
        )
        out[:, span] = product.astype(jnp.bfloat16).reshape(reps, count, -1)


def output_kernel(core, slabs, near, far, weight, after):
    reps, rows, _ = near.shape
    vmem = pl.BlockSpec(memory_space=pltpu.VMEM)
    return pl.pallas_call(
        output_body,
        out_shape=jax.ShapeDtypeStruct((reps, rows, weight.shape[1]), jnp.bfloat16),
        in_specs=smem_space(1) + [vmem] * 4 + any_space(len(after)),
        out_specs=vmem,
        compiler_params=pltpu.CompilerParams(vmem_limit_bytes=VMEM_COMPUTE),
        cost_estimate=moved_cost(6 << 20),
        name="output_rows",
    )(core[None].astype(jnp.int32), slabs, near, far, weight, *after)


def per_device(
    new_tokens, norm_gain, w_query, w_keyval, w_output, kv_cache, block_counts, new_slot
):
    reps = lax.axis_size("rep")
    tps = lax.axis_size("tp")
    rep_index = lax.axis_index("rep")
    core = rep_index % 2
    chips = reps // 2
    same_core = [[2 * chip + one for chip in range(chips)] for one in range(2)]
    other_core = [(one, one ^ 1) for one in range(reps)]
    num_steps, num_rows, feat_width = new_tokens.shape
    row_total = num_steps * num_rows
    all_rows = reps * row_total
    depth = feat_width // reps
    head_cols = w_query.shape[1]
    pair_cols = w_keyval.shape[2]
    out_cols = w_output.shape[1]

    own_table = jnp.stack([new_slot, block_counts])
    other_table = lax.ppermute(own_table, "rep", other_core)
    slabs = norm_kernel(
        new_slot, block_counts, new_tokens.reshape(row_total, feat_width), norm_gain, reps
    )
    lent = lax.ppermute(kv_cache, "rep", other_core)
    slabs = lax.all_to_all(slabs, "rep", split_axis=0, concat_axis=0, tiled=True)
    my_chip = rep_index // 2
    pair_table = jnp.where(
        core == 0,
        jnp.concatenate([own_table, other_table], axis=1),
        jnp.concatenate([other_table, own_table], axis=1),
    )
    chip_rows = 2 * num_rows
    pair_slots, pair_lengths = pair_table[0], pair_table[1]
    moves, spot, fits = first_leg(
        core, jnp.broadcast_to(my_chip, (chip_rows,)), pair_slots // chip_rows, pair_lengths
    )
    order = jnp.arange(chip_rows, dtype=jnp.int32)
    at_home = jnp.where(order // num_rows == core, 1, 2)
    pack_table = jnp.stack(
        [
            jnp.where(moves, at_home, 0),
            order % num_rows,
            spot,
            jnp.clip(fits, 0, pair_lengths),
        ]
    ).astype(jnp.int32)
    sent = pack_kernel(core, pack_table, kv_cache, lent, [], 1 << 10)
    leg_one = [
        lax.ppermute(piece, "rep", line_pairs(reps, line, 0)) for line, piece in enumerate(sent)
    ]

    w_pair, *_ = lax.optimization_barrier((w_keyval, *sent))
    w_pair = w_pair.reshape(depth, 2 * pair_cols)
    theirs = project_kernel(1, core, slabs, w_query, w_pair, [sent[0]])
    late_slabs, theirs = lax.optimization_barrier((slabs, theirs))
    theirs = lax.ppermute(theirs, "rep", other_core)
    pair_sum = project_kernel(0, core, slabs, w_query, w_pair, [theirs])
    pair_sum = lax.all_to_all(
        pair_sum, "rep", split_axis=0, concat_axis=0, tiled=True, axis_index_groups=same_core
    )

    slot_table = late_slabs[:, row_total:, 0].astype(jnp.int32).reshape(-1)
    length_table = late_slabs[:, row_total:, depth // 2].astype(jnp.int32).reshape(-1)

    every = jnp.arange(reps * num_rows, dtype=jnp.int32)
    source, target = every // chip_rows, slot_table // chip_rows
    plans = []
    for one in range(2):
        moves_one, spot_one, fits_one = first_leg(one, source, target, length_table)
        moves_two, spot_two, fits_two = second_leg(one, source, target, length_table)
        done = jnp.clip(jnp.minimum(fits_one, fits_two), 0, length_table)
        missed = length_table - done
        late_place = places(source * chips + target, missed)
        plans.append((moves_one, spot_one, moves_two, spot_two, done, missed, late_place))
    most = jnp.maximum(*[jnp.max(jnp.where(plan[5] > 0, plan[6] + plan[5], 0)) for plan in plans])
    moves_one, spot_one, moves_two, spot_two, done, missed, late_place = [
        jnp.where(core == 0, one, other) for one, other in zip(*plans)
    ]
    between = jnp.where(core == 0, target // 2 * 2 + source % 2, source // 2 * 2 + target % 2)
    home = jnp.where(every // num_rows % 2 == core, 1, 2)
    from_home = every % num_rows
    passing = jnp.where(moves_two & (between == my_chip), 1, 0)
    wanted = jnp.arange(2 * chip_rows, dtype=jnp.int32)
    across_chip = my_chip // 2 * 2 + 1 - my_chip % 2
    passing_match = jnp.where(
        core == 0,
        (slot_table[None, :] == (across_chip * chip_rows + wanted)[:, None])
        & (wanted < chip_rows)[:, None],
        every[None, :] == (my_chip // 2 * 2 * chip_rows + wanted)[:, None],
    )
    passing_table = pick(
        passing_match,
        [
            passing * jnp.where(moves_one, 3, home),
            jnp.where(moves_one, spot_one, from_home),
            spot_two,
            done,
        ],
    )
    arrive_match = slot_table[None, :] == (my_chip * chip_rows + order)[:, None]
    unpack_table = pick(
        arrive_match,
        [
            jnp.where(moves_two, 4, jnp.where(moves_one, 3, home)),
            jnp.where(moves_two, spot_two, jnp.where(moves_one, spot_one, from_home)),
            done,
        ],
    )
    late_fields = [late_place, done, missed]
    late_pack = pick(
        every[None, :] == (my_chip * chip_rows + order)[:, None], [target] + late_fields
    )
    late_unpack = pick(arrive_match, [source] + late_fields)

    passed = pack_kernel(core, passing_table, kv_cache, lent, leg_one, 8 << 20)
    leg_two = [
        lax.ppermute(piece, "rep", line_pairs(reps, line, 1)) for line, piece in enumerate(passed)
    ]


    kept, given = attend_kernel(
        core,
        block_counts,
        pair_sum,
        kv_cache,
        [passed[0], unpack_table, late_pack, late_unpack],
    )

    given = lax.ppermute(given, "rep", other_core)
    kept = jnp.where(core == 0, jnp.stack([kept, given]), jnp.stack([given, kept]))
    near = lax.all_to_all(
        jnp.broadcast_to(kept[None], (chips,) + kept.shape),
        "rep",
        split_axis=0,
        concat_axis=0,
        tiled=True,
        axis_index_groups=same_core,
    ).reshape(reps, row_total, head_cols // 2)
    near, *_ = lax.optimization_barrier((near, *leg_two))
    far = lax.ppermute(near, "rep", other_core)

    partial_out = output_kernel(core, slabs, near, far, w_output, [])
    exchanged = lax.all_to_all(
        partial_out.reshape(tps, all_rows // tps, out_cols),
        "tp",
        split_axis=0,
        concat_axis=0,
        tiled=True,
    )
    first, exchanged = lax.optimization_barrier((jnp.int32(0), exchanged))
    summed = jnp.sum(exchanged.astype(jnp.float32), axis=0).astype(jnp.bfloat16)
    summed = summed.reshape(2, row_total, out_cols)
    straight = [
        (r * tps + t, (2 * t + r % 2) * tps + r // 2) for r in range(reps) for t in range(tps)
    ]
    crossed = [
        (r * tps + t, (2 * t + 1 - r % 2) * tps + r // 2) for r in range(reps) for t in range(tps)
    ]
    left = lax.ppermute(
        lax.dynamic_index_in_dim(summed, core, 0, keepdims=False), ("rep", "tp"), straight
    )
    right = lax.ppermute(
        lax.dynamic_index_in_dim(summed, 1 - core, 0, keepdims=False), ("rep", "tp"), crossed
    )
    layer_out = jnp.where(
        core == 0,
        jnp.concatenate([left, right], axis=1),
        jnp.concatenate([right, left], axis=1),
    ).reshape(num_steps, num_rows, 2 * out_cols)

    cache_moved, held = unpack_kernel(
        core, unpack_table, kv_cache, lent, leg_one, leg_two, partial_out
    )


    def more(state):
        start, moved, other = state
        pieces = lax.all_to_all(
            pack_more_kernel(core, start, late_pack, kv_cache, lent, chips),
            "rep",
            split_axis=0,
            concat_axis=0,
            tiled=True,
            axis_index_groups=same_core,
        )
        moved, other = unpack_more_kernel(core, start, late_unpack, pieces, moved, other)
        return start + LATER, moved, other

    _, cache_moved, held = lax.while_loop(
        lambda state: state[0] < most, more, (first, cache_moved, held)
    )
    returned = lax.ppermute(held, "rep", other_core)
    cache_moved = finish_kernel(core, returned, cache_moved)
    return (layer_out, cache_moved)


def solution(mesh):
    placed = (
        P(None, "rep", None),
        P(),
        P("rep", "tp"),
        P("rep", None, "tp"),
        P("tp", "rep"),
        P("rep", None, None, "tp"),
        P("rep"),
        P("rep"),
    )
    return jax.shard_map(
        per_device,
        mesh=mesh,
        in_specs=placed,
        out_specs=(P(None, "rep", "tp"), P("rep", None, None, "tp")),
        check_vma=False,
    )
```

```python
import functools

import jax
import jax.numpy as jnp
from jax import lax
from jax.experimental import pallas as pl
from jax.experimental.pallas import tpu as pltpu
from jax.sharding import PartitionSpec as P

HEADDIM = 128
BLOCK = 128
ROOM = 38
LATER = 4
VMEM_LIMIT = 56 << 20
VMEM_COMPUTE = 24 << 20


def line_pairs(reps, line, along_first):
    across, pairs = reps // 4, []
    for one in range(reps):
        x, y, core = one // 4, one // 2 % 2, one % 2
        if core == along_first:
            pairs.append((one, (x + (1, 3, 2)[line]) % across * 4 + y * 2 + core))
        elif line < 2:
            pairs.append((one, x * 4 + (1 - y) * 2 + core))
    return pairs


def places(key, lengths):
    order = jnp.arange(key.shape[0])
    before = (key[:, None] == key[None, :]) & (order[None, :] < order[:, None])
    return jnp.sum(jnp.where(before, lengths[None, :], 0), axis=-1)


def x_leg(source, target, key, lengths):
    along = (target // 2 - source // 2) % 4
    moves = along > 0
    place = places(key, jnp.where(moves, lengths, 0))
    line = jnp.where(along == 1, 0, jnp.where(along == 3, 1, 2))
    return moves, line * ROOM + place, jnp.where(moves, ROOM - place, lengths)


def y_leg(source, target, key, lengths):
    moves = target % 2 != source % 2
    place = places(key, jnp.where(moves, lengths, 0))
    return moves, place, jnp.where(moves, 2 * ROOM - place, lengths)


def first_leg(core, source, target, lengths):
    x = x_leg(source, target, source * 4 + target // 2, lengths)
    y = y_leg(source, target, source * 2 + target % 2, lengths)
    return [jnp.where(core == 0, one, other) for one, other in zip(x, y)]


def second_leg(core, source, target, lengths):
    x = x_leg(source, target, source // 2 * 8 + target, lengths)
    y = y_leg(source, target, source % 2 * 8 + target, lengths)
    return [jnp.where(core == 0, one, other) for one, other in zip(y, x)]


def pick(match, fields):
    return jnp.sum(jnp.where(match[None], jnp.stack(fields)[:, None, :], 0), axis=-1).astype(
        jnp.int32
    )


def blocks_of(cache, rows, block, core=None):
    span = pl.ds(pl.multiple_of(block * BLOCK, BLOCK), BLOCK)
    if core is None:
        return cache.at[rows, span]
    return cache.at[rows, core, span]


def fetch_blocks(entry, core, cache, lent, legs, put, sem):
    place, at, count = entry

    def fetch(condition, source):
        @pl.when(condition)
        def _():
            @pl.loop(0, count)
            def _(block):
                pltpu.make_async_copy(source(block), put(block), sem).start()

    fetch(place == 1, lambda block: blocks_of(cache, at, block, core))
    fetch(place == 2, lambda block: blocks_of(lent, at, block, core))
    for number, lines in enumerate(legs, 3):

        @pl.when(place == number)
        def _():
            @pl.loop(0, count)
            def _(block):
                spot = at + block
                for one, line in enumerate(lines):

                    @pl.when(spot // ROOM == one)
                    def _():
                        pltpu.make_async_copy(
                            line.at[spot - one * ROOM], put(block), sem
                        ).start()

    return jnp.where(place > 0, jnp.maximum(count, 0), 0)


def wait_blocks(total, example, sem):
    @pl.loop(0, total)
    def _(_):
        pltpu.make_async_copy(example, example, sem).wait()


def pack_body(legs, core, table, cache, lent, *rest):
    lines, (out, held, sem, out_sem) = rest[:legs], (rest[-6:-3],) + rest[-3:]

    def send(at, total):
        to = table[2, at]
        entry = (table[0, at], table[1, at], table[3, at])
        return total + fetch_blocks(
            entry, core[0], cache, lent, [lines], lambda block: held.at[to + block], sem
        )

    total = lax.fori_loop(0, table.shape[1], send, jnp.int32(0))
    wait_blocks(total, held.at[0], sem)
    copies = [
        pltpu.make_async_copy(held.at[pl.ds(line * ROOM, ROOM)], one, out_sem.at[line])
        for line, one in enumerate(out)
    ]
    for copy in copies:
        copy.start()
    for copy in copies:
        copy.wait()


def any_space(number):
    return [pl.BlockSpec(memory_space=pl.ANY)] * number


def smem_space(number):
    return [pl.BlockSpec(memory_space=pltpu.SMEM)] * number


def moved_cost(size):
    return pl.CostEstimate(flops=0, bytes_accessed=size, transcendentals=0)


def pack_kernel(core, table, cache, lent, lines, cost):
    line = jax.ShapeDtypeStruct((ROOM, BLOCK, HEADDIM), jnp.bfloat16)
    return pl.pallas_call(
        functools.partial(pack_body, len(lines)),
        out_shape=[line] * 3,
        in_specs=smem_space(2) + any_space(2 + len(lines)),
        out_specs=any_space(3),
        scratch_shapes=[
            pltpu.VMEM((3 * ROOM, BLOCK, HEADDIM), jnp.bfloat16),
            pltpu.SemaphoreType.DMA,
            pltpu.SemaphoreType.DMA((3,)),
        ],
        compiler_params=pltpu.CompilerParams(vmem_limit_bytes=VMEM_LIMIT),
        cost_estimate=moved_cost(cost),
        name="pack_blocks",
    )(core[None].astype(jnp.int32), table, cache, lent, *lines)


def unpack_body(scalars, table, cache, lent, *rest):
    first, second, rest = rest[:3], rest[3:6], rest[6:]
    _, moved, theirs, held, sem, out_sem = rest
    core = scalars[0]
    half = theirs.shape[0]
    most = cache.shape[2] // BLOCK

    def receive(at, total):
        count = table[2, at]
        entry = (table[0, at], table[1, at], count)

        @pl.loop(count, most)
        def _(block):
            span = pl.ds(pl.multiple_of(block * BLOCK, BLOCK), BLOCK)
            held[at, span] = jnp.zeros((BLOCK, HEADDIM), held.dtype)

        return total + fetch_blocks(
            entry, core, cache, lent, [first, second], lambda block: blocks_of(held, at, block), sem
        )

    total = lax.fori_loop(0, 2 * half, receive, jnp.int32(0))
    wait_blocks(total, first[0].at[0], sem)
    copies = [
        pltpu.make_async_copy(held.at[pl.ds((1 - core) * half, half)], theirs, out_sem.at[0]),
        pltpu.make_async_copy(held.at[pl.ds(core * half, half)], moved.at[:, core], out_sem.at[1]),
    ]
    for copy in copies:
        copy.start()
    for copy in copies:
        copy.wait()


def unpack_kernel(core, table, cache, lent, first, second, after):
    rows, _, span, width = cache.shape
    return pl.pallas_call(
        unpack_body,
        out_shape=[
            jax.ShapeDtypeStruct(cache.shape, jnp.bfloat16),
            jax.ShapeDtypeStruct((rows, span, width), jnp.bfloat16),
        ],
        in_specs=smem_space(2) + any_space(9),
        out_specs=any_space(2),
        scratch_shapes=[
            pltpu.VMEM((2 * rows, span, width), jnp.bfloat16),
            pltpu.SemaphoreType.DMA,
            pltpu.SemaphoreType.DMA((2,)),
        ],
        compiler_params=pltpu.CompilerParams(vmem_limit_bytes=VMEM_LIMIT),
        cost_estimate=moved_cost(10 << 20),
        name="unpack_blocks",
    )(core[None].astype(jnp.int32), table, cache, lent, *first, *second, after)


def pack_more_body(scalars, table, cache, lent, out, held, sem):
    core, start = scalars[0], scalars[1]
    room = out.shape[1]
    requests = table.shape[1]
    half = requests // 2

    def send(at, total):
        line, place, skip, left = (table[field, at] for field in range(4))
        low = jnp.maximum(start - place, 0)
        count = jnp.maximum(jnp.minimum(left, start + room - place) - low, 0)

        def fetch(condition, source):
            @pl.when(condition)
            def _():
                @pl.loop(0, count)
                def _(block):
                    pltpu.make_async_copy(
                        source(skip + low + block), held.at[line, place + low + block - start], sem
                    ).start()

        row = at % half
        fetch(at // half == core, lambda block: blocks_of(cache, row, block, core))
        fetch(at // half != core, lambda block: blocks_of(lent, row, block, core))
        return total + count

    total = lax.fori_loop(0, requests, send, jnp.int32(0))
    wait_blocks(total, held.at[0, 0], sem)
    copy = pltpu.make_async_copy(held, out, sem)
    copy.start()
    copy.wait()


def pack_more_kernel(core, start, table, cache, lent, chips):
    lines = jax.ShapeDtypeStruct((chips, LATER, BLOCK, HEADDIM), jnp.bfloat16)
    return pl.pallas_call(
        pack_more_body,
        out_shape=lines,
        in_specs=smem_space(2) + any_space(2),
        out_specs=any_space(1)[0],
        scratch_shapes=[pltpu.VMEM(lines.shape, lines.dtype), pltpu.SemaphoreType.DMA],
        compiler_params=pltpu.CompilerParams(vmem_limit_bytes=VMEM_LIMIT),
        name="pack_later_blocks",
    )(jnp.stack([core, start]).astype(jnp.int32), table, cache, lent)


def unpack_more_body(scalars, table, pieces, _moved, _theirs, moved, theirs, held, sem):
    core, start = scalars[0], scalars[1]
    room = pieces.shape[1]
    half = theirs.shape[0]
    copy = pltpu.make_async_copy(pieces, held, sem)
    copy.start()
    copy.wait()

    def receive(at, total):
        line, place, skip, left = (table[field, at] for field in range(4))
        slot = at % half
        low = jnp.maximum(start - place, 0)
        count = jnp.maximum(jnp.minimum(left, start + room - place) - low, 0)

        def put(condition, target):
            @pl.when(condition)
            def _():
                @pl.loop(0, count)
                def _(block):
                    pltpu.make_async_copy(
                        held.at[line, place + low + block - start], target(skip + low + block), sem
                    ).start()

        put(at // half == core, lambda block: blocks_of(moved, slot, block, core))
        put(at // half != core, lambda block: blocks_of(theirs, slot, block))
        return total + count

    total = lax.fori_loop(0, 2 * half, receive, jnp.int32(0))
    wait_blocks(total, held.at[0, 0], sem)


def unpack_more_kernel(core, start, table, pieces, moved, theirs):
    return pl.pallas_call(
        unpack_more_body,
        out_shape=[
            jax.ShapeDtypeStruct(moved.shape, moved.dtype),
            jax.ShapeDtypeStruct(theirs.shape, theirs.dtype),
        ],
        in_specs=smem_space(2) + any_space(3),
        out_specs=any_space(2),
        scratch_shapes=[pltpu.VMEM(pieces.shape, pieces.dtype), pltpu.SemaphoreType.DMA],
        input_output_aliases={3: 0, 4: 1},
        compiler_params=pltpu.CompilerParams(vmem_limit_bytes=VMEM_LIMIT),
        name="unpack_later_blocks",
    )(jnp.stack([core, start]).astype(jnp.int32), table, pieces, moved, theirs)


def finish_body(scalars, returned, _, moved, held, in_sem, out_sem):
    parts = in_sem.shape[0]
    rows = returned.shape[0] // parts
    spans = [pl.ds(part * rows, rows) for part in range(parts)]
    fetches = [
        pltpu.make_async_copy(returned.at[span], held.at[span], in_sem.at[part])
        for part, span in enumerate(spans)
    ]
    stores = [
        pltpu.make_async_copy(held.at[span], moved.at[span, 1 - scalars[0]], out_sem.at[part])
        for part, span in enumerate(spans)
    ]
    for fetch in fetches:
        fetch.start()
    for fetch, store in zip(fetches, stores):
        fetch.wait()
        store.start()
    for store in stores:
        store.wait()


def finish_kernel(core, returned, moved):
    return pl.pallas_call(
        finish_body,
        out_shape=jax.ShapeDtypeStruct(moved.shape, moved.dtype),
        in_specs=smem_space(1) + any_space(2),
        out_specs=any_space(1)[0],
        scratch_shapes=[
            pltpu.VMEM(returned.shape, returned.dtype),
            pltpu.SemaphoreType.DMA((4,)),
            pltpu.SemaphoreType.DMA((4,)),
        ],
        compiler_params=pltpu.CompilerParams(vmem_limit_bytes=VMEM_LIMIT),
        input_output_aliases={2: 0},
        cost_estimate=moved_cost(6 << 20),
        name="put_other_kind",
    )(core[None].astype(jnp.int32), returned, moved)


def norm_body(slots, counts, tokens, gain, out):
    rows, width = tokens.shape
    reps, _, depth = out.shape
    chunk = 1024
    total = jnp.zeros((rows, 1), jnp.float32)
    for at in range(0, width, chunk):
        part = tokens[:, at : at + chunk].astype(jnp.float32)
        total = total + jnp.sum(part * part, axis=-1, keepdims=True)
    inverse = lax.rsqrt(total * (1.0 / width) + 1e-05)
    shape = (slots.shape[0], depth)
    row = lax.broadcasted_iota(jnp.int32, shape, 0)
    left = lax.broadcasted_iota(jnp.int32, shape, 1) < depth // 2
    table = jnp.zeros(shape, jnp.int32)
    for one in range(slots.shape[0]):
        table = jnp.where(row == one, jnp.where(left, slots[one], counts[one]), table)
    table = table.astype(jnp.float32).astype(jnp.bfloat16)
    for rep in range(reps):
        span = slice(rep * depth, (rep + 1) * depth)
        scale = gain[span].astype(jnp.float32).reshape(1, depth)
        part = tokens[:, span].astype(jnp.float32) * inverse * scale
        out[rep, :rows] = part.astype(jnp.bfloat16)
        out[rep, rows:] = table


def norm_kernel(slots, counts, tokens, gain, reps):
    rows, width = tokens.shape
    vmem = pl.BlockSpec(memory_space=pltpu.VMEM)
    return pl.pallas_call(
        norm_body,
        out_shape=jax.ShapeDtypeStruct((reps, rows + 16, width // reps), jnp.bfloat16),
        in_specs=smem_space(2) + [vmem] * 2,
        out_specs=vmem,
        compiler_params=pltpu.CompilerParams(vmem_limit_bytes=VMEM_COMPUTE),
        cost_estimate=moved_cost(4 << 20),
        name="norm_rows",
    )(slots, counts, tokens, gain)


def project_body(pick, core, slabs, w_query, w_keyval, *rest):
    out = rest[-1]
    reps, rows, depth = slabs.shape
    chips = reps // 2
    count = 16
    steps = (rows - count) // count
    requests = reps * count
    core = core[0] if pick == 0 else 1 - core[0]
    owners = slabs[:, rows - count :, :requests].reshape(chips, 2, count, requests)
    owners = jnp.where(core == 0, owners[:, 0], owners[:, 1])
    owners = owners.reshape(requests // 2, requests).astype(jnp.float32)
    number = lax.broadcasted_iota(jnp.int32, owners.shape, 1).astype(jnp.float32)
    shuffle = jnp.where(owners == number, 1.0, 0.0).astype(jnp.bfloat16)
    query_cols = w_query.shape[1]
    for step in range(steps):
        span = slice(step * count, (step + 1) * count)
        features = slabs[:, span].reshape(requests, depth)
        features = jnp.dot(shuffle, features, preferred_element_type=jnp.float32)
        features = features.astype(jnp.bfloat16)
        for weight, at in ((w_query, 0), (w_keyval, query_cols)):
            product = jnp.dot(features, weight[...], preferred_element_type=jnp.float32)
            width = product.shape[1]
            product = product.reshape(chips, count, width)
            if pick == 0:
                product = product + rest[0][:, span, at : at + width].astype(jnp.float32)
            out[:, span, at : at + width] = product.astype(jnp.bfloat16)


def project_kernel(pick, core, slabs, w_query, w_keyval, operands):
    reps, rows, _ = slabs.shape
    width = w_query.shape[1] + w_keyval.shape[1]
    vmem = pl.BlockSpec(memory_space=pltpu.VMEM)
    return pl.pallas_call(
        functools.partial(project_body, pick),
        out_shape=jax.ShapeDtypeStruct((reps // 2, rows - 16, width), jnp.bfloat16),
        in_specs=smem_space(1)
        + [vmem] * 3
        + ([vmem] if pick == 0 else any_space(len(operands))),
        out_specs=vmem,
        compiler_params=pltpu.CompilerParams(vmem_limit_bytes=VMEM_COMPUTE),
        cost_estimate=moved_cost(4 << 20),
        name="project_rows",
    )(core[None].astype(jnp.int32), slabs, w_query, w_keyval, *operands)


def attend_body(core, counts, sums, cache, *rest):
    kept, given, queries, keys, values, mixed = rest[-6:]
    at = pl.program_id(0)
    together, _, span, width = cache.shape
    rows = sums.shape[1]
    per_step = 16
    steps = rows // per_step
    heads = (sums.shape[2] - 2 * width) // width

    @pl.when(at == 0)
    def _():
        for head in range(heads + 2):
            cols = slice(head * width, (head + 1) * width)
            total = jnp.sum(sums[:, :, cols].astype(jnp.float32), axis=0)
            total = total.astype(jnp.bfloat16).astype(jnp.float32)
            if head < heads:
                queries[head * rows : (head + 1) * rows] = total
            elif head == heads:
                keys[...] = total
            else:
                values[...] = total

    many = heads * steps
    lanes = together * many
    factor = 1.0 / width**0.5
    first = at * together
    longest = counts[first]
    for one in range(1, together):
        longest = jnp.maximum(longest, counts[first + one])
    flat = (((1,), (1,)), ((), ()))
    turned = (((0,), (0,)), ((), ()))

    def gather(ref, number):
        rows_of = [ref[pl.ds(first + one, number, stride=per_step)] for one in range(together)]
        return jnp.concatenate(rows_of, axis=0).astype(jnp.bfloat16)

    def attend(reach):
        query = gather(queries, many)
        lane = lax.broadcasted_iota(jnp.int32, (1, lanes), 1)
        live = jnp.zeros((1, lanes), jnp.int32)
        old = jnp.zeros((reach, lanes), jnp.float32)
        for one in range(together):
            here = lane // many == one
            live = jnp.where(here, counts[first + one] * BLOCK, live)
            product = lax.dot_general(
                cache[one, 0, :reach], query, flat, preferred_element_type=jnp.float32
            )
            old = jnp.where(here, product, old)
        place = lax.broadcasted_iota(jnp.int32, (reach, lanes), 0)
        old = jnp.where(place < live, old * factor, -1e30)
        new = lax.dot_general(
            gather(keys, steps), query, flat, preferred_element_type=jnp.float32
        )
        row = lax.broadcasted_iota(jnp.int32, new.shape, 0)
        column = lax.broadcasted_iota(jnp.int32, new.shape, 1)
        seen = (row // steps == column // many) & (row % steps <= column % steps)
        new = jnp.where(seen, new * factor, -1e30)
        peak = jnp.maximum(
            jnp.max(old, axis=0, keepdims=True), jnp.max(new, axis=0, keepdims=True)
        )
        old = jnp.exp(old - peak)
        new = jnp.exp(new - peak)
        total = jnp.sum(old, axis=0, keepdims=True) + jnp.sum(new, axis=0, keepdims=True)
        share = 1.0 / total
        old = (old * share).astype(jnp.bfloat16)
        new = (new * share).astype(jnp.bfloat16)
        fresh = lax.dot_general(
            new, gather(values, steps), turned, preferred_element_type=jnp.float32
        )
        turned_old = jnp.transpose(old)
        for one in range(together):
            span_of = slice(one * many, (one + 1) * many)
            result = jnp.dot(
                turned_old[span_of], cache[one, 1, :reach], preferred_element_type=jnp.float32
            )
            mixed[pl.ds(first + one, many, stride=per_step)] = result + fresh[span_of]

    short = span // 2

    @pl.when(longest * BLOCK <= short)
    def _():
        attend(short)

    @pl.when(longest * BLOCK > short)
    def _():
        attend(span)

    @pl.when(at == pl.num_programs(0) - 1)
    def _():
        for one in range(2):

            @pl.when(core[0] == one)
            def _():
                for head in range(heads):
                    out = kept if head // (heads // 2) == one else given
                    at = head % (heads // 2) * width
                    out[:, at : at + width] = mixed[head * rows : (head + 1) * rows].astype(
                        jnp.bfloat16
                    )


def attend_kernel(core, counts, sums, cache, after):
    requests, kinds, span, width = cache.shape
    rows = sums.shape[1]
    cols = sums.shape[2] - 2 * width
    heads = cols // width
    together = 4
    return pl.pallas_call(
        attend_body,
        out_shape=[jax.ShapeDtypeStruct((rows, cols // 2), jnp.bfloat16)] * 2,
        grid=(requests // together,),
        in_specs=smem_space(2)
        + [
            pl.BlockSpec(sums.shape, lambda at: (0, 0, 0)),
            pl.BlockSpec((together, kinds, span, width), lambda at: (at, 0, 0, 0)),
        ]
        + any_space(len(after)),
        out_specs=[pl.BlockSpec((rows, cols // 2), lambda at: (0, 0))] * 2,
        scratch_shapes=[
            pltpu.VMEM((heads * rows, width), jnp.float32),
            pltpu.VMEM((rows, width), jnp.float32),
            pltpu.VMEM((rows, width), jnp.float32),
            pltpu.VMEM((heads * rows, width), jnp.float32),
        ],
        compiler_params=pltpu.CompilerParams(vmem_limit_bytes=VMEM_COMPUTE),
        cost_estimate=moved_cost(16 << 20),
        name="attend_old_place",
    )(core[None].astype(jnp.int32), counts, sums, cache, *after)


def output_body(core, slabs, near, far, weight, *rest):
    out = rest[-1]
    reps, rows, half = near.shape
    count = 16
    steps = rows // count
    requests = reps * count
    owners = slabs[:, rows:, :requests].reshape(requests, requests).astype(jnp.float32)
    number = lax.broadcasted_iota(jnp.int32, (requests, requests), 1).astype(jnp.float32)
    shuffle = jnp.where(owners == number, 1.0, 0.0).astype(jnp.bfloat16)
    first = pl.multiple_of(core[0] * half, half)
    second = pl.multiple_of((1 - core[0]) * half, half)
    for step in range(steps):
        span = slice(step * count, (step + 1) * count)
        product = jnp.dot(
            near[:, span].reshape(requests, half),
            weight[pl.ds(first, half)],
            preferred_element_type=jnp.float32,
        )
        product = product + jnp.dot(
            far[:, span].reshape(requests, half),
            weight[pl.ds(second, half)],
            preferred_element_type=jnp.float32,
        )
        product = lax.dot_general(
            shuffle,
            product.astype(jnp.bfloat16),
            (((0,), (0,)), ((), ())),
            preferred_element_type=jnp.float32,
        )
        out[:, span] = product.astype(jnp.bfloat16).reshape(reps, count, -1)


def output_kernel(core, slabs, near, far, weight, after):
    reps, rows, _ = near.shape
    vmem = pl.BlockSpec(memory_space=pltpu.VMEM)
    return pl.pallas_call(
        output_body,
        out_shape=jax.ShapeDtypeStruct((reps, rows, weight.shape[1]), jnp.bfloat16),
        in_specs=smem_space(1) + [vmem] * 4 + any_space(len(after)),
        out_specs=vmem,
        compiler_params=pltpu.CompilerParams(vmem_limit_bytes=VMEM_COMPUTE),
        cost_estimate=moved_cost(6 << 20),
        name="output_rows",
    )(core[None].astype(jnp.int32), slabs, near, far, weight, *after)


def per_device(
    new_tokens, norm_gain, w_query, w_keyval, w_output, kv_cache, block_counts, new_slot
):
    reps = lax.axis_size("rep")
    tps = lax.axis_size("tp")
    rep_index = lax.axis_index("rep")
    core = rep_index % 2
    chips = reps // 2
    same_core = [[2 * chip + one for chip in range(chips)] for one in range(2)]
    other_core = [(one, one ^ 1) for one in range(reps)]
    num_steps, num_rows, feat_width = new_tokens.shape
    row_total = num_steps * num_rows
    all_rows = reps * row_total
    depth = feat_width // reps
    head_cols = w_query.shape[1]
    pair_cols = w_keyval.shape[2]
    out_cols = w_output.shape[1]

    own_table = jnp.stack([new_slot, block_counts])
    other_table = lax.ppermute(own_table, "rep", other_core)
    slabs = norm_kernel(
        new_slot, block_counts, new_tokens.reshape(row_total, feat_width), norm_gain, reps
    )
    lent = lax.ppermute(kv_cache, "rep", other_core)
    slabs = lax.all_to_all(slabs, "rep", split_axis=0, concat_axis=0, tiled=True)
    my_chip = rep_index // 2
    pair_table = jnp.where(
        core == 0,
        jnp.concatenate([own_table, other_table], axis=1),
        jnp.concatenate([other_table, own_table], axis=1),
    )
    chip_rows = 2 * num_rows
    pair_slots, pair_lengths = pair_table[0], pair_table[1]
    moves, spot, fits = first_leg(
        core, jnp.broadcast_to(my_chip, (chip_rows,)), pair_slots // chip_rows, pair_lengths
    )
    order = jnp.arange(chip_rows, dtype=jnp.int32)
    at_home = jnp.where(order // num_rows == core, 1, 2)
    pack_table = jnp.stack(
        [
            jnp.where(moves, at_home, 0),
            order % num_rows,
            spot,
            jnp.clip(fits, 0, pair_lengths),
        ]
    ).astype(jnp.int32)
    sent = pack_kernel(core, pack_table, kv_cache, lent, [], 1 << 10)
    leg_one = [
        lax.ppermute(piece, "rep", line_pairs(reps, line, 0)) for line, piece in enumerate(sent)
    ]

    w_pair, *_ = lax.optimization_barrier((w_keyval, *sent))
    w_pair = w_pair.reshape(depth, 2 * pair_cols)
    theirs = project_kernel(1, core, slabs, w_query, w_pair, [sent[0]])
    late_slabs, theirs = lax.optimization_barrier((slabs, theirs))
    theirs = lax.ppermute(theirs, "rep", other_core)
    pair_sum = project_kernel(0, core, slabs, w_query, w_pair, [theirs])
    pair_sum = lax.all_to_all(
        pair_sum, "rep", split_axis=0, concat_axis=0, tiled=True, axis_index_groups=same_core
    )

    slot_table = late_slabs[:, row_total:, 0].astype(jnp.int32).reshape(-1)
    length_table = late_slabs[:, row_total:, depth // 2].astype(jnp.int32).reshape(-1)

    every = jnp.arange(reps * num_rows, dtype=jnp.int32)
    source, target = every // chip_rows, slot_table // chip_rows
    plans = []
    for one in range(2):
        moves_one, spot_one, fits_one = first_leg(one, source, target, length_table)
        moves_two, spot_two, fits_two = second_leg(one, source, target, length_table)
        done = jnp.clip(jnp.minimum(fits_one, fits_two), 0, length_table)
        missed = length_table - done
        late_place = places(source * chips + target, missed)
        plans.append((moves_one, spot_one, moves_two, spot_two, done, missed, late_place))
    most = jnp.maximum(*[jnp.max(jnp.where(plan[5] > 0, plan[6] + plan[5], 0)) for plan in plans])
    moves_one, spot_one, moves_two, spot_two, done, missed, late_place = [
        jnp.where(core == 0, one, other) for one, other in zip(*plans)
    ]
    between = jnp.where(core == 0, target // 2 * 2 + source % 2, source // 2 * 2 + target % 2)
    home = jnp.where(every // num_rows % 2 == core, 1, 2)
    from_home = every % num_rows
    passing = jnp.where(moves_two & (between == my_chip), 1, 0)
    wanted = jnp.arange(2 * chip_rows, dtype=jnp.int32)
    across_chip = my_chip // 2 * 2 + 1 - my_chip % 2
    passing_match = jnp.where(
        core == 0,
        (slot_table[None, :] == (across_chip * chip_rows + wanted)[:, None])
        & (wanted < chip_rows)[:, None],
        every[None, :] == (my_chip // 2 * 2 * chip_rows + wanted)[:, None],
    )
    passing_table = pick(
        passing_match,
        [
            passing * jnp.where(moves_one, 3, home),
            jnp.where(moves_one, spot_one, from_home),
            spot_two,
            done,
        ],
    )
    arrive_match = slot_table[None, :] == (my_chip * chip_rows + order)[:, None]
    unpack_table = pick(
        arrive_match,
        [
            jnp.where(moves_two, 4, jnp.where(moves_one, 3, home)),
            jnp.where(moves_two, spot_two, jnp.where(moves_one, spot_one, from_home)),
            done,
        ],
    )
    late_fields = [late_place, done, missed]
    late_pack = pick(
        every[None, :] == (my_chip * chip_rows + order)[:, None], [target] + late_fields
    )
    late_unpack = pick(arrive_match, [source] + late_fields)

    late_pack, late_unpack, most = lax.optimization_barrier((late_pack, late_unpack, most))
    most_row = jnp.broadcast_to(most, (1, late_pack.shape[1]))
    late_pack = jnp.concatenate([late_pack, most_row.astype(jnp.int32)])
    passed = pack_kernel(core, passing_table, kv_cache, lent, leg_one, 8 << 20)
    leg_two = [
        lax.ppermute(piece, "rep", line_pairs(reps, line, 1)) for line, piece in enumerate(passed)
    ]


    kept, given = attend_kernel(
        core,
        block_counts,
        pair_sum,
        kv_cache,
        [passed[0], unpack_table, late_pack, late_unpack],
    )

    given = lax.ppermute(given, "rep", other_core)
    kept = jnp.where(core == 0, jnp.stack([kept, given]), jnp.stack([given, kept]))
    near = lax.all_to_all(
        jnp.broadcast_to(kept[None], (chips,) + kept.shape),
        "rep",
        split_axis=0,
        concat_axis=0,
        tiled=True,
        axis_index_groups=same_core,
    ).reshape(reps, row_total, head_cols // 2)
    near, *_ = lax.optimization_barrier((near, *leg_two))
    far = lax.ppermute(near, "rep", other_core)

    partial_out = output_kernel(core, slabs, near, far, w_output, [])
    cache_moved, held = unpack_kernel(
        core, unpack_table, kv_cache, lent, leg_one, leg_two, partial_out
    )
    exchanged = lax.all_to_all(
        partial_out.reshape(tps, all_rows // tps, out_cols),
        "tp",
        split_axis=0,
        concat_axis=0,
        tiled=True,
    )
    first, exchanged = lax.optimization_barrier((jnp.int32(0), exchanged))

    def more(state):
        start, moved, other = state
        pieces = lax.all_to_all(
            pack_more_kernel(core, start, late_pack, kv_cache, lent, chips),
            "rep",
            split_axis=0,
            concat_axis=0,
            tiled=True,
            axis_index_groups=same_core,
        )
        moved, other = unpack_more_kernel(core, start, late_unpack, pieces, moved, other)
        return start + LATER, moved, other

    _, cache_moved, held = lax.while_loop(
        lambda state: state[0] < late_pack[4, 0], more, (first, cache_moved, held)
    )
    returned = lax.ppermute(held, "rep", other_core)
    cache_moved = finish_kernel(core, returned, cache_moved)
    summed = jnp.sum(exchanged.astype(jnp.float32), axis=0).astype(jnp.bfloat16)
    summed = summed.reshape(2, row_total, out_cols)
    straight = [
        (r * tps + t, (2 * t + r % 2) * tps + r // 2) for r in range(reps) for t in range(tps)
    ]
    crossed = [
        (r * tps + t, (2 * t + 1 - r % 2) * tps + r // 2) for r in range(reps) for t in range(tps)
    ]
    left = lax.ppermute(
        lax.dynamic_index_in_dim(summed, core, 0, keepdims=False), ("rep", "tp"), straight
    )
    right = lax.ppermute(
        lax.dynamic_index_in_dim(summed, 1 - core, 0, keepdims=False), ("rep", "tp"), crossed
    )
    left, right, cache_moved = lax.optimization_barrier((left, right, cache_moved))
    layer_out = jnp.where(
        core == 0,
        jnp.concatenate([left, right], axis=1),
        jnp.concatenate([right, left], axis=1),
    ).reshape(num_steps, num_rows, 2 * out_cols)

    return (layer_out, cache_moved)


def solution(mesh):
    placed = (
        P(None, "rep", None),
        P(),
        P("rep", "tp"),
        P("rep", None, "tp"),
        P("tp", "rep"),
        P("rep", None, None, "tp"),
        P("rep"),
        P("rep"),
    )
    return jax.shard_map(
        per_device,
        mesh=mesh,
        in_specs=placed,
        out_specs=(P(None, "rep", "tp"), P("rep", None, None, "tp")),
        check_vma=False,
    )
```

```python
import functools

import jax
import jax.numpy as jnp
from jax import lax
from jax.experimental import pallas as pl
from jax.experimental.pallas import tpu as pltpu
from jax.sharding import PartitionSpec as P

HEADDIM = 128
BLOCK = 128
ROOM = 38
LATER = 4
VMEM_LIMIT = 56 << 20
VMEM_COMPUTE = 24 << 20


def line_pairs(reps, line, along_first):
    across, pairs = reps // 4, []
    for one in range(reps):
        x, y, core = one // 4, one // 2 % 2, one % 2
        if core == along_first:
            pairs.append((one, (x + (1, 3, 2)[line]) % across * 4 + y * 2 + core))
        elif line < 2:
            pairs.append((one, x * 4 + (1 - y) * 2 + core))
    return pairs


def places(key, lengths):
    order = jnp.arange(key.shape[0])
    before = (key[:, None] == key[None, :]) & (order[None, :] < order[:, None])
    return jnp.sum(jnp.where(before, lengths[None, :], 0), axis=-1)


def one_leg(goes_x, source, target, x_key, y_key, lengths):
    along = (target // 2 - source // 2) % 4
    line = jnp.where(along == 1, 0, jnp.where(along == 3, 1, 2))
    moves = jnp.where(goes_x, along > 0, target % 2 != source % 2)
    place = places(jnp.where(goes_x, x_key, y_key), jnp.where(moves, lengths, 0))
    room = jnp.where(goes_x, ROOM, 2 * ROOM)
    return moves, place + jnp.where(goes_x, line * ROOM, 0), jnp.where(moves, room - place, lengths)


def first_leg(core, source, target, lengths):
    x_key, y_key = source * 4 + target // 2, source * 2 + target % 2
    return one_leg(core == 0, source, target, x_key, y_key, lengths)


def second_leg(core, source, target, lengths):
    x_key, y_key = source // 2 * 8 + target, source % 2 * 8 + target
    return one_leg(core != 0, source, target, x_key, y_key, lengths)


def too_full(source, target, lengths):
    x_part = jnp.where(target // 2 != source // 2, lengths, 0)
    y_part = jnp.where(target % 2 != source % 2, lengths, 0)
    full = jnp.zeros((), jnp.bool_)
    flows = jnp.arange(32, dtype=jnp.int32)[:, None]
    for key, part, room in (
        (source * 4 + target // 2, x_part, ROOM),
        (source // 2 * 8 + target, x_part, ROOM),
        (source * 2 + target % 2, y_part, 2 * ROOM),
        (source % 2 * 8 + target, y_part, 2 * ROOM),
    ):
        held = jnp.sum(jnp.where(key[None, :] == flows, part[None, :], 0), axis=1)
        full = full | jnp.any(held > room)
    return full


def pick(match, fields):
    return jnp.sum(jnp.where(match[None], jnp.stack(fields)[:, None, :], 0), axis=-1).astype(
        jnp.int32
    )


def blocks_of(cache, rows, block, core=None):
    span = pl.ds(pl.multiple_of(block * BLOCK, BLOCK), BLOCK)
    if core is None:
        return cache.at[rows, span]
    return cache.at[rows, core, span]


def fetch_blocks(entry, core, cache, lent, legs, put, sem):
    place, at, count = entry

    def fetch(condition, source):
        @pl.when(condition)
        def _():
            @pl.loop(0, count)
            def _(block):
                pltpu.make_async_copy(source(block), put(block), sem).start()

    fetch(place == 1, lambda block: blocks_of(cache, at, block, core))
    fetch(place == 2, lambda block: blocks_of(lent, at, block, core))
    for number, lines in enumerate(legs, 3):

        @pl.when(place == number)
        def _():
            @pl.loop(0, count)
            def _(block):
                spot = at + block
                for one, line in enumerate(lines):

                    @pl.when(spot // ROOM == one)
                    def _():
                        pltpu.make_async_copy(
                            line.at[spot - one * ROOM], put(block), sem
                        ).start()

    return jnp.where(place > 0, jnp.maximum(count, 0), 0)


def wait_blocks(total, example, sem):
    @pl.loop(0, total)
    def _(_):
        pltpu.make_async_copy(example, example, sem).wait()


def pack_body(legs, core, table, cache, lent, *rest):
    lines, (out, held, sem, out_sem) = rest[:legs], (rest[-6:-3],) + rest[-3:]

    def send(at, total):
        to = table[2, at]
        entry = (table[0, at], table[1, at], table[3, at])
        return total + fetch_blocks(
            entry, core[0], cache, lent, [lines], lambda block: held.at[to + block], sem
        )

    total = lax.fori_loop(0, table.shape[1], send, jnp.int32(0))
    wait_blocks(total, held.at[0], sem)
    copies = [
        pltpu.make_async_copy(held.at[pl.ds(line * ROOM, ROOM)], one, out_sem.at[line])
        for line, one in enumerate(out)
    ]
    for copy in copies:
        copy.start()
    for copy in copies:
        copy.wait()


def any_space(number):
    return [pl.BlockSpec(memory_space=pl.ANY)] * number


def smem_space(number):
    return [pl.BlockSpec(memory_space=pltpu.SMEM)] * number


def moved_cost(size):
    return pl.CostEstimate(flops=0, bytes_accessed=size, transcendentals=0)


def pack_kernel(core, table, cache, lent, lines, cost):
    line = jax.ShapeDtypeStruct((ROOM, BLOCK, HEADDIM), jnp.bfloat16)
    return pl.pallas_call(
        functools.partial(pack_body, len(lines)),
        out_shape=[line] * 3,
        in_specs=smem_space(2) + any_space(2 + len(lines)),
        out_specs=any_space(3),
        scratch_shapes=[
            pltpu.VMEM((3 * ROOM, BLOCK, HEADDIM), jnp.bfloat16),
            pltpu.SemaphoreType.DMA,
            pltpu.SemaphoreType.DMA((3,)),
        ],
        compiler_params=pltpu.CompilerParams(vmem_limit_bytes=VMEM_LIMIT),
        cost_estimate=moved_cost(cost),
        name="pack_blocks",
    )(core[None].astype(jnp.int32), table, cache, lent, *lines)


def unpack_body(scalars, table, cache, lent, *rest):
    first, second, rest = rest[:3], rest[3:6], rest[6:]
    _, moved, theirs, held, sem, out_sem = rest
    core = scalars[0]
    half = theirs.shape[0]
    most = cache.shape[2] // BLOCK

    def receive(at, total):
        count = table[2, at]
        entry = (table[0, at], table[1, at], count)

        @pl.loop(count, most)
        def _(block):
            span = pl.ds(pl.multiple_of(block * BLOCK, BLOCK), BLOCK)
            held[at, span] = jnp.zeros((BLOCK, HEADDIM), held.dtype)

        return total + fetch_blocks(
            entry, core, cache, lent, [first, second], lambda block: blocks_of(held, at, block), sem
        )

    total = lax.fori_loop(0, 2 * half, receive, jnp.int32(0))
    wait_blocks(total, first[0].at[0], sem)
    copies = [
        pltpu.make_async_copy(held.at[pl.ds((1 - core) * half, half)], theirs, out_sem.at[0]),
        pltpu.make_async_copy(held.at[pl.ds(core * half, half)], moved.at[:, core], out_sem.at[1]),
    ]
    for copy in copies:
        copy.start()
    for copy in copies:
        copy.wait()


def unpack_kernel(core, table, cache, lent, first, second, after):
    rows, _, span, width = cache.shape
    return pl.pallas_call(
        unpack_body,
        out_shape=[
            jax.ShapeDtypeStruct(cache.shape, jnp.bfloat16),
            jax.ShapeDtypeStruct((rows, span, width), jnp.bfloat16),
        ],
        in_specs=smem_space(2) + any_space(9),
        out_specs=any_space(2),
        scratch_shapes=[
            pltpu.VMEM((2 * rows, span, width), jnp.bfloat16),
            pltpu.SemaphoreType.DMA,
            pltpu.SemaphoreType.DMA((2,)),
        ],
        compiler_params=pltpu.CompilerParams(vmem_limit_bytes=VMEM_LIMIT),
        cost_estimate=moved_cost(10 << 20),
        name="unpack_blocks",
    )(core[None].astype(jnp.int32), table, cache, lent, *first, *second, after)


def pack_more_body(scalars, table, cache, lent, out, held, sem):
    core, start = scalars[0], scalars[1]
    room = out.shape[1]
    requests = table.shape[1]
    half = requests // 2

    def send(at, total):
        line, place, skip, left = (table[field, at] for field in range(4))
        low = jnp.maximum(start - place, 0)
        count = jnp.maximum(jnp.minimum(left, start + room - place) - low, 0)

        def fetch(condition, source):
            @pl.when(condition)
            def _():
                @pl.loop(0, count)
                def _(block):
                    pltpu.make_async_copy(
                        source(skip + low + block), held.at[line, place + low + block - start], sem
                    ).start()

        row = at % half
        fetch(at // half == core, lambda block: blocks_of(cache, row, block, core))
        fetch(at // half != core, lambda block: blocks_of(lent, row, block, core))
        return total + count

    total = lax.fori_loop(0, requests, send, jnp.int32(0))
    wait_blocks(total, held.at[0, 0], sem)
    copy = pltpu.make_async_copy(held, out, sem)
    copy.start()
    copy.wait()


def pack_more_kernel(core, start, table, cache, lent, chips):
    lines = jax.ShapeDtypeStruct((chips, LATER, BLOCK, HEADDIM), jnp.bfloat16)
    return pl.pallas_call(
        pack_more_body,
        out_shape=lines,
        in_specs=smem_space(2) + any_space(2),
        out_specs=any_space(1)[0],
        scratch_shapes=[pltpu.VMEM(lines.shape, lines.dtype), pltpu.SemaphoreType.DMA],
        compiler_params=pltpu.CompilerParams(vmem_limit_bytes=VMEM_LIMIT),
        name="pack_later_blocks",
    )(jnp.stack([core, start]).astype(jnp.int32), table, cache, lent)


def unpack_more_body(scalars, table, pieces, _moved, _theirs, moved, theirs, held, sem):
    core, start = scalars[0], scalars[1]
    room = pieces.shape[1]
    half = theirs.shape[0]
    copy = pltpu.make_async_copy(pieces, held, sem)
    copy.start()
    copy.wait()

    def receive(at, total):
        line, place, skip, left = (table[field, at] for field in range(4))
        slot = at % half
        low = jnp.maximum(start - place, 0)
        count = jnp.maximum(jnp.minimum(left, start + room - place) - low, 0)

        def put(condition, target):
            @pl.when(condition)
            def _():
                @pl.loop(0, count)
                def _(block):
                    pltpu.make_async_copy(
                        held.at[line, place + low + block - start], target(skip + low + block), sem
                    ).start()

        put(at // half == core, lambda block: blocks_of(moved, slot, block, core))
        put(at // half != core, lambda block: blocks_of(theirs, slot, block))
        return total + count

    total = lax.fori_loop(0, 2 * half, receive, jnp.int32(0))
    wait_blocks(total, held.at[0, 0], sem)


def unpack_more_kernel(core, start, table, pieces, moved, theirs):
    return pl.pallas_call(
        unpack_more_body,
        out_shape=[
            jax.ShapeDtypeStruct(moved.shape, moved.dtype),
            jax.ShapeDtypeStruct(theirs.shape, theirs.dtype),
        ],
        in_specs=smem_space(2) + any_space(3),
        out_specs=any_space(2),
        scratch_shapes=[pltpu.VMEM(pieces.shape, pieces.dtype), pltpu.SemaphoreType.DMA],
        input_output_aliases={3: 0, 4: 1},
        compiler_params=pltpu.CompilerParams(vmem_limit_bytes=VMEM_LIMIT),
        name="unpack_later_blocks",
    )(jnp.stack([core, start]).astype(jnp.int32), table, pieces, moved, theirs)


def finish_body(scalars, returned, _, moved, held, in_sem, out_sem):
    parts = in_sem.shape[0]
    rows = returned.shape[0] // parts
    spans = [pl.ds(part * rows, rows) for part in range(parts)]
    fetches = [
        pltpu.make_async_copy(returned.at[span], held.at[span], in_sem.at[part])
        for part, span in enumerate(spans)
    ]
    stores = [
        pltpu.make_async_copy(held.at[span], moved.at[span, 1 - scalars[0]], out_sem.at[part])
        for part, span in enumerate(spans)
    ]
    for fetch in fetches:
        fetch.start()
    for fetch, store in zip(fetches, stores):
        fetch.wait()
        store.start()
    for store in stores:
        store.wait()


def finish_kernel(core, returned, moved):
    return pl.pallas_call(
        finish_body,
        out_shape=jax.ShapeDtypeStruct(moved.shape, moved.dtype),
        in_specs=smem_space(1) + any_space(2),
        out_specs=any_space(1)[0],
        scratch_shapes=[
            pltpu.VMEM(returned.shape, returned.dtype),
            pltpu.SemaphoreType.DMA((4,)),
            pltpu.SemaphoreType.DMA((4,)),
        ],
        compiler_params=pltpu.CompilerParams(vmem_limit_bytes=VMEM_LIMIT),
        input_output_aliases={2: 0},
        cost_estimate=moved_cost(6 << 20),
        name="put_other_kind",
    )(core[None].astype(jnp.int32), returned, moved)


def norm_body(slots, counts, tokens, gain, out):
    rows, width = tokens.shape
    reps, _, depth = out.shape
    chunk = 1024
    total = jnp.zeros((rows, 1), jnp.float32)
    for at in range(0, width, chunk):
        part = tokens[:, at : at + chunk].astype(jnp.float32)
        total = total + jnp.sum(part * part, axis=-1, keepdims=True)
    inverse = lax.rsqrt(total * (1.0 / width) + 1e-05)
    shape = (slots.shape[0], depth)
    row = lax.broadcasted_iota(jnp.int32, shape, 0)
    left = lax.broadcasted_iota(jnp.int32, shape, 1) < depth // 2
    table = jnp.zeros(shape, jnp.int32)
    for one in range(slots.shape[0]):
        table = jnp.where(row == one, jnp.where(left, slots[one], counts[one]), table)
    table = table.astype(jnp.float32).astype(jnp.bfloat16)
    for rep in range(reps):
        span = slice(rep * depth, (rep + 1) * depth)
        scale = gain[span].astype(jnp.float32).reshape(1, depth)
        part = tokens[:, span].astype(jnp.float32) * inverse * scale
        out[rep, :rows] = part.astype(jnp.bfloat16)
        out[rep, rows:] = table


def norm_kernel(slots, counts, tokens, gain, reps):
    rows, width = tokens.shape
    vmem = pl.BlockSpec(memory_space=pltpu.VMEM)
    return pl.pallas_call(
        norm_body,
        out_shape=jax.ShapeDtypeStruct((reps, rows + 16, width // reps), jnp.bfloat16),
        in_specs=smem_space(2) + [vmem] * 2,
        out_specs=vmem,
        compiler_params=pltpu.CompilerParams(vmem_limit_bytes=VMEM_COMPUTE),
        cost_estimate=moved_cost(4 << 20),
        name="norm_rows",
    )(slots, counts, tokens, gain)


def project_body(pick, core, slabs, w_query, w_keyval, *rest):
    out = rest[-1]
    reps, rows, depth = slabs.shape
    chips = reps // 2
    count = 16
    steps = (rows - count) // count
    requests = reps * count
    core = core[0] if pick == 0 else 1 - core[0]
    owners = slabs[:, rows - count :, :requests].reshape(chips, 2, count, requests)
    owners = jnp.where(core == 0, owners[:, 0], owners[:, 1])
    owners = owners.reshape(requests // 2, requests).astype(jnp.float32)
    number = lax.broadcasted_iota(jnp.int32, owners.shape, 1).astype(jnp.float32)
    shuffle = jnp.where(owners == number, 1.0, 0.0).astype(jnp.bfloat16)
    query_cols = w_query.shape[1]
    for step in range(steps):
        span = slice(step * count, (step + 1) * count)
        features = slabs[:, span].reshape(requests, depth)
        features = jnp.dot(shuffle, features, preferred_element_type=jnp.float32)
        features = features.astype(jnp.bfloat16)
        for weight, at in ((w_query, 0), (w_keyval, query_cols)):
            product = jnp.dot(features, weight[...], preferred_element_type=jnp.float32)
            width = product.shape[1]
            product = product.reshape(chips, count, width)
            if pick == 0:
                product = product + rest[0][:, span, at : at + width].astype(jnp.float32)
            out[:, span, at : at + width] = product.astype(jnp.bfloat16)


def project_kernel(pick, core, slabs, w_query, w_keyval, operands):
    reps, rows, _ = slabs.shape
    width = w_query.shape[1] + w_keyval.shape[1]
    vmem = pl.BlockSpec(memory_space=pltpu.VMEM)
    return pl.pallas_call(
        functools.partial(project_body, pick),
        out_shape=jax.ShapeDtypeStruct((reps // 2, rows - 16, width), jnp.bfloat16),
        in_specs=smem_space(1)
        + [vmem] * 3
        + ([vmem] if pick == 0 else any_space(len(operands))),
        out_specs=vmem,
        compiler_params=pltpu.CompilerParams(vmem_limit_bytes=VMEM_COMPUTE),
        cost_estimate=moved_cost(4 << 20),
        name="project_rows",
    )(core[None].astype(jnp.int32), slabs, w_query, w_keyval, *operands)


def attend_body(core, counts, sums, cache, *rest):
    kept, given, queries, keys, values, mixed = rest[-6:]
    at = pl.program_id(0)
    together, _, span, width = cache.shape
    rows = sums.shape[1]
    per_step = 16
    steps = rows // per_step
    heads = (sums.shape[2] - 2 * width) // width

    @pl.when(at == 0)
    def _():
        for head in range(heads + 2):
            cols = slice(head * width, (head + 1) * width)
            total = jnp.sum(sums[:, :, cols].astype(jnp.float32), axis=0)
            total = total.astype(jnp.bfloat16).astype(jnp.float32)
            if head < heads:
                queries[head * rows : (head + 1) * rows] = total
            elif head == heads:
                keys[...] = total
            else:
                values[...] = total

    many = heads * steps
    lanes = together * many
    factor = 1.0 / width**0.5
    first = at * together
    longest = counts[first]
    for one in range(1, together):
        longest = jnp.maximum(longest, counts[first + one])
    flat = (((1,), (1,)), ((), ()))
    turned = (((0,), (0,)), ((), ()))

    def gather(ref, number):
        rows_of = [ref[pl.ds(first + one, number, stride=per_step)] for one in range(together)]
        return jnp.concatenate(rows_of, axis=0).astype(jnp.bfloat16)

    def attend(reach):
        query = gather(queries, many)
        lane = lax.broadcasted_iota(jnp.int32, (1, lanes), 1)
        live = jnp.zeros((1, lanes), jnp.int32)
        old = jnp.zeros((reach, lanes), jnp.float32)
        for one in range(together):
            here = lane // many == one
            live = jnp.where(here, counts[first + one] * BLOCK, live)
            product = lax.dot_general(
                cache[one, 0, :reach], query, flat, preferred_element_type=jnp.float32
            )
            old = jnp.where(here, product, old)
        place = lax.broadcasted_iota(jnp.int32, (reach, lanes), 0)
        old = jnp.where(place < live, old * factor, -1e30)
        new = lax.dot_general(
            gather(keys, steps), query, flat, preferred_element_type=jnp.float32
        )
        row = lax.broadcasted_iota(jnp.int32, new.shape, 0)
        column = lax.broadcasted_iota(jnp.int32, new.shape, 1)
        seen = (row // steps == column // many) & (row % steps <= column % steps)
        new = jnp.where(seen, new * factor, -1e30)
        peak = jnp.maximum(
            jnp.max(old, axis=0, keepdims=True), jnp.max(new, axis=0, keepdims=True)
        )
        old = jnp.exp(old - peak)
        new = jnp.exp(new - peak)
        total = jnp.sum(old, axis=0, keepdims=True) + jnp.sum(new, axis=0, keepdims=True)
        share = 1.0 / total
        old = (old * share).astype(jnp.bfloat16)
        new = (new * share).astype(jnp.bfloat16)
        fresh = lax.dot_general(
            new, gather(values, steps), turned, preferred_element_type=jnp.float32
        )
        turned_old = jnp.transpose(old)
        for one in range(together):
            span_of = slice(one * many, (one + 1) * many)
            result = jnp.dot(
                turned_old[span_of], cache[one, 1, :reach], preferred_element_type=jnp.float32
            )
            mixed[pl.ds(first + one, many, stride=per_step)] = result + fresh[span_of]

    short = span // 2

    @pl.when(longest * BLOCK <= short)
    def _():
        attend(short)

    @pl.when(longest * BLOCK > short)
    def _():
        attend(span)

    @pl.when(at == pl.num_programs(0) - 1)
    def _():
        for one in range(2):

            @pl.when(core[0] == one)
            def _():
                for head in range(heads):
                    out = kept if head // (heads // 2) == one else given
                    at = head % (heads // 2) * width
                    out[:, at : at + width] = mixed[head * rows : (head + 1) * rows].astype(
                        jnp.bfloat16
                    )


def attend_kernel(core, counts, sums, cache, after):
    requests, kinds, span, width = cache.shape
    rows = sums.shape[1]
    cols = sums.shape[2] - 2 * width
    heads = cols // width
    together = 4
    return pl.pallas_call(
        attend_body,
        out_shape=[jax.ShapeDtypeStruct((rows, cols // 2), jnp.bfloat16)] * 2,
        grid=(requests // together,),
        in_specs=smem_space(2)
        + [
            pl.BlockSpec(sums.shape, lambda at: (0, 0, 0)),
            pl.BlockSpec((together, kinds, span, width), lambda at: (at, 0, 0, 0)),
        ]
        + any_space(len(after)),
        out_specs=[pl.BlockSpec((rows, cols // 2), lambda at: (0, 0))] * 2,
        scratch_shapes=[
            pltpu.VMEM((heads * rows, width), jnp.float32),
            pltpu.VMEM((rows, width), jnp.float32),
            pltpu.VMEM((rows, width), jnp.float32),
            pltpu.VMEM((heads * rows, width), jnp.float32),
        ],
        compiler_params=pltpu.CompilerParams(vmem_limit_bytes=VMEM_COMPUTE),
        cost_estimate=moved_cost(16 << 20),
        name="attend_old_place",
    )(core[None].astype(jnp.int32), counts, sums, cache, *after)


def output_body(core, slabs, near, far, weight, *rest):
    out = rest[-1]
    reps, rows, half = near.shape
    count = 16
    steps = rows // count
    requests = reps * count
    owners = slabs[:, rows:, :requests].reshape(requests, requests).astype(jnp.float32)
    number = lax.broadcasted_iota(jnp.int32, (requests, requests), 1).astype(jnp.float32)
    shuffle = jnp.where(owners == number, 1.0, 0.0).astype(jnp.bfloat16)
    first = pl.multiple_of(core[0] * half, half)
    second = pl.multiple_of((1 - core[0]) * half, half)
    for step in range(steps):
        span = slice(step * count, (step + 1) * count)
        product = jnp.dot(
            near[:, span].reshape(requests, half),
            weight[pl.ds(first, half)],
            preferred_element_type=jnp.float32,
        )
        product = product + jnp.dot(
            far[:, span].reshape(requests, half),
            weight[pl.ds(second, half)],
            preferred_element_type=jnp.float32,
        )
        product = lax.dot_general(
            shuffle,
            product.astype(jnp.bfloat16),
            (((0,), (0,)), ((), ())),
            preferred_element_type=jnp.float32,
        )
        out[:, span] = product.astype(jnp.bfloat16).reshape(reps, count, -1)


def output_kernel(core, slabs, near, far, weight, after):
    reps, rows, _ = near.shape
    vmem = pl.BlockSpec(memory_space=pltpu.VMEM)
    return pl.pallas_call(
        output_body,
        out_shape=jax.ShapeDtypeStruct((reps, rows, weight.shape[1]), jnp.bfloat16),
        in_specs=smem_space(1) + [vmem] * 4 + any_space(len(after)),
        out_specs=vmem,
        compiler_params=pltpu.CompilerParams(vmem_limit_bytes=VMEM_COMPUTE),
        cost_estimate=moved_cost(6 << 20),
        name="output_rows",
    )(core[None].astype(jnp.int32), slabs, near, far, weight, *after)


def per_device(
    new_tokens, norm_gain, w_query, w_keyval, w_output, kv_cache, block_counts, new_slot
):
    reps = lax.axis_size("rep")
    tps = lax.axis_size("tp")
    rep_index = lax.axis_index("rep")
    core = rep_index % 2
    chips = reps // 2
    same_core = [[2 * chip + one for chip in range(chips)] for one in range(2)]
    other_core = [(one, one ^ 1) for one in range(reps)]
    num_steps, num_rows, feat_width = new_tokens.shape
    row_total = num_steps * num_rows
    all_rows = reps * row_total
    depth = feat_width // reps
    head_cols = w_query.shape[1]
    pair_cols = w_keyval.shape[2]
    out_cols = w_output.shape[1]

    own_table = jnp.stack([new_slot, block_counts])
    other_table = lax.ppermute(own_table, "rep", other_core)
    slabs = norm_kernel(
        new_slot, block_counts, new_tokens.reshape(row_total, feat_width), norm_gain, reps
    )
    lent = lax.ppermute(kv_cache, "rep", other_core)
    slabs = lax.all_to_all(slabs, "rep", split_axis=0, concat_axis=0, tiled=True)
    my_chip = rep_index // 2
    pair_table = jnp.where(
        core == 0,
        jnp.concatenate([own_table, other_table], axis=1),
        jnp.concatenate([other_table, own_table], axis=1),
    )
    chip_rows = 2 * num_rows
    pair_slots, pair_lengths = pair_table[0], pair_table[1]
    moves, spot, fits = first_leg(
        core, jnp.broadcast_to(my_chip, (chip_rows,)), pair_slots // chip_rows, pair_lengths
    )
    order = jnp.arange(chip_rows, dtype=jnp.int32)
    at_home = jnp.where(order // num_rows == core, 1, 2)
    pack_table = jnp.stack(
        [
            jnp.where(moves, at_home, 0),
            order % num_rows,
            spot,
            jnp.clip(fits, 0, pair_lengths),
        ]
    ).astype(jnp.int32)
    sent = pack_kernel(core, pack_table, kv_cache, lent, [], 1 << 10)
    leg_one = [
        lax.ppermute(piece, "rep", line_pairs(reps, line, 0)) for line, piece in enumerate(sent)
    ]

    w_pair, *_ = lax.optimization_barrier((w_keyval, *sent))
    w_pair = w_pair.reshape(depth, 2 * pair_cols)
    theirs = project_kernel(1, core, slabs, w_query, w_pair, [sent[0]])
    late_slabs, theirs = lax.optimization_barrier((slabs, theirs))
    theirs = lax.ppermute(theirs, "rep", other_core)
    pair_sum = project_kernel(0, core, slabs, w_query, w_pair, [theirs])
    pair_sum = lax.all_to_all(
        pair_sum, "rep", split_axis=0, concat_axis=0, tiled=True, axis_index_groups=same_core
    )

    slot_table = late_slabs[:, row_total:, 0].astype(jnp.int32).reshape(-1)
    length_table = late_slabs[:, row_total:, depth // 2].astype(jnp.int32).reshape(-1)

    every = jnp.arange(reps * num_rows, dtype=jnp.int32)
    source, target = every // chip_rows, slot_table // chip_rows
    moves_one, spot_one, fits_one = first_leg(core, source, target, length_table)
    moves_two, spot_two, fits_two = second_leg(core, source, target, length_table)
    done = jnp.clip(jnp.minimum(fits_one, fits_two), 0, length_table)
    overflow = too_full(source, target, length_table)
    between = jnp.where(core == 0, target // 2 * 2 + source % 2, source // 2 * 2 + target % 2)
    home = jnp.where(every // num_rows % 2 == core, 1, 2)
    from_home = every % num_rows
    passing = jnp.where(moves_two & (between == my_chip), 1, 0)
    wanted = jnp.arange(2 * chip_rows, dtype=jnp.int32)
    across_chip = my_chip // 2 * 2 + 1 - my_chip % 2
    passing_match = jnp.where(
        core == 0,
        (slot_table[None, :] == (across_chip * chip_rows + wanted)[:, None])
        & (wanted < chip_rows)[:, None],
        every[None, :] == (my_chip // 2 * 2 * chip_rows + wanted)[:, None],
    )
    passing_table = pick(
        passing_match,
        [
            passing * jnp.where(moves_one, 3, home),
            jnp.where(moves_one, spot_one, from_home),
            spot_two,
            done,
        ],
    )
    arrive_match = slot_table[None, :] == (my_chip * chip_rows + order)[:, None]
    unpack_table = pick(
        arrive_match,
        [
            jnp.where(moves_two, 4, jnp.where(moves_one, 3, home)),
            jnp.where(moves_two, spot_two, jnp.where(moves_one, spot_one, from_home)),
            done,
        ],
    )
    passed = pack_kernel(core, passing_table, kv_cache, lent, leg_one, 8 << 20)
    leg_two = [
        lax.ppermute(piece, "rep", line_pairs(reps, line, 1)) for line, piece in enumerate(passed)
    ]


    kept, given = attend_kernel(
        core,
        block_counts,
        pair_sum,
        kv_cache,
        [passed[0], unpack_table],
    )

    given = lax.ppermute(given, "rep", other_core)
    kept = jnp.where(core == 0, jnp.stack([kept, given]), jnp.stack([given, kept]))
    near = lax.all_to_all(
        jnp.broadcast_to(kept[None], (chips,) + kept.shape),
        "rep",
        split_axis=0,
        concat_axis=0,
        tiled=True,
        axis_index_groups=same_core,
    ).reshape(reps, row_total, head_cols // 2)
    near, overflow, *_ = lax.optimization_barrier((near, overflow, *leg_two))
    far = lax.ppermute(near, "rep", other_core)

    partial_out = output_kernel(core, slabs, near, far, w_output, [])
    cache_moved, held = unpack_kernel(
        core, unpack_table, kv_cache, lent, leg_one, leg_two, partial_out
    )
    exchanged = lax.all_to_all(
        partial_out.reshape(tps, all_rows // tps, out_cols),
        "tp",
        split_axis=0,
        concat_axis=0,
        tiled=True,
    )
    first, exchanged = lax.optimization_barrier((jnp.int32(0), exchanged))

    def more(state):
        start, _, moved, other = state
        plans = []
        for one in range(2):
            _, _, fits_a = first_leg(one, source, target, length_table)
            _, _, fits_b = second_leg(one, source, target, length_table)
            went = jnp.clip(jnp.minimum(fits_a, fits_b), 0, length_table)
            missed = length_table - went
            late_place = places(source * chips + target, missed)
            end = jnp.max(jnp.where(missed > 0, late_place + missed, 0))
            plans.append((late_place, went, missed, end))
        most = jnp.maximum(plans[0][3], plans[1][3])
        late_fields = [jnp.where(core == 0, one, other_one) for one, other_one in zip(*plans)][:3]
        leave_match = every[None, :] == (my_chip * chip_rows + order)[:, None]
        late_pack = pick(leave_match, [target] + late_fields)
        late_unpack = pick(arrive_match, [source] + late_fields)
        pieces = lax.all_to_all(
            pack_more_kernel(core, start, late_pack, kv_cache, lent, chips),
            "rep",
            split_axis=0,
            concat_axis=0,
            tiled=True,
            axis_index_groups=same_core,
        )
        moved, other = unpack_more_kernel(core, start, late_unpack, pieces, moved, other)
        return start + LATER, most, moved, other

    most = jnp.where(overflow, 1, 0).astype(jnp.int32)
    _, _, cache_moved, held = lax.while_loop(
        lambda state: state[0] < state[1], more, (first, most, cache_moved, held)
    )
    returned = lax.ppermute(held, "rep", other_core)
    cache_moved = finish_kernel(core, returned, cache_moved)
    summed = jnp.sum(exchanged.astype(jnp.float32), axis=0).astype(jnp.bfloat16)
    summed = summed.reshape(2, row_total, out_cols)
    straight = [
        (r * tps + t, (2 * t + r % 2) * tps + r // 2) for r in range(reps) for t in range(tps)
    ]
    crossed = [
        (r * tps + t, (2 * t + 1 - r % 2) * tps + r // 2) for r in range(reps) for t in range(tps)
    ]
    left = lax.ppermute(
        lax.dynamic_index_in_dim(summed, core, 0, keepdims=False), ("rep", "tp"), straight
    )
    right = lax.ppermute(
        lax.dynamic_index_in_dim(summed, 1 - core, 0, keepdims=False), ("rep", "tp"), crossed
    )
    left, right, cache_moved = lax.optimization_barrier((left, right, cache_moved))
    layer_out = jnp.where(
        core == 0,
        jnp.concatenate([left, right], axis=1),
        jnp.concatenate([right, left], axis=1),
    ).reshape(num_steps, num_rows, 2 * out_cols)

    return (layer_out, cache_moved)


def solution(mesh):
    placed = (
        P(None, "rep", None),
        P(),
        P("rep", "tp"),
        P("rep", None, "tp"),
        P("tp", "rep"),
        P("rep", None, None, "tp"),
        P("rep"),
        P("rep"),
    )
    return jax.shard_map(
        per_device,
        mesh=mesh,
        in_specs=placed,
        out_specs=(P(None, "rep", "tp"), P("rep", None, None, "tp")),
        check_vma=False,
    )
```

```python
import functools

import jax
import jax.numpy as jnp
from jax import lax
from jax.experimental import pallas as pl
from jax.experimental.pallas import tpu as pltpu
from jax.sharding import PartitionSpec as P

HEADDIM = 128
BLOCK = 128
ROOM = 38
LATER = 4
VMEM_LIMIT = 56 << 20
VMEM_COMPUTE = 24 << 20


def line_pairs(reps, line, along_first):
    across, pairs = reps // 4, []
    for one in range(reps):
        x, y, core = one // 4, one // 2 % 2, one % 2
        if core == along_first:
            pairs.append((one, (x + (1, 3, 2)[line]) % across * 4 + y * 2 + core))
        elif line < 2:
            pairs.append((one, x * 4 + (1 - y) * 2 + core))
    return pairs


def places(key, lengths):
    order = jnp.arange(key.shape[0])
    before = (key[:, None] == key[None, :]) & (order[None, :] < order[:, None])
    return jnp.sum(jnp.where(before, lengths[None, :], 0), axis=-1)


def one_leg(goes_x, source, target, x_key, y_key, lengths):
    along = (target // 2 - source // 2) % 4
    line = jnp.where(along == 1, 0, jnp.where(along == 3, 1, 2))
    moves = jnp.where(goes_x, along > 0, target % 2 != source % 2)
    place = places(jnp.where(goes_x, x_key, y_key), jnp.where(moves, lengths, 0))
    room = jnp.where(goes_x, ROOM, 2 * ROOM)
    return moves, place + jnp.where(goes_x, line * ROOM, 0), jnp.where(moves, room - place, lengths)


def first_leg(core, source, target, lengths):
    x_key, y_key = source * 4 + target // 2, source * 2 + target % 2
    return one_leg(core == 0, source, target, x_key, y_key, lengths)


def second_leg(core, source, target, lengths):
    x_key, y_key = source // 2 * 8 + target, source % 2 * 8 + target
    return one_leg(core != 0, source, target, x_key, y_key, lengths)


def too_full(source, target, lengths):
    x_part = jnp.where(target // 2 != source // 2, lengths, 0)
    y_part = jnp.where(target % 2 != source % 2, lengths, 0)
    full = jnp.zeros((), jnp.bool_)
    flows = jnp.arange(32, dtype=jnp.int32)[:, None]
    for key, part, room in (
        (source * 4 + target // 2, x_part, ROOM),
        (source // 2 * 8 + target, x_part, ROOM),
        (source * 2 + target % 2, y_part, 2 * ROOM),
        (source % 2 * 8 + target, y_part, 2 * ROOM),
    ):
        held = jnp.sum(jnp.where(key[None, :] == flows, part[None, :], 0), axis=1)
        full = full | jnp.any(held > room)
    return full


def pick(match, fields):
    return jnp.sum(jnp.where(match[None], jnp.stack(fields)[:, None, :], 0), axis=-1).astype(
        jnp.int32
    )


def blocks_of(cache, rows, block, core=None):
    span = pl.ds(pl.multiple_of(block * BLOCK, BLOCK), BLOCK)
    if core is None:
        return cache.at[rows, span]
    return cache.at[rows, core, span]


def fetch_blocks(entry, core, cache, lent, legs, put, sem):
    place, at, count = entry

    def fetch(condition, source):
        @pl.when(condition)
        def _():
            @pl.loop(0, count)
            def _(block):
                pltpu.make_async_copy(source(block), put(block), sem).start()

    fetch(place == 1, lambda block: blocks_of(cache, at, block, core))
    fetch(place == 2, lambda block: blocks_of(lent, at, block, core))
    for number, lines in enumerate(legs, 3):

        @pl.when(place == number)
        def _():
            @pl.loop(0, count)
            def _(block):
                spot = at + block
                for one, line in enumerate(lines):

                    @pl.when(spot // ROOM == one)
                    def _():
                        pltpu.make_async_copy(
                            line.at[spot - one * ROOM], put(block), sem
                        ).start()

    return jnp.where(place > 0, jnp.maximum(count, 0), 0)


def wait_blocks(total, example, sem):
    @pl.loop(0, total)
    def _(_):
        pltpu.make_async_copy(example, example, sem).wait()


def pack_body(legs, core, table, cache, lent, *rest):
    lines, (out, held, sem, out_sem) = rest[:legs], (rest[-6:-3],) + rest[-3:]

    def send(at, total):
        to = table[2, at]
        entry = (table[0, at], table[1, at], table[3, at])
        return total + fetch_blocks(
            entry, core[0], cache, lent, [lines], lambda block: held.at[to + block], sem
        )

    total = lax.fori_loop(0, table.shape[1], send, jnp.int32(0))
    wait_blocks(total, held.at[0], sem)
    copies = [
        pltpu.make_async_copy(held.at[pl.ds(line * ROOM, ROOM)], one, out_sem.at[line])
        for line, one in enumerate(out)
    ]
    for copy in copies:
        copy.start()
    for copy in copies:
        copy.wait()


def any_space(number):
    return [pl.BlockSpec(memory_space=pl.ANY)] * number


def smem_space(number):
    return [pl.BlockSpec(memory_space=pltpu.SMEM)] * number


def moved_cost(size):
    return pl.CostEstimate(flops=0, bytes_accessed=size, transcendentals=0)


def pack_kernel(core, table, cache, lent, lines, cost):
    line = jax.ShapeDtypeStruct((ROOM, BLOCK, HEADDIM), jnp.bfloat16)
    return pl.pallas_call(
        functools.partial(pack_body, len(lines)),
        out_shape=[line] * 3,
        in_specs=smem_space(2) + any_space(2 + len(lines)),
        out_specs=any_space(3),
        scratch_shapes=[
            pltpu.VMEM((3 * ROOM, BLOCK, HEADDIM), jnp.bfloat16),
            pltpu.SemaphoreType.DMA,
            pltpu.SemaphoreType.DMA((3,)),
        ],
        compiler_params=pltpu.CompilerParams(vmem_limit_bytes=VMEM_LIMIT),
        cost_estimate=moved_cost(cost),
        name="pack_blocks",
    )(core[None].astype(jnp.int32), table, cache, lent, *lines)


def unpack_body(scalars, table, cache, lent, *rest):
    first, second, rest = rest[:3], rest[3:6], rest[6:]
    _, moved, theirs, held, sem, out_sem = rest
    core = scalars[0]
    half = theirs.shape[0]
    most = cache.shape[2] // BLOCK

    def receive(at, total):
        count = table[2, at]
        entry = (table[0, at], table[1, at], count)

        @pl.loop(count, most)
        def _(block):
            span = pl.ds(pl.multiple_of(block * BLOCK, BLOCK), BLOCK)
            held[at, span] = jnp.zeros((BLOCK, HEADDIM), held.dtype)

        return total + fetch_blocks(
            entry, core, cache, lent, [first, second], lambda block: blocks_of(held, at, block), sem
        )

    total = lax.fori_loop(0, 2 * half, receive, jnp.int32(0))
    wait_blocks(total, first[0].at[0], sem)
    copies = [
        pltpu.make_async_copy(held.at[pl.ds((1 - core) * half, half)], theirs, out_sem.at[0]),
        pltpu.make_async_copy(held.at[pl.ds(core * half, half)], moved.at[:, core], out_sem.at[1]),
    ]
    for copy in copies:
        copy.start()
    for copy in copies:
        copy.wait()


def unpack_kernel(core, table, cache, lent, first, second, after):
    rows, _, span, width = cache.shape
    return pl.pallas_call(
        unpack_body,
        out_shape=[
            jax.ShapeDtypeStruct(cache.shape, jnp.bfloat16),
            jax.ShapeDtypeStruct((rows, span, width), jnp.bfloat16),
        ],
        in_specs=smem_space(2) + any_space(9),
        out_specs=any_space(2),
        scratch_shapes=[
            pltpu.VMEM((2 * rows, span, width), jnp.bfloat16),
            pltpu.SemaphoreType.DMA,
            pltpu.SemaphoreType.DMA((2,)),
        ],
        compiler_params=pltpu.CompilerParams(vmem_limit_bytes=VMEM_LIMIT),
        cost_estimate=moved_cost(10 << 20),
        name="unpack_blocks",
    )(core[None].astype(jnp.int32), table, cache, lent, *first, *second, after)


def pack_more_body(scalars, table, cache, lent, out, held, sem):
    core, start = scalars[0], scalars[1]
    room = out.shape[1]
    requests = table.shape[1]
    half = requests // 2

    def send(at, total):
        line, place, skip, left = (table[field, at] for field in range(4))
        low = jnp.maximum(start - place, 0)
        count = jnp.maximum(jnp.minimum(left, start + room - place) - low, 0)

        def fetch(condition, source):
            @pl.when(condition)
            def _():
                @pl.loop(0, count)
                def _(block):
                    pltpu.make_async_copy(
                        source(skip + low + block), held.at[line, place + low + block - start], sem
                    ).start()

        row = at % half
        fetch(at // half == core, lambda block: blocks_of(cache, row, block, core))
        fetch(at // half != core, lambda block: blocks_of(lent, row, block, core))
        return total + count

    total = lax.fori_loop(0, requests, send, jnp.int32(0))
    wait_blocks(total, held.at[0, 0], sem)
    copy = pltpu.make_async_copy(held, out, sem)
    copy.start()
    copy.wait()


def pack_more_kernel(core, start, table, cache, lent, chips):
    lines = jax.ShapeDtypeStruct((chips, LATER, BLOCK, HEADDIM), jnp.bfloat16)
    return pl.pallas_call(
        pack_more_body,
        out_shape=lines,
        in_specs=smem_space(2) + any_space(2),
        out_specs=any_space(1)[0],
        scratch_shapes=[pltpu.VMEM(lines.shape, lines.dtype), pltpu.SemaphoreType.DMA],
        compiler_params=pltpu.CompilerParams(vmem_limit_bytes=VMEM_LIMIT),
        name="pack_later_blocks",
    )(jnp.stack([core, start]).astype(jnp.int32), table, cache, lent)


def unpack_more_body(scalars, table, pieces, _moved, _theirs, moved, theirs, held, sem):
    core, start = scalars[0], scalars[1]
    room = pieces.shape[1]
    half = theirs.shape[0]
    copy = pltpu.make_async_copy(pieces, held, sem)
    copy.start()
    copy.wait()

    def receive(at, total):
        line, place, skip, left = (table[field, at] for field in range(4))
        slot = at % half
        low = jnp.maximum(start - place, 0)
        count = jnp.maximum(jnp.minimum(left, start + room - place) - low, 0)

        def put(condition, target):
            @pl.when(condition)
            def _():
                @pl.loop(0, count)
                def _(block):
                    pltpu.make_async_copy(
                        held.at[line, place + low + block - start], target(skip + low + block), sem
                    ).start()

        put(at // half == core, lambda block: blocks_of(moved, slot, block, core))
        put(at // half != core, lambda block: blocks_of(theirs, slot, block))
        return total + count

    total = lax.fori_loop(0, 2 * half, receive, jnp.int32(0))
    wait_blocks(total, held.at[0, 0], sem)


def unpack_more_kernel(core, start, table, pieces, moved, theirs):
    return pl.pallas_call(
        unpack_more_body,
        out_shape=[
            jax.ShapeDtypeStruct(moved.shape, moved.dtype),
            jax.ShapeDtypeStruct(theirs.shape, theirs.dtype),
        ],
        in_specs=smem_space(2) + any_space(3),
        out_specs=any_space(2),
        scratch_shapes=[pltpu.VMEM(pieces.shape, pieces.dtype), pltpu.SemaphoreType.DMA],
        input_output_aliases={3: 0, 4: 1},
        compiler_params=pltpu.CompilerParams(vmem_limit_bytes=VMEM_LIMIT),
        name="unpack_later_blocks",
    )(jnp.stack([core, start]).astype(jnp.int32), table, pieces, moved, theirs)


def finish_body(scalars, returned, _, moved, held, in_sem, out_sem):
    parts = in_sem.shape[0]
    rows = returned.shape[0] // parts
    spans = [pl.ds(part * rows, rows) for part in range(parts)]
    fetches = [
        pltpu.make_async_copy(returned.at[span], held.at[span], in_sem.at[part])
        for part, span in enumerate(spans)
    ]
    stores = [
        pltpu.make_async_copy(held.at[span], moved.at[span, 1 - scalars[0]], out_sem.at[part])
        for part, span in enumerate(spans)
    ]
    for fetch in fetches:
        fetch.start()
    for fetch, store in zip(fetches, stores):
        fetch.wait()
        store.start()
    for store in stores:
        store.wait()


def finish_kernel(core, returned, moved):
    return pl.pallas_call(
        finish_body,
        out_shape=jax.ShapeDtypeStruct(moved.shape, moved.dtype),
        in_specs=smem_space(1) + any_space(2),
        out_specs=any_space(1)[0],
        scratch_shapes=[
            pltpu.VMEM(returned.shape, returned.dtype),
            pltpu.SemaphoreType.DMA((4,)),
            pltpu.SemaphoreType.DMA((4,)),
        ],
        compiler_params=pltpu.CompilerParams(vmem_limit_bytes=VMEM_LIMIT),
        input_output_aliases={2: 0},
        cost_estimate=moved_cost(6 << 20),
        name="put_other_kind",
    )(core[None].astype(jnp.int32), returned, moved)


def norm_body(slots, counts, tokens, gain, out):
    rows, width = tokens.shape
    reps, _, depth = out.shape
    chunk = 1024
    total = jnp.zeros((rows, 1), jnp.float32)
    for at in range(0, width, chunk):
        part = tokens[:, at : at + chunk].astype(jnp.float32)
        total = total + jnp.sum(part * part, axis=-1, keepdims=True)
    inverse = lax.rsqrt(total * (1.0 / width) + 1e-05)
    shape = (slots.shape[0], depth)
    row = lax.broadcasted_iota(jnp.int32, shape, 0)
    left = lax.broadcasted_iota(jnp.int32, shape, 1) < depth // 2
    table = jnp.zeros(shape, jnp.int32)
    for one in range(slots.shape[0]):
        table = jnp.where(row == one, jnp.where(left, slots[one], counts[one]), table)
    table = table.astype(jnp.float32).astype(jnp.bfloat16)
    for rep in range(reps):
        span = slice(rep * depth, (rep + 1) * depth)
        scale = gain[span].astype(jnp.float32).reshape(1, depth)
        part = tokens[:, span].astype(jnp.float32) * inverse * scale
        out[rep, :rows] = part.astype(jnp.bfloat16)
        out[rep, rows:] = table


def norm_kernel(slots, counts, tokens, gain, reps):
    rows, width = tokens.shape
    vmem = pl.BlockSpec(memory_space=pltpu.VMEM)
    return pl.pallas_call(
        norm_body,
        out_shape=jax.ShapeDtypeStruct((reps, rows + 16, width // reps), jnp.bfloat16),
        in_specs=smem_space(2) + [vmem] * 2,
        out_specs=vmem,
        compiler_params=pltpu.CompilerParams(vmem_limit_bytes=VMEM_COMPUTE),
        cost_estimate=moved_cost(4 << 20),
        name="norm_rows",
    )(slots, counts, tokens, gain)


def project_body(pick, core, slabs, w_query, w_keyval, *rest):
    out = rest[-1]
    reps, rows, depth = slabs.shape
    chips = reps // 2
    count = 16
    steps = (rows - count) // count
    requests = reps * count
    core = core[0] if pick == 0 else 1 - core[0]
    owners = slabs[:, rows - count :, :requests].reshape(chips, 2, count, requests)
    owners = jnp.where(core == 0, owners[:, 0], owners[:, 1])
    owners = owners.reshape(requests // 2, requests).astype(jnp.float32)
    number = lax.broadcasted_iota(jnp.int32, owners.shape, 1).astype(jnp.float32)
    shuffle = jnp.where(owners == number, 1.0, 0.0).astype(jnp.bfloat16)
    query_cols = w_query.shape[1]
    for step in range(steps):
        span = slice(step * count, (step + 1) * count)
        features = slabs[:, span].reshape(requests, depth)
        features = jnp.dot(shuffle, features, preferred_element_type=jnp.float32)
        features = features.astype(jnp.bfloat16)
        for weight, at in ((w_query, 0), (w_keyval, query_cols)):
            product = jnp.dot(features, weight[...], preferred_element_type=jnp.float32)
            width = product.shape[1]
            product = product.reshape(chips, count, width)
            if pick == 0:
                product = product + rest[0][:, span, at : at + width].astype(jnp.float32)
            out[:, span, at : at + width] = product.astype(jnp.bfloat16)


def project_kernel(pick, core, slabs, w_query, w_keyval, operands):
    reps, rows, _ = slabs.shape
    width = w_query.shape[1] + w_keyval.shape[1]
    vmem = pl.BlockSpec(memory_space=pltpu.VMEM)
    return pl.pallas_call(
        functools.partial(project_body, pick),
        out_shape=jax.ShapeDtypeStruct((reps // 2, rows - 16, width), jnp.bfloat16),
        in_specs=smem_space(1)
        + [vmem] * 3
        + ([vmem] if pick == 0 else any_space(len(operands))),
        out_specs=vmem,
        compiler_params=pltpu.CompilerParams(vmem_limit_bytes=VMEM_COMPUTE),
        cost_estimate=moved_cost(4 << 20),
        name="project_rows",
    )(core[None].astype(jnp.int32), slabs, w_query, w_keyval, *operands)


def attend_body(core, counts, sums, cache, *rest):
    kept, given, queries, keys, values, mixed = rest[-6:]
    at = pl.program_id(0)
    together, _, span, width = cache.shape
    rows = sums.shape[1]
    per_step = 16
    steps = rows // per_step
    heads = (sums.shape[2] - 2 * width) // width

    @pl.when(at == 0)
    def _():
        for head in range(heads + 2):
            cols = slice(head * width, (head + 1) * width)
            total = jnp.sum(sums[:, :, cols].astype(jnp.float32), axis=0)
            total = total.astype(jnp.bfloat16).astype(jnp.float32)
            if head < heads:
                queries[head * rows : (head + 1) * rows] = total
            elif head == heads:
                keys[...] = total
            else:
                values[...] = total

    many = heads * steps
    lanes = together * many
    factor = 1.0 / width**0.5
    first = at * together
    longest = counts[first]
    for one in range(1, together):
        longest = jnp.maximum(longest, counts[first + one])
    flat = (((1,), (1,)), ((), ()))
    turned = (((0,), (0,)), ((), ()))

    def gather(ref, number):
        rows_of = [ref[pl.ds(first + one, number, stride=per_step)] for one in range(together)]
        return jnp.concatenate(rows_of, axis=0).astype(jnp.bfloat16)

    def attend(reach):
        query = gather(queries, many)
        lane = lax.broadcasted_iota(jnp.int32, (1, lanes), 1)
        live = jnp.zeros((1, lanes), jnp.int32)
        old = jnp.zeros((reach, lanes), jnp.float32)
        for one in range(together):
            here = lane // many == one
            live = jnp.where(here, counts[first + one] * BLOCK, live)
            product = lax.dot_general(
                cache[one, 0, :reach], query, flat, preferred_element_type=jnp.float32
            )
            old = jnp.where(here, product, old)
        place = lax.broadcasted_iota(jnp.int32, (reach, lanes), 0)
        old = jnp.where(place < live, old * factor, -1e30)
        new = lax.dot_general(
            gather(keys, steps), query, flat, preferred_element_type=jnp.float32
        )
        row = lax.broadcasted_iota(jnp.int32, new.shape, 0)
        column = lax.broadcasted_iota(jnp.int32, new.shape, 1)
        seen = (row // steps == column // many) & (row % steps <= column % steps)
        new = jnp.where(seen, new * factor, -1e30)
        peak = jnp.maximum(
            jnp.max(old, axis=0, keepdims=True), jnp.max(new, axis=0, keepdims=True)
        )
        old = jnp.exp(old - peak)
        new = jnp.exp(new - peak)
        total = jnp.sum(old, axis=0, keepdims=True) + jnp.sum(new, axis=0, keepdims=True)
        share = 1.0 / total
        old = (old * share).astype(jnp.bfloat16)
        new = (new * share).astype(jnp.bfloat16)
        fresh = lax.dot_general(
            new, gather(values, steps), turned, preferred_element_type=jnp.float32
        )
        turned_old = jnp.transpose(old)
        for one in range(together):
            span_of = slice(one * many, (one + 1) * many)
            result = jnp.dot(
                turned_old[span_of], cache[one, 1, :reach], preferred_element_type=jnp.float32
            )
            mixed[pl.ds(first + one, many, stride=per_step)] = result + fresh[span_of]

    short = span // 2

    @pl.when(longest * BLOCK <= short)
    def _():
        attend(short)

    @pl.when(longest * BLOCK > short)
    def _():
        attend(span)

    @pl.when(at == pl.num_programs(0) - 1)
    def _():
        for one in range(2):

            @pl.when(core[0] == one)
            def _():
                for head in range(heads):
                    out = kept if head // (heads // 2) == one else given
                    at = head % (heads // 2) * width
                    out[:, at : at + width] = mixed[head * rows : (head + 1) * rows].astype(
                        jnp.bfloat16
                    )


def attend_kernel(core, counts, sums, cache, after):
    requests, kinds, span, width = cache.shape
    rows = sums.shape[1]
    cols = sums.shape[2] - 2 * width
    heads = cols // width
    together = 4
    return pl.pallas_call(
        attend_body,
        out_shape=[jax.ShapeDtypeStruct((rows, cols // 2), jnp.bfloat16)] * 2,
        grid=(requests // together,),
        in_specs=smem_space(2)
        + [
            pl.BlockSpec(sums.shape, lambda at: (0, 0, 0)),
            pl.BlockSpec((together, kinds, span, width), lambda at: (at, 0, 0, 0)),
        ]
        + any_space(len(after)),
        out_specs=[pl.BlockSpec((rows, cols // 2), lambda at: (0, 0))] * 2,
        scratch_shapes=[
            pltpu.VMEM((heads * rows, width), jnp.float32),
            pltpu.VMEM((rows, width), jnp.float32),
            pltpu.VMEM((rows, width), jnp.float32),
            pltpu.VMEM((heads * rows, width), jnp.float32),
        ],
        compiler_params=pltpu.CompilerParams(vmem_limit_bytes=VMEM_COMPUTE),
        cost_estimate=moved_cost(16 << 20),
        name="attend_old_place",
    )(core[None].astype(jnp.int32), counts, sums, cache, *after)


def output_body(core, slabs, near, far, weight, *rest):
    out = rest[-1]
    reps, rows, half = near.shape
    count = 16
    steps = rows // count
    requests = reps * count
    owners = slabs[:, rows:, :requests].reshape(requests, requests).astype(jnp.float32)
    number = lax.broadcasted_iota(jnp.int32, (requests, requests), 1).astype(jnp.float32)
    shuffle = jnp.where(owners == number, 1.0, 0.0).astype(jnp.bfloat16)
    first = pl.multiple_of(core[0] * half, half)
    second = pl.multiple_of((1 - core[0]) * half, half)
    for step in range(steps):
        span = slice(step * count, (step + 1) * count)
        product = jnp.dot(
            near[:, span].reshape(requests, half),
            weight[pl.ds(first, half)],
            preferred_element_type=jnp.float32,
        )
        product = product + jnp.dot(
            far[:, span].reshape(requests, half),
            weight[pl.ds(second, half)],
            preferred_element_type=jnp.float32,
        )
        product = lax.dot_general(
            shuffle,
            product.astype(jnp.bfloat16),
            (((0,), (0,)), ((), ())),
            preferred_element_type=jnp.float32,
        )
        product = product.astype(jnp.bfloat16).reshape(reps, count, -1)
        for pair in range(reps // 2):
            slot = (pair // 2 + reps // 4 - core[1]) % (reps // 4) * 2 + pair % 2
            out[pl.ds(2 * slot, 2), span] = product[2 * pair : 2 * pair + 2]


def output_kernel(core, turn, slabs, near, far, weight, after):
    reps, rows, _ = near.shape
    vmem = pl.BlockSpec(memory_space=pltpu.VMEM)
    return pl.pallas_call(
        output_body,
        out_shape=jax.ShapeDtypeStruct((reps, rows, weight.shape[1]), jnp.bfloat16),
        in_specs=smem_space(1) + [vmem] * 4 + any_space(len(after)),
        out_specs=vmem,
        compiler_params=pltpu.CompilerParams(vmem_limit_bytes=VMEM_COMPUTE),
        cost_estimate=moved_cost(6 << 20),
        name="output_rows",
    )(jnp.stack([core, turn]).astype(jnp.int32), slabs, near, far, weight, *after)


def per_device(
    new_tokens, norm_gain, w_query, w_keyval, w_output, kv_cache, block_counts, new_slot
):
    reps = lax.axis_size("rep")
    tps = lax.axis_size("tp")
    rep_index = lax.axis_index("rep")
    core = rep_index % 2
    chips = reps // 2
    same_core = [[2 * chip + one for chip in range(chips)] for one in range(2)]
    other_core = [(one, one ^ 1) for one in range(reps)]
    num_steps, num_rows, feat_width = new_tokens.shape
    row_total = num_steps * num_rows
    all_rows = reps * row_total
    depth = feat_width // reps
    head_cols = w_query.shape[1]
    pair_cols = w_keyval.shape[2]
    out_cols = w_output.shape[1]

    own_table = jnp.stack([new_slot, block_counts])
    other_table = lax.ppermute(own_table, "rep", other_core)
    slabs = norm_kernel(
        new_slot, block_counts, new_tokens.reshape(row_total, feat_width), norm_gain, reps
    )
    lent = lax.ppermute(kv_cache, "rep", other_core)
    slabs = lax.all_to_all(slabs, "rep", split_axis=0, concat_axis=0, tiled=True)
    my_chip = rep_index // 2
    pair_table = jnp.where(
        core == 0,
        jnp.concatenate([own_table, other_table], axis=1),
        jnp.concatenate([other_table, own_table], axis=1),
    )
    chip_rows = 2 * num_rows
    pair_slots, pair_lengths = pair_table[0], pair_table[1]
    moves, spot, fits = first_leg(
        core, jnp.broadcast_to(my_chip, (chip_rows,)), pair_slots // chip_rows, pair_lengths
    )
    order = jnp.arange(chip_rows, dtype=jnp.int32)
    at_home = jnp.where(order // num_rows == core, 1, 2)
    pack_table = jnp.stack(
        [
            jnp.where(moves, at_home, 0),
            order % num_rows,
            spot,
            jnp.clip(fits, 0, pair_lengths),
        ]
    ).astype(jnp.int32)
    sent = pack_kernel(core, pack_table, kv_cache, lent, [], 1 << 10)
    leg_one = [
        lax.ppermute(piece, "rep", line_pairs(reps, line, 0)) for line, piece in enumerate(sent)
    ]

    w_pair, *_ = lax.optimization_barrier((w_keyval, *sent))
    w_pair = w_pair.reshape(depth, 2 * pair_cols)
    theirs = project_kernel(1, core, slabs, w_query, w_pair, [sent[0]])
    late_slabs, theirs = lax.optimization_barrier((slabs, theirs))
    theirs = lax.ppermute(theirs, "rep", other_core)
    pair_sum = project_kernel(0, core, slabs, w_query, w_pair, [theirs])
    pair_sum = lax.all_to_all(
        pair_sum, "rep", split_axis=0, concat_axis=0, tiled=True, axis_index_groups=same_core
    )

    slot_table = late_slabs[:, row_total:, 0].astype(jnp.int32).reshape(-1)
    length_table = late_slabs[:, row_total:, depth // 2].astype(jnp.int32).reshape(-1)

    every = jnp.arange(reps * num_rows, dtype=jnp.int32)
    source, target = every // chip_rows, slot_table // chip_rows
    moves_one, spot_one, fits_one = first_leg(core, source, target, length_table)
    moves_two, spot_two, fits_two = second_leg(core, source, target, length_table)
    done = jnp.clip(jnp.minimum(fits_one, fits_two), 0, length_table)
    overflow = too_full(source, target, length_table)
    between = jnp.where(core == 0, target // 2 * 2 + source % 2, source // 2 * 2 + target % 2)
    home = jnp.where(every // num_rows % 2 == core, 1, 2)
    from_home = every % num_rows
    passing = jnp.where(moves_two & (between == my_chip), 1, 0)
    wanted = jnp.arange(2 * chip_rows, dtype=jnp.int32)
    across_chip = my_chip // 2 * 2 + 1 - my_chip % 2
    passing_match = jnp.where(
        core == 0,
        (slot_table[None, :] == (across_chip * chip_rows + wanted)[:, None])
        & (wanted < chip_rows)[:, None],
        every[None, :] == (my_chip // 2 * 2 * chip_rows + wanted)[:, None],
    )
    passing_table = pick(
        passing_match,
        [
            passing * jnp.where(moves_one, 3, home),
            jnp.where(moves_one, spot_one, from_home),
            spot_two,
            done,
        ],
    )
    arrive_match = slot_table[None, :] == (my_chip * chip_rows + order)[:, None]
    unpack_table = pick(
        arrive_match,
        [
            jnp.where(moves_two, 4, jnp.where(moves_one, 3, home)),
            jnp.where(moves_two, spot_two, jnp.where(moves_one, spot_one, from_home)),
            done,
        ],
    )
    passed = pack_kernel(core, passing_table, kv_cache, lent, leg_one, 8 << 20)
    leg_two = [
        lax.ppermute(piece, "rep", line_pairs(reps, line, 1)) for line, piece in enumerate(passed)
    ]


    kept, given = attend_kernel(
        core,
        block_counts,
        pair_sum,
        kv_cache,
        [passed[0], unpack_table],
    )

    given = lax.ppermute(given, "rep", other_core)
    kept = jnp.where(core == 0, jnp.stack([kept, given]), jnp.stack([given, kept]))
    near = lax.all_to_all(
        jnp.broadcast_to(kept[None], (chips,) + kept.shape),
        "rep",
        split_axis=0,
        concat_axis=0,
        tiled=True,
        axis_index_groups=same_core,
    ).reshape(reps, row_total, head_cols // 2)
    near, overflow, *_ = lax.optimization_barrier((near, overflow, *leg_two))
    far = lax.ppermute(near, "rep", other_core)

    partial_out = output_kernel(core, rep_index // 4, slabs, near, far, w_output, [])
    cache_moved, held = unpack_kernel(
        core, unpack_table, kv_cache, lent, leg_one, leg_two, partial_out
    )
    exchanged = lax.all_to_all(
        partial_out.reshape(tps, all_rows // tps, out_cols),
        "tp",
        split_axis=0,
        concat_axis=0,
        tiled=True,
    )
    first, exchanged = lax.optimization_barrier((jnp.int32(0), exchanged))

    def more(state):
        start, _, moved, other = state
        plans = []
        for one in range(2):
            _, _, fits_a = first_leg(one, source, target, length_table)
            _, _, fits_b = second_leg(one, source, target, length_table)
            went = jnp.clip(jnp.minimum(fits_a, fits_b), 0, length_table)
            missed = length_table - went
            late_place = places(source * chips + target, missed)
            end = jnp.max(jnp.where(missed > 0, late_place + missed, 0))
            plans.append((late_place, went, missed, end))
        most = jnp.maximum(plans[0][3], plans[1][3])
        late_fields = [jnp.where(core == 0, one, other_one) for one, other_one in zip(*plans)][:3]
        leave_match = every[None, :] == (my_chip * chip_rows + order)[:, None]
        late_pack = pick(leave_match, [target] + late_fields)
        late_unpack = pick(arrive_match, [source] + late_fields)
        pieces = lax.all_to_all(
            pack_more_kernel(core, start, late_pack, kv_cache, lent, chips),
            "rep",
            split_axis=0,
            concat_axis=0,
            tiled=True,
            axis_index_groups=same_core,
        )
        moved, other = unpack_more_kernel(core, start, late_unpack, pieces, moved, other)
        return start + LATER, most, moved, other

    most = jnp.where(overflow, 1, 0).astype(jnp.int32)
    _, _, cache_moved, held = lax.while_loop(
        lambda state: state[0] < state[1], more, (first, most, cache_moved, held)
    )
    returned = lax.ppermute(held, "rep", other_core)
    cache_moved = finish_kernel(core, returned, cache_moved)
    summed = jnp.sum(exchanged.astype(jnp.float32), axis=0).astype(jnp.bfloat16)
    summed = summed.reshape(2, row_total, out_cols)
    straight, crossed = [], []
    for r in range(reps):
        for t in range(tps):
            pair = (r // 4 + t // 2) % (reps // 4) * 2 + t % 2
            straight.append((r * tps + t, (2 * pair + r % 2) * tps + r // 2))
            crossed.append((r * tps + t, (2 * pair + 1 - r % 2) * tps + r // 2))
    left = lax.ppermute(
        lax.dynamic_index_in_dim(summed, core, 0, keepdims=False), ("rep", "tp"), straight
    )
    right = lax.ppermute(
        lax.dynamic_index_in_dim(summed, 1 - core, 0, keepdims=False), ("rep", "tp"), crossed
    )
    left, right, cache_moved = lax.optimization_barrier((left, right, cache_moved))
    layer_out = jnp.where(
        core == 0,
        jnp.concatenate([left, right], axis=1),
        jnp.concatenate([right, left], axis=1),
    ).reshape(num_steps, num_rows, 2 * out_cols)

    return (layer_out, cache_moved)


def solution(mesh):
    placed = (
        P(None, "rep", None),
        P(),
        P("rep", "tp"),
        P("rep", None, "tp"),
        P("tp", "rep"),
        P("rep", None, None, "tp"),
        P("rep"),
        P("rep"),
    )
    return jax.shard_map(
        per_device,
        mesh=mesh,
        in_specs=placed,
        out_specs=(P(None, "rep", "tp"), P("rep", None, None, "tp")),
        check_vma=False,
    )
```
